256 devices in a mesh: batch: 16 (over z, x_lo), mp: 16 (over x_hi, y, core).
Axes of the slice: x: 4 (x_hi: 2, x_lo: 2; x = x_hi * 2 + x_lo), y: 4, z: 8, core: 2. Of those that a mesh axis runs over, the one named last changes fastest.
Arguments:
- hidden_in: bfloat16 [512, 16384], P('batch'), may hold values from -36 to 36
- queries: bfloat16 [512, 16384], P('batch', 'mp'), may hold values from -128 to 128
- key_cache: bfloat16 [512, 1024], P('batch'), may hold values from -4.5 to 4.5
- value_cache: bfloat16 [512, 1024], P('batch'), may hold values from -4 to 4
- question: int32 [128], P('batch'), may hold values from 0 to 15
- prefix_len: int32 [16], replicated, may hold values from 6 to 24, as said below
- norm_gain: float32 [16384], replicated, may hold values from 0.1 to 1.9
- gate_weight: bfloat16 [16384, 26624], P('batch', 'mp'), may hold values from -0.046875 to 0.046875
- up_weight: bfloat16 [16384, 26624], P('batch', 'mp'), may hold values from -0.046875 to 0.046875
- down_weight: bfloat16 [26624, 16384], P('mp', 'batch'), may hold values from -0.0390625 to 0.0390625
Outputs:
- layer_out: bfloat16 [512, 16384], P('mp', 'batch')
The draws below stay inside these ranges and needn't reach their ends.
Inputs may be any that keep to these rules, and one draw needn't show every extreme that they name: `prefix_len`: some question has all 24 prefix tokens live, and another question has the fewest allowed.
All inputs are finite; a program needn't handle non-finite values.
Results may differ from the reference program's by a relative error of at most 0.0055.
Values may be sent and summed in bfloat16 or wider, within the bound.
No kernel may reach another device: no remote copies, remote signals or barrier semaphores. Data moves between devices by JAX's collectives and lax.ppermute only.
A program may use at most 64 MiB of HBM per device.

```python
import math
import jax
import jax.numpy as jnp
from jax import lax

D = 16384
HEADS = 128
KV_HEADS = 8
HEAD_DIM = 128
FF = 26624
PREFIX = 24
OPT_DEV = 8
ROWS_DEV = 32
QUESTIONS = 16
OPTIONS = 128
ROWS = 512
KV_WIDTH = 1024


def shared_keys(key):
    return jax.random.truncated_normal(jax.random.fold_in(key, 101), -4.0, 4.0, (ROWS, KV_WIDTH), jnp.float32)


def shared_map(key):
    return jax.random.randint(jax.random.fold_in(key, 103), (OPTIONS,), 0, QUESTIONS).astype(jnp.int32)


def draw_key_cache(key, part):
    drawn = shared_keys(key)
    return drawn.astype(jnp.bfloat16)


def draw_queries(key, part):
    key = jax.random.fold_in(key, 7)
    queries = jax.random.truncated_normal(key, -4.0, 4.0, (ROWS, D), jnp.float32)
    return queries.astype(jnp.bfloat16)


def draw_question(key, part):
    return shared_map(key)


def draw_prefix_len(key, part):
    key = jax.random.fold_in(key, 11)
    first_key, second_key, third_key = jax.random.split(key, 3)
    fewest = max(2, PREFIX // 4)
    lengths = jax.random.randint(first_key, (QUESTIONS,), fewest, PREFIX + 1)
    chosen = jax.random.randint(second_key, (), 0, QUESTIONS)
    other = (chosen + 1 + jax.random.randint(third_key, (), 0, QUESTIONS - 1)) % QUESTIONS
    positions = jnp.arange(QUESTIONS)
    lengths = jnp.where(positions == other, fewest, lengths)
    return jnp.where(positions == chosen, PREFIX, lengths).astype(jnp.int32)


def draw_hidden_in(key, part):
    key = jax.random.fold_in(key, 13)
    first_key, second_key, third_key = jax.random.split(key, 3)
    row_scale = jnp.exp(jax.random.uniform(first_key, (ROWS, 1), jnp.float32, math.log(0.3), math.log(3.0)))
    col_scale = jnp.exp(jax.random.uniform(second_key, (1, D), jnp.float32, math.log(0.3), math.log(3.0)))
    drawn = jax.random.truncated_normal(third_key, -4.0, 4.0, (ROWS, D), jnp.float32)
    return (drawn * row_scale * col_scale).astype(jnp.bfloat16)


def steps_of(key, dims, shards, smallest, top_value):
    gain, own = 1.0, jax.random.fold_in(key, 6)
    for axis_at, shards_of in shards:
        heights = jnp.exp(jax.random.uniform(jax.random.fold_in(own, axis_at), (shards_of,), jnp.float32, smallest / len(shards), top_value / len(shards)))
        gain = gain * jnp.repeat(heights, dims[axis_at] // shards_of).reshape([-1 if axis == axis_at else 1 for axis in range(len(dims))])
    return gain


def normal_values(rng, extent, width, reach, cuts=(), held_as=jnp.bfloat16):
    result = jax.random.normal(rng, extent, jnp.float32) * width
    if len(cuts) > 0:
        result = steps_of(rng, extent, cuts, -0.22, 0.18) * result
    return jnp.clip(result, min=-reach, max=reach).astype(held_as)


def setup_inputs(seed: int = 0) -> dict:
    keys = jax.random.split(jax.random.key(seed), 11)
    return {
        "hidden_in": draw_hidden_in(jax.random.fold_in(keys[10], 71), 0),
        "queries": draw_queries(jax.random.fold_in(keys[10], 71), 0),
        "key_cache": draw_key_cache(jax.random.fold_in(keys[10], 71), 0),
        "value_cache": normal_values(keys[3], (ROWS, KV_WIDTH), 1.0, 4.0, ((0, 16),)),
        "question": draw_question(jax.random.fold_in(keys[10], 71), 0),
        "prefix_len": draw_prefix_len(jax.random.fold_in(keys[10], 71), 0),
        "norm_gain": jnp.clip(1.0 + 0.18 * jax.random.normal(keys[6], (D,), jnp.float32), 0.1, 1.9),
        "gate_weight": normal_values(keys[7], (D, FF), D ** -0.5, 0.046875, ((0, 16), (1, 16))),
        "up_weight": normal_values(keys[8], (D, FF), D ** -0.5, 0.046875, ((0, 16), (1, 16))),
        "down_weight": normal_values(keys[9], (FF, D), FF ** -0.5, 0.0390625, ((0, 16), (1, 16))),
    }


def attend(batch_index, query_block, key_cache, value_cache, question, prefix_len):
    group_size = HEADS // KV_HEADS
    total_rows = key_cache.shape[0]
    local_rows = jnp.arange(ROWS_DEV, dtype=jnp.int32)
    option_owner = lax.dynamic_slice_in_dim(question, (batch_index * OPT_DEV).astype(jnp.int32), OPT_DEV)
    owner_rows = jnp.concatenate([jnp.zeros((PREFIX,), jnp.int32) + batch_index, option_owner.astype(jnp.int32)])
    owner_length = prefix_len[owner_rows]
    key_limit = jnp.where(local_rows < PREFIX, jnp.minimum(local_rows + 1, owner_length), owner_length)
    key_index = jnp.arange(total_rows, dtype=jnp.int32)
    key_batch = key_index // ROWS_DEV
    key_local = key_index % ROWS_DEV
    own_index = batch_index * ROWS_DEV + local_rows
    allowed = (key_batch[None, :] == owner_rows[:, None]) & (key_local[None, :] < key_limit[:, None]) | (key_index[None, :] == own_index[:, None]) & (local_rows[:, None] >= PREFIX)
    query_heads = query_block.astype(jnp.float32).reshape(ROWS_DEV, KV_HEADS, group_size, HEAD_DIM)
    key_heads = key_cache.astype(jnp.float32).reshape(total_rows, KV_HEADS, HEAD_DIM)
    value_heads = value_cache.astype(jnp.float32).reshape(total_rows, KV_HEADS, HEAD_DIM)
    scores = jnp.einsum('rgpd,kgd->gprk', query_heads, key_heads) / jnp.sqrt(jnp.float32(HEAD_DIM))
    scores = jnp.where(allowed[None, None], scores, jnp.float32(-1e+30))
    row_peak = lax.optimization_barrier(jnp.max(scores, axis=-1, keepdims=True))
    exponent = jnp.exp(scores - row_peak)
    attention = (exponent / lax.optimization_barrier(jnp.sum(exponent, axis=-1, keepdims=True))).astype(jnp.bfloat16)
    context = jnp.einsum('gprk,kgd->rgpd', attention.astype(jnp.float32), value_heads)
    return context.reshape(ROWS_DEV, D).astype(jnp.bfloat16)

def reference(hidden_in, queries, key_cache, value_cache, question, prefix_len, norm_gain, gate_weight, up_weight, down_weight):
    query_blocks = queries.reshape(QUESTIONS, ROWS_DEV, D)

    def one_block(pair):
        return attend(pair[0], pair[1], key_cache, value_cache, question, prefix_len)
    context = lax.map(one_block, (jnp.arange(QUESTIONS, dtype=jnp.int32), query_blocks)).reshape(ROWS, D)
    residual = (hidden_in.astype(jnp.float32) + context.astype(jnp.float32)).astype(jnp.bfloat16)
    widened = residual.astype(jnp.float32)
    mean_square = lax.optimization_barrier(jnp.mean(widened * widened, axis=-1, keepdims=True))
    normed = (widened * lax.rsqrt(mean_square + 1e-05) * norm_gain).astype(jnp.bfloat16)
    gate = jnp.dot(normed, gate_weight, preferred_element_type=jnp.float32)
    up_part = jnp.dot(normed, up_weight, preferred_element_type=jnp.float32)
    hidden = (jax.nn.silu(gate) * up_part).astype(jnp.bfloat16)
    branch_out = jnp.dot(hidden, down_weight, preferred_element_type=jnp.float32)
    return (residual.astype(jnp.float32) + branch_out).astype(jnp.bfloat16)
```

```python
import jax
import jax.numpy as jnp
from jax import lax
from jax.sharding import PartitionSpec as P

HEADS = 128
KV_HEADS = 8
HEAD_DIM = 128
PREFIX = 24
ROWS_DEV = 32
ZN = 8
YN = 4
BF = jnp.bfloat16
F32 = jnp.float32


def permute(value, axis, target, count=16):
    return lax.ppermute(value, axis, [(i, target(i)) for i in range(count)])


def along_z(value, step):
    return permute(value, "batch", lambda i: (i + 2 * step) % 16)


def x_pair(value):
    return permute(value, "batch", lambda i: i ^ 1)


def along_y(value, step):
    return permute(value, "mp", lambda i: (i & 9) | ((i + 2 * step) & 6))


def x_far(value):
    return permute(value, "mp", lambda i: i ^ 8)


def core_pair(value):
    return permute(value, "mp", lambda i: i ^ 1)


def transpose_mesh(value):
    return lax.ppermute(
        value,
        ("batch", "mp"),
        [(b * 16 + m, m * 16 + b) for b in range(16) for m in range(16)],
    )


def attend(queries, keys, values, allowed):
    rows = queries.shape[0]
    heads = queries.shape[1] // HEAD_DIM
    flat = queries.reshape(rows, heads, HEAD_DIM)
    scores = jnp.einsum("rpd,kd->prk", flat, keys, preferred_element_type=F32) / jnp.sqrt(
        F32(HEAD_DIM)
    )
    scores = jnp.where(allowed[None], scores, F32(-1e30))
    exponent = jnp.exp(scores - jnp.max(scores, axis=-1, keepdims=True))
    attention = (exponent / jnp.sum(exponent, axis=-1, keepdims=True)).astype(BF)
    context = jnp.einsum("prk,kd->rpd", attention, values, preferred_element_type=F32)
    return context.reshape(rows, heads * HEAD_DIM).astype(BF)


def pick(array, index):
    return lax.dynamic_index_in_dim(array, index, 0, keepdims=False)


def gather_rows(block, place):
    x_hi, y, core = place
    rows, width = block.shape
    other = x_far(block)
    pair = jnp.where(x_hi == 0, jnp.stack([block, other]), jnp.stack([other, block]))
    after, before, across = along_y(pair, -1), along_y(pair, 1), along_y(pair, 2)
    ring = jnp.stack([pair, after, across, before])
    ring = jnp.stack([pick(ring, (i - y) % YN) for i in range(YN)], axis=1)
    theirs = core_pair(ring)
    both = jnp.where(
        core == 0, jnp.stack([ring, theirs], axis=2), jnp.stack([theirs, ring], axis=2)
    )
    return both.reshape(16, rows, width)


def sum_over_batch(partial, place, split):
    z, x_lo = place

    def take(step):
        return pick(partial, (z + step) % ZN)

    far = take(4)
    up, down = along_z(far[..., :split], 1), along_z(far[..., split:], -1)
    for step in (3, 2, 1):
        mine_up, mine_down = take(step), take(-step)
        if step == 3:
            mine_up = jnp.concatenate(
                [
                    (mine_up[..., :split].astype(F32) + up.astype(F32)).astype(BF),
                    mine_up[..., split:],
                ],
                axis=-1,
            )
            mine_down = jnp.concatenate(
                [
                    mine_down[..., :split],
                    (mine_down[..., split:].astype(F32) + down.astype(F32)).astype(BF),
                ],
                axis=-1,
            )
        else:
            mine_up = (mine_up.astype(F32) + up.astype(F32)).astype(BF)
            mine_down = (mine_down.astype(F32) + down.astype(F32)).astype(BF)
        up, down = along_z(mine_up, 1), along_z(mine_down, -1)
    both = take(0).astype(F32) + up.astype(F32) + down.astype(F32)
    theirs = x_pair(pick(both, 1 - x_lo).astype(BF))
    return pick(both, x_lo) + theirs.astype(F32)


def gather_over_batch(block, place):
    z, x_lo = place
    rows, width = block.shape
    other = x_pair(block)
    pair = jnp.where(x_lo == 0, jnp.stack([block, other]), jnp.stack([other, block]))
    up, down = pair, pair
    found = {0: pair}
    for step in (1, 2, 3):
        up, down = along_z(up, 1), along_z(down, -1)
        found[-step], found[step] = up, down
    up, down = along_z(up[:1], 1), along_z(down[1:], -1)
    found[4] = jnp.concatenate([up, down])
    ring = jnp.stack([found[s if s <= 4 else s - 8] for s in range(ZN)])
    ring = jnp.concatenate([ring, ring])
    ring = lax.dynamic_slice_in_dim(ring, (ZN - z) % ZN, ZN, 0)
    return ring.reshape(16, rows, width)


def sum_over_mp(partial, place):
    x_hi, y, core = place
    keep = lax.dynamic_index_in_dim(partial, core, 2, keepdims=False)
    give = lax.dynamic_index_in_dim(partial, 1 - core, 2, keepdims=False)
    held = keep + core_pair(give.astype(BF)).astype(F32)

    def take(step):
        return lax.dynamic_index_in_dim(held, (y + step) % YN, 1, keepdims=False)

    parts = [along_y(take(s).astype(BF), s) for s in (1, -1, 2)]
    held2 = take(0) + parts[0].astype(F32) + parts[1].astype(F32) + parts[2].astype(F32)
    theirs = x_far(pick(held2, 1 - x_hi).astype(BF))
    return pick(held2, x_hi) + theirs.astype(F32)


def feed_forward(residual, gain, gate_weight, up_weight, down_weight, batch_place, mp_place):
    rows, width = residual.shape
    hidden_width = gate_weight.shape[1]
    own = transpose_mesh(residual)
    x = gather_rows(own, mp_place).reshape(16 * rows, width).astype(F32)
    squares = jnp.sum((x * x).reshape(16 * rows, width // 128, 128), axis=1).astype(BF)
    scaled = (x * gain).astype(BF)
    partial = jnp.concatenate(
        [
            jnp.dot(scaled, gate_weight, preferred_element_type=F32).astype(BF),
            jnp.dot(scaled, up_weight, preferred_element_type=F32).astype(BF),
            squares,
        ],
        axis=1,
    ).reshape(ZN, 2, rows, 2 * hidden_width + 128)
    summed = sum_over_batch(partial, batch_place, hidden_width)
    mean_square = jnp.sum(summed[:, 2 * hidden_width :], axis=1, keepdims=True) / F32(16 * width)
    scale = lax.rsqrt(mean_square + 1e-05)
    gate = summed[:, :hidden_width] * scale
    lift = summed[:, hidden_width : 2 * hidden_width] * scale
    hidden = (jax.nn.silu(gate) * lift).astype(BF)
    hidden_all = gather_over_batch(hidden, batch_place).reshape(16 * rows, hidden_width)
    branch = jnp.dot(hidden_all, down_weight, preferred_element_type=F32)
    branch = sum_over_mp(branch.reshape(2, YN, 2, rows, width), mp_place)
    return (own.astype(F32) + branch).astype(BF)


def body(
    hidden_in,
    queries,
    key_cache,
    value_cache,
    question,
    prefix_len,
    norm_gain,
    gate_weight,
    up_weight,
    down_weight,
):
    batch_index = lax.axis_index("batch")
    mp_index = lax.axis_index("mp")
    batch_place = (batch_index // 2, batch_index % 2)
    mp_place = (mp_index // 8, (mp_index // 2) % YN, mp_index % 2)
    width = queries.shape[1]
    group = mp_index // 2
    keys = lax.dynamic_slice_in_dim(key_cache, group * HEAD_DIM, HEAD_DIM, 1)
    values = lax.dynamic_slice_in_dim(value_cache, group * HEAD_DIM, HEAD_DIM, 1)
    incoming = lax.dynamic_slice_in_dim(hidden_in, mp_index * width, width, 1)
    gain = lax.dynamic_slice_in_dim(norm_gain, batch_index * width, width, 0)
    both_all = lax.all_gather(jnp.concatenate([keys, values], axis=1), "batch", axis=0, tiled=True)

    row = jnp.arange(PREFIX, dtype=jnp.int32)
    prefix_allowed = (row[None, :] <= row[:, None]) & (row[None, :] < prefix_len[batch_index])
    prefix_context = attend(queries[:PREFIX], keys[:PREFIX], values[:PREFIX], prefix_allowed)
    prefix_residual = (incoming[:PREFIX].astype(F32) + prefix_context.astype(F32)).astype(BF)

    key_index = jnp.arange(16 * ROWS_DEV, dtype=jnp.int32)
    own_index = batch_index * ROWS_DEV + PREFIX + jnp.arange(ROWS_DEV - PREFIX, dtype=jnp.int32)
    option_allowed = (key_index[None, :] // ROWS_DEV == question[:, None]) & (
        key_index[None, :] % ROWS_DEV < prefix_len[question][:, None]
    ) | (key_index[None, :] == own_index[:, None])
    option_context = attend(
        queries[PREFIX:], both_all[:, :HEAD_DIM], both_all[:, HEAD_DIM:], option_allowed
    )
    option_residual = (incoming[PREFIX:].astype(F32) + option_context.astype(F32)).astype(BF)

    outs = [
        feed_forward(
            part, gain, gate_weight, up_weight, down_weight, batch_place, mp_place
        )
        for part in (prefix_residual, option_residual)
    ]
    return jnp.concatenate(outs, axis=0)


def solution(mesh):
    return jax.shard_map(
        body,
        mesh=mesh,
        in_specs=(
            P("batch", None),
            P("batch", "mp"),
            P("batch", None),
            P("batch", None),
            P("batch"),
            P(),
            P(),
            P("batch", "mp"),
            P("batch", "mp"),
            P("mp", "batch"),
        ),
        out_specs=P("mp", "batch"),
        check_vma=False,
    )
```

```python
import jax
import jax.numpy as jnp
from jax import lax
from jax.experimental import pallas as pl
from jax.experimental.pallas import tpu as pltpu
from jax.sharding import PartitionSpec as P

HEADS = 128
KV_HEADS = 8
HEAD_DIM = 128
PREFIX = 24
ROWS_DEV = 32
ZN = 8
YN = 4
BF = jnp.bfloat16
F32 = jnp.float32


def permute(value, axis, target, count=16):
    return lax.ppermute(value, axis, [(i, target(i)) for i in range(count)])


def along_z(value, step):
    return permute(value, "batch", lambda i: (i + 2 * step) % 16)


def x_pair(value):
    return permute(value, "batch", lambda i: i ^ 1)


def along_y(value, step):
    return permute(value, "mp", lambda i: (i & 9) | ((i + 2 * step) & 6))


def x_far(value):
    return permute(value, "mp", lambda i: i ^ 8)


def core_pair(value):
    return permute(value, "mp", lambda i: i ^ 1)


def transpose_mesh(value):
    return lax.ppermute(
        value,
        ("batch", "mp"),
        [(b * 16 + m, m * 16 + b) for b in range(16) for m in range(16)],
    )


def together(*pairs):
    values = lax.optimization_barrier(tuple(value for value, _ in pairs))
    sent = tuple(move(value) for value, (_, move) in zip(values, pairs))
    return lax.optimization_barrier(sent)


def pick(array, index, axis=0):
    return lax.dynamic_index_in_dim(array, index, axis, keepdims=False, allow_negative_indices=False)


def block_of(array, index, size, axis):
    return lax.dynamic_slice_in_dim(array, index * size, size, axis, allow_negative_indices=False)


def attend_kernel(own_ref, length_ref, rows_ref, pairs_ref, out_ref):
    width = out_ref.shape[1]
    heads = width // HEAD_DIM
    total = pairs_ref.shape[0]
    own = own_ref[0]
    shape = (ROWS_DEV, total)
    key_index = lax.broadcasted_iota(jnp.int32, shape, 1)
    row = lax.broadcasted_iota(jnp.int32, shape, 0)
    key_block = key_index >> 5
    key_local = key_index & (ROWS_DEV - 1)
    live = jnp.zeros(shape, jnp.int32)
    for block in range(total // ROWS_DEV):
        live = jnp.where(key_block == block, length_ref[block], live)
    question = rows_ref[:, 2 * width :].astype(F32).astype(jnp.int32)
    question = jnp.concatenate([question] * (total // HEAD_DIM), axis=1)
    option = row >= PREFIX
    owner = jnp.where(option, question, own)
    seen = (key_block == owner) & (key_local < live) & (option | (key_local <= row))
    seen = seen | (option & (key_index == own * ROWS_DEV + row))
    bias = jnp.where(seen, F32(0), F32(-1e30))
    bias = jnp.concatenate([bias] * heads, axis=0)
    queries = jnp.concatenate(
        [rows_ref[:, h * HEAD_DIM : (h + 1) * HEAD_DIM] for h in range(heads)], axis=0
    )
    scores = lax.dot_general(
        queries, pairs_ref[:, :HEAD_DIM], (((1,), (1,)), ((), ())), preferred_element_type=F32
    )
    scores = jnp.where(bias < 0, bias, scores * F32(HEAD_DIM**-0.5))
    exponent = jnp.exp(scores - jnp.max(scores, axis=1, keepdims=True))
    attention = (exponent / jnp.sum(exponent, axis=1, keepdims=True)).astype(BF)
    context = jnp.dot(attention, pairs_ref[:, HEAD_DIM:], preferred_element_type=F32).astype(BF)
    for h in range(heads):
        columns = slice(h * HEAD_DIM, (h + 1) * HEAD_DIM)
        mine = context[h * ROWS_DEV : (h + 1) * ROWS_DEV].astype(F32)
        hidden = rows_ref[:, width + h * HEAD_DIM : width + (h + 1) * HEAD_DIM].astype(F32)
        out_ref[:, columns] = (hidden + mine).astype(BF)


def attend(own, prefix_len, rows, pairs, width):
    return pl.pallas_call(
        attend_kernel,
        out_shape=jax.ShapeDtypeStruct((ROWS_DEV, width), BF),
        in_specs=[
            pl.BlockSpec(memory_space=pltpu.SMEM),
            pl.BlockSpec(memory_space=pltpu.SMEM),
            pl.BlockSpec(memory_space=pltpu.VMEM),
            pl.BlockSpec(memory_space=pltpu.VMEM),
        ],
        out_specs=pl.BlockSpec(memory_space=pltpu.VMEM),
        compiler_params=pltpu.CompilerParams(vmem_limit_bytes=16 * 2**20),
    )(own.reshape(1), prefix_len, rows, pairs)


def gather_rows(block, place):
    x_hi, y, core = place
    rows, width = block.shape
    other = x_far(block)
    pair = jnp.where(x_hi == 0, jnp.stack([block, other]), jnp.stack([other, block]))
    after, before, across = together(
        (pair, lambda v: along_y(v, -1)),
        (pair, lambda v: along_y(v, 1)),
        (pair, lambda v: along_y(v, 2)),
    )
    ring = jnp.stack([pair, after, across, before])
    ring = jnp.stack([pick(ring, (i - y) & (YN - 1)) for i in range(YN)], axis=1)
    theirs = core_pair(ring)
    both = jnp.where(
        core == 0, jnp.stack([ring, theirs], axis=2), jnp.stack([theirs, ring], axis=2)
    )
    return both.reshape(16, rows, width)


def add(mine, theirs):
    return (mine.astype(F32) + theirs.astype(F32)).astype(BF)


def sum_over_batch(partial, place, split):
    z, x_lo = place

    def take(step):
        return pick(partial, (z + step) & (ZN - 1))

    def ring(up, down):
        return together((up, lambda v: along_z(v, 1)), (down, lambda v: along_z(v, -1)))

    far = take(4)
    up, down = ring(far[..., :split], far[..., split:])
    mine_up, mine_down = take(3), take(-3)
    up, down = ring(
        jnp.concatenate([add(mine_up[..., :split], up), mine_up[..., split:]], axis=-1),
        jnp.concatenate([mine_down[..., :split], add(mine_down[..., split:], down)], axis=-1),
    )
    for step in (2, 1):
        up, down = ring(add(take(step), up), add(take(-step), down))
    both = take(0).astype(F32) + up.astype(F32) + down.astype(F32)
    theirs = x_pair(pick(both, 1 - x_lo).astype(BF))
    return pick(both, x_lo) + theirs.astype(F32)


def gather_over_batch(block, place):
    z, x_lo = place
    rows, width = block.shape
    other = x_pair(block)
    pair = jnp.where(x_lo == 0, jnp.stack([block, other]), jnp.stack([other, block]))

    def ring(up, down):
        return together((up, lambda v: along_z(v, 1)), (down, lambda v: along_z(v, -1)))

    up, down = pair, pair
    found = {0: pair}
    for step in (1, 2, 3):
        up, down = ring(up, down)
        found[-step], found[step] = up, down
    up, down = ring(up[:1], down[1:])
    found[4] = jnp.concatenate([up, down])
    ordered = jnp.stack([found[s if s <= 4 else s - 8] for s in range(ZN)])
    ordered = jnp.stack([pick(ordered, (i - z) & (ZN - 1)) for i in range(ZN)])
    return ordered.reshape(16, rows, width)


def sum_over_mp(partial, place):
    x_hi, y, core = place
    held = pick(partial, core, 2) + core_pair(pick(partial, 1 - core, 2).astype(BF)).astype(F32)

    def take(step):
        return pick(held, (y + step) & (YN - 1), 1)

    after, before, across = together(
        (take(1).astype(BF), lambda v: along_y(v, 1)),
        (take(-1).astype(BF), lambda v: along_y(v, -1)),
        (take(2).astype(BF), lambda v: along_y(v, 2)),
    )
    summed = take(0) + after.astype(F32) + before.astype(F32) + across.astype(F32)
    theirs = x_far(pick(summed, 1 - x_hi).astype(BF))
    return pick(summed, x_hi) + theirs.astype(F32)


def body(
    hidden_in,
    queries,
    key_cache,
    value_cache,
    question,
    prefix_len,
    norm_gain,
    gate_weight,
    up_weight,
    down_weight,
):
    batch_index = lax.axis_index("batch")
    mp_index = lax.axis_index("mp")
    batch_place = (batch_index >> 1, batch_index & 1)
    mp_place = (mp_index >> 3, (mp_index >> 1) & (YN - 1), mp_index & 1)
    rows, width = queries.shape
    hidden_width = gate_weight.shape[1]
    group_size = HEADS // KV_HEADS
    copies = group_size * HEAD_DIM // width

    asked = jnp.concatenate([jnp.zeros((PREFIX,), jnp.int32), question]).astype(BF)
    mine = jnp.concatenate(
        [
            queries,
            block_of(hidden_in, mp_index, width, 1),
            jnp.broadcast_to(asked[:, None], (rows, HEAD_DIM)),
        ],
        axis=1,
    )
    theirs = transpose_mesh(mine)
    pairs = jnp.concatenate(
        [
            key_cache.reshape(rows, KV_HEADS, HEAD_DIM),
            value_cache.reshape(rows, KV_HEADS, HEAD_DIM),
        ],
        axis=2,
    ).transpose(1, 0, 2)
    pairs = jnp.repeat(pairs, copies, axis=0)
    pairs = lax.all_to_all(pairs, "batch", split_axis=0, concat_axis=0, tiled=True)

    own = attend(mp_index, prefix_len, theirs, pairs.reshape(16 * rows, 2 * HEAD_DIM), width)
    gain = block_of(norm_gain, batch_index, width, 0)
    x = gather_rows(own, mp_place).reshape(16 * rows, width).astype(F32)
    squares = jnp.sum((x * x).reshape(16 * rows, width // 128, 128), axis=1).astype(BF)
    scaled = (x * gain).astype(BF)
    partial = jnp.concatenate(
        [
            jnp.dot(scaled, gate_weight, preferred_element_type=F32).astype(BF),
            jnp.dot(scaled, up_weight, preferred_element_type=F32).astype(BF),
            squares,
        ],
        axis=1,
    ).reshape(ZN, 2, rows, 2 * hidden_width + 128)
    summed = sum_over_batch(partial, batch_place, hidden_width)
    mean_square = jnp.sum(summed[:, 2 * hidden_width :], axis=1, keepdims=True) / F32(16 * width)
    scale = lax.rsqrt(mean_square + 1e-05)
    gate = summed[:, :hidden_width] * scale
    lift = summed[:, hidden_width : 2 * hidden_width] * scale
    hidden = (jax.nn.silu(gate) * lift).astype(BF)
    hidden_all = gather_over_batch(hidden, batch_place).reshape(16 * rows, hidden_width)
    branch = jnp.dot(hidden_all, down_weight, preferred_element_type=F32)
    branch = sum_over_mp(branch.reshape(2, YN, 2, rows, width), mp_place)
    return (own.astype(F32) + branch).astype(BF)


def solution(mesh):
    return jax.shard_map(
        body,
        mesh=mesh,
        in_specs=(
            P("batch", None),
            P("batch", "mp"),
            P("batch", None),
            P("batch", None),
            P("batch"),
            P(),
            P(),
            P("batch", "mp"),
            P("batch", "mp"),
            P("mp", "batch"),
        ),
        out_specs=P("mp", "batch"),
        check_vma=False,
    )
```

```python
import jax
import jax.numpy as jnp
from jax import lax
from jax.experimental import pallas as pl
from jax.experimental.pallas import tpu as pltpu
from jax.sharding import PartitionSpec as P

HEADS = 128
KV_HEADS = 8
HEAD_DIM = 128
PREFIX = 24
ROWS_DEV = 32
ZN = 8
LANE = 128
BF = jnp.bfloat16
F32 = jnp.float32
PLANE = [[2 * i + core for i in range(8)] for core in range(2)]
VMEM = pl.BlockSpec(memory_space=pltpu.VMEM)
SMEM = pl.BlockSpec(memory_space=pltpu.SMEM)
ANY = pl.BlockSpec(memory_space=pl.ANY)
PARAMS = pltpu.CompilerParams(vmem_limit_bytes=24 * 2**20)


def permute(value, axis, target, count=16):
    return lax.ppermute(value, axis, [(i, target(i)) for i in range(count)])


def along_z(value, step):
    return permute(value, "batch", lambda i: (i + 2 * step) % 16)


def x_pair(value):
    return permute(value, "batch", lambda i: i ^ 1)


def core_pair(value):
    return permute(value, "mp", lambda i: i ^ 1)


def transpose_mesh(value):
    return lax.ppermute(
        value,
        ("batch", "mp"),
        [(b * 16 + m, m * 16 + b) for b in range(16) for m in range(16)],
    )


def over_plane(value):
    return lax.all_to_all(value, "mp", 0, 0, axis_index_groups=PLANE, tiled=True)


def together(*pairs):
    values = lax.optimization_barrier(tuple(value for value, _ in pairs))
    sent = tuple(move(value) for value, (_, move) in zip(values, pairs))
    return lax.optimization_barrier(sent)


def in_vmem(*shapes):
    made = tuple(pltpu.VMEM(shape, dtype) for shape, dtype in shapes)
    return made if len(made) > 1 else made[0]


def pack_kernel(group_ref, key_ref, value_ref, out_ref, held, sems):
    at = pl.ds(pl.multiple_of(group_ref[0] * HEAD_DIM, HEAD_DIM), HEAD_DIM)
    first = pltpu.make_async_copy(key_ref.at[:, at], held.at[:, :HEAD_DIM], sems.at[0])
    second = pltpu.make_async_copy(value_ref.at[:, at], held.at[:, HEAD_DIM:], sems.at[1])
    first.start()
    second.start()
    first.wait()
    second.wait()
    for i in range(out_ref.shape[0]):
        out_ref[i] = held[...]


def pack(group, key_cache, value_cache):
    return pl.pallas_call(
        pack_kernel,
        out_shape=jax.ShapeDtypeStruct((16, ROWS_DEV, 2 * HEAD_DIM), BF),
        in_specs=[SMEM, ANY, ANY],
        out_specs=VMEM,
        scratch_shapes=[
            pltpu.VMEM((ROWS_DEV, 2 * HEAD_DIM), BF),
            pltpu.SemaphoreType.DMA((2,)),
        ],
        compiler_params=PARAMS,
    )(group.reshape(1), key_cache, value_cache)


def attend_kernel(place_ref, length_ref, question_ref, queries_ref, hidden_ref, pairs_ref, out_ref, held, sem):
    width = out_ref.shape[1]
    heads = width // HEAD_DIM
    total = pairs_ref.shape[0]
    own = place_ref[0]
    at = pl.ds(pl.multiple_of(place_ref[1] * width, width), width)
    fetch = pltpu.make_async_copy(hidden_ref.at[:, at], held, sem)
    fetch.start()
    shape = (ROWS_DEV, total)
    key_index = lax.broadcasted_iota(jnp.int32, shape, 1)
    row = lax.broadcasted_iota(jnp.int32, shape, 0)
    key_block = key_index >> 5
    key_local = key_index & (ROWS_DEV - 1)
    live = jnp.zeros(shape, jnp.int32)
    for block in range(total // ROWS_DEV):
        live = jnp.where(key_block == block, length_ref[block], live)
    owner = jnp.full(shape, own)
    for option in range(ROWS_DEV - PREFIX):
        owner = jnp.where(row == PREFIX + option, question_ref[option], owner)
    option = row >= PREFIX
    seen = (key_block == owner) & (key_local < live) & (option | (key_local <= row))
    seen = seen | (option & (key_index == own * ROWS_DEV + row))
    bias = jnp.where(seen, F32(0), F32(-1e30))
    bias = jnp.concatenate([bias] * heads, axis=0)
    queries = jnp.concatenate(
        [queries_ref[:, h * HEAD_DIM : (h + 1) * HEAD_DIM] for h in range(heads)], axis=0
    )
    scores = lax.dot_general(
        queries, pairs_ref[:, :HEAD_DIM], (((1,), (1,)), ((), ())), preferred_element_type=F32
    )
    scores = jnp.where(bias < 0, bias, scores * F32(HEAD_DIM**-0.5))
    exponent = jnp.exp(scores - jnp.max(scores, axis=1, keepdims=True))
    attention = (exponent / jnp.sum(exponent, axis=1, keepdims=True)).astype(BF)
    context = jnp.dot(attention, pairs_ref[:, HEAD_DIM:], preferred_element_type=F32).astype(BF)
    fetch.wait()
    for h in range(heads):
        columns = slice(h * HEAD_DIM, (h + 1) * HEAD_DIM)
        mine = context[h * ROWS_DEV : (h + 1) * ROWS_DEV].astype(F32)
        out_ref[:, columns] = (held[:, columns].astype(F32) + mine).astype(BF)


def attend(place, prefix_len, question, queries, hidden_in, pairs):
    return pl.pallas_call(
        attend_kernel,
        out_shape=in_vmem((queries.shape, BF)),
        in_specs=[SMEM, SMEM, SMEM, VMEM, ANY, VMEM],
        out_specs=VMEM,
        scratch_shapes=[pltpu.VMEM(queries.shape, BF), pltpu.SemaphoreType.DMA(())],
        compiler_params=PARAMS,
    )(place, prefix_len, question, queries, hidden_in, pairs)


FAR, KEEP = 4, 0


def project_kernel(tiles, early, place_ref, mine_ref, theirs_ref, gain_ref, gate_ref, up_ref, *refs):
    give, kept, far_low, far_high = refs[0:8], refs[8:15], refs[15], refs[16]
    rows, weights, sems, squares = refs[17:]
    n = ROWS_DEV
    width = mine_ref.shape[2]
    slots = weights.shape[0]
    wide = 2 * tiles + 1

    def copies(t, slot):
        at = pl.ds(pl.multiple_of(t * LANE, LANE), LANE)
        return (
            pltpu.make_async_copy(gate_ref.at[:, at], weights.at[slot, :, :LANE], sems.at[slot, 0]),
            pltpu.make_async_copy(up_ref.at[:, at], weights.at[slot, :, LANE:], sems.at[slot, 1]),
        )

    for t in range(slots - 1):
        for copy in copies(t, t):
            copy.start()

    def put(s, j, tile, value, is_early):
        if is_early:
            column = pl.multiple_of(tile * LANE, LANE)
            if j == 1:
                give[s][:, pl.ds(column, LANE)] = value
            elif s == FAR:
                far_low[:, pl.ds(column, LANE)] = value
            else:
                kept[s if s < FAR else s - 1][:, pl.ds(column, LANE)] = value
        else:
            late = tile - early + j * (wide - early)
            if s == FAR:
                far_high[:, pl.ds(pl.multiple_of(late * LANE, LANE), LANE)] = value
            else:
                column = pl.multiple_of((late + early) * LANE, LANE)
                kept[s if s < FAR else s - 1][:, pl.ds(column, LANE)] = value

    z, flip = place_ref[0], place_ref[1]
    gain = gain_ref[...]
    for s in range(ZN):
        source = (z + s) & (ZN - 1)
        for ref, j in ((mine_ref, flip), (theirs_ref, 1 - flip)):
            x = ref[source].astype(F32)
            rows[pl.ds(pl.multiple_of(s * 2 * n + j * n, n), n), :] = (x * gain).astype(BF)
            square = x * x
            total = square[:, :LANE]
            for k in range(1, width // LANE):
                total = total + square[:, k * LANE : (k + 1) * LANE]
            squares[pl.ds(pl.multiple_of(s * 2 * n + j * n, n), n), :] = total.astype(BF)
    for s in range(ZN):
        for j in range(2):
            put(s, j, wide - 1, squares[s * 2 * n + j * n : s * 2 * n + (j + 1) * n, :], False)

    def step(t, up_early):
        slot = lax.rem(t, slots)
        ahead = t + slots - 1

        @pl.when(ahead < tiles)
        def _():
            for copy in copies(ahead, lax.rem(ahead, slots)):
                copy.start()

        for copy in copies(t, slot):
            copy.wait()
        product = jnp.dot(rows[...], weights[slot], preferred_element_type=F32).astype(BF)
        for s in range(ZN):
            for j in range(2):
                part = product[s * 2 * n + j * n : s * 2 * n + (j + 1) * n]
                put(s, j, t, part[:, :LANE], True)
                put(s, j, tiles + t, part[:, LANE:], up_early)

    lax.fori_loop(0, early - tiles, lambda t, _: (step(t, True), 0)[1], 0)
    lax.fori_loop(early - tiles, tiles, lambda t, _: (step(t, False), 0)[1], 0)


def project(place, mine, theirs, gain, gate_weight, up_weight):
    width, hidden_width = gate_weight.shape
    tiles = hidden_width // LANE
    early = 2 * (2 * tiles + 1) // 3
    low = (ROWS_DEV, early * LANE)
    high = (ROWS_DEV, 2 * (2 * tiles + 1 - early) * LANE)
    whole = (ROWS_DEV, low[1] + high[1])
    n = 2 * ZN * ROWS_DEV
    refs = pl.pallas_call(
        lambda *refs: project_kernel(tiles, early, *refs),
        out_shape=in_vmem(*[(low, BF)] * 8, *[(whole, BF)] * 7, (low, BF), (high, BF)),
        in_specs=[SMEM, VMEM, VMEM, VMEM, ANY, ANY],
        out_specs=(VMEM,) * 17,
        scratch_shapes=[
            pltpu.VMEM((n, width), BF),
            pltpu.VMEM((3, width, 2 * LANE), BF),
            pltpu.SemaphoreType.DMA((3, 2)),
            pltpu.VMEM((n, LANE), BF),
        ],
        compiler_params=PARAMS,
    )(place, mine, theirs, gain, gate_weight, up_weight)
    kept = list(refs[8:15])
    return refs[:8], kept[:4] + [None] + kept[4:], refs[15], refs[16], early


def add_first_kernel(low_ref, x_ref, out_ref):
    out_ref[...] = (low_ref[...].astype(F32) + x_ref[...].astype(F32)).astype(BF)


def add_far_kernel(mine_up, mine_down, x_up, x_down, up, down, out_up, out_down):
    low = x_up.shape[1]
    out_up[:, :low] = (
        mine_up[:, :low].astype(F32) + x_up[...].astype(F32) + up[...].astype(F32)
    ).astype(BF)
    out_up[:, low:] = mine_up[:, low:]
    out_down[:, :low] = (mine_down[:, :low].astype(F32) + x_down[...].astype(F32)).astype(BF)
    out_down[:, low:] = (mine_down[:, low:].astype(F32) + down[...].astype(F32)).astype(BF)


def add_ring_kernel(mine_up, mine_down, x_up, x_down, up, down, out_up, out_down):
    low = x_up.shape[1]
    for mine, x, come, out in ((mine_up, x_up, up, out_up), (mine_down, x_down, down, out_down)):
        out[:, :low] = (
            mine[:, :low].astype(F32) + x[...].astype(F32) + come[:, :low].astype(F32)
        ).astype(BF)
        out[:, low:] = (mine[:, low:].astype(F32) + come[:, low:].astype(F32)).astype(BF)


def add_last_kernel(mine, x, up, down, keep, give):
    low, wide = x.shape[1], keep.shape[1]
    keep[:, :low] = (
        mine[:, :low].astype(F32)
        + x[...].astype(F32)
        + up[:, :low].astype(F32)
        + down[:, :low].astype(F32)
    )
    keep[:, low:] = (
        mine[:, low:wide].astype(F32) + up[:, low:wide].astype(F32) + down[:, low:wide].astype(F32)
    )
    give[...] = (
        mine[:, wide:].astype(F32) + up[:, wide:].astype(F32) + down[:, wide:].astype(F32)
    ).astype(BF)


def local(kernel, shapes, *args):
    return pl.pallas_call(
        kernel,
        out_shape=in_vmem(*shapes),
        in_specs=[VMEM] * len(args),
        out_specs=(VMEM,) * len(shapes) if len(shapes) > 1 else VMEM,
        compiler_params=PARAMS,
    )(*args)


def gated_kernel(keep, x, out):
    hidden_width = out.shape[1]
    wide = keep.shape[1]
    low = wide - x.shape[1]
    late = keep[:, low:] + x[...].astype(F32)
    squares = late[:, 2 * hidden_width - low :]
    scale = lax.rsqrt(jnp.sum(squares, axis=1, keepdims=True) * F32(1 / 16384) + 1e-05)
    gate = keep[:, :hidden_width] * scale
    lift = jnp.concatenate([keep[:, hidden_width:low], late[:, : 2 * hidden_width - low]], axis=1) * scale
    out[...] = (gate / (1 + jnp.exp(-gate)) * lift).astype(BF)


def down_kernel(place_ref, *refs):
    blocks, down_ref, give, keep = refs[:9], refs[9], refs[10], refs[11]
    rows, weights, sems = refs[12:]
    n = ROWS_DEV
    tiles = weights.shape[0]
    width = give.shape[2] // tiles
    copies = [
        pltpu.make_async_copy(down_ref.at[:, i * width : (i + 1) * width], weights.at[i], sems.at[i])
        for i in range(tiles)
    ]
    for copy in copies:
        copy.start()
    z, flip = place_ref[0], place_ref[1]
    for s in range(ZN):
        for j in range(2):
            if s == FAR:
                value = blocks[7 + j][0]
            else:
                value = blocks[s if s < FAR else s - 1][j]
            target = (z + s) & (ZN - 1)
            other = (flip + j) & 1
            at = (1 - other) * ZN * n + target * n
            rows[pl.ds(pl.multiple_of(at, n), n), :] = value
    for i in range(tiles):
        copies[i].wait()
        product = jnp.dot(rows[...], weights[i], preferred_element_type=F32)
        for target in range(ZN):
            give[target, :, i * width : (i + 1) * width] = product[target * n : (target + 1) * n].astype(BF)
            at = (ZN + target) * n
            keep[target, :, i * width : (i + 1) * width] = product[at : at + n]


def project_down(place, blocks, down_weight):
    hidden_width, width = down_weight.shape
    shape = (ZN, ROWS_DEV, width)
    return pl.pallas_call(
        down_kernel,
        out_shape=in_vmem((shape, BF), (shape, F32)),
        in_specs=[SMEM] + [VMEM] * 9 + [ANY],
        out_specs=(VMEM, VMEM),
        scratch_shapes=[
            pltpu.VMEM((2 * ZN * ROWS_DEV, hidden_width), BF),
            pltpu.VMEM((4, hidden_width, width // 4), BF),
            pltpu.SemaphoreType.DMA((4,)),
        ],
        compiler_params=PARAMS,
    )(place, *blocks, down_weight)


def add_core_kernel(keep, come, out):
    out[...] = (keep[...] + come[...].astype(F32)).astype(BF)


def finish_kernel(own, parts, out):
    total = own[...].astype(F32)
    for i in range(parts.shape[0]):
        total = total + parts[i].astype(F32)
    out[...] = total.astype(BF)


def ring(up, down, *more):
    return together(
        (up, lambda v: along_z(v, 1)), (down, lambda v: along_z(v, -1)), *more
    )


def body(
    hidden_in,
    queries,
    key_cache,
    value_cache,
    question,
    prefix_len,
    norm_gain,
    gate_weight,
    up_weight,
    down_weight,
):
    batch_index = lax.axis_index("batch")
    mp_index = lax.axis_index("mp")
    z, x_lo, core = batch_index >> 1, batch_index & 1, mp_index & 1
    rows, width = queries.shape
    hidden_width = gate_weight.shape[1]
    place = jnp.stack([z, x_lo ^ core])

    pairs = pack(mp_index >> 1, key_cache, value_cache)
    pairs = lax.all_to_all(pairs, "batch", 0, 0, tiled=True).reshape(16 * rows, 2 * HEAD_DIM)
    mine = attend(jnp.stack([batch_index, mp_index]), prefix_len, question, queries, hidden_in, pairs)

    own = transpose_mesh(mine)
    mine = over_plane(jnp.broadcast_to(own[None], (ZN, rows, width)))
    theirs = core_pair(mine)
    gain = lax.dynamic_slice_in_dim(norm_gain, batch_index * width, width, 0, allow_negative_indices=False)
    give, kept, far_low, far_high, early = project(
        place, mine, theirs, gain.reshape(1, width), gate_weight, up_weight
    )
    low, whole = far_low.shape, kept[0].shape

    def handed(s):
        return (give[s], x_pair)

    (x_far,) = together(handed(FAR))
    up, down, x_up, x_down = ring(
        local(add_first_kernel, [(low, BF)], far_low, x_far), far_high, handed(3), handed(5)
    )
    up, down = local(
        add_far_kernel, [(whole, BF)] * 2, kept[3], kept[5], x_up, x_down, up, down
    )
    up, down, x_up, x_down = ring(up, down, handed(2), handed(6))
    up, down = local(
        add_ring_kernel, [(whole, BF)] * 2, kept[2], kept[6], x_up, x_down, up, down
    )
    up, down, x_up, x_down = ring(up, down, handed(1), handed(7))
    up, down = local(
        add_ring_kernel, [(whole, BF)] * 2, kept[1], kept[7], x_up, x_down, up, down
    )
    up, down, x_own = ring(up, down, handed(0))
    late = whole[1] - 2 * hidden_width - LANE
    keep, last = local(
        add_last_kernel,
        [((rows, 2 * hidden_width + LANE), F32), ((rows, late), BF)],
        kept[0],
        x_own,
        up,
        down,
    )
    hidden = local(gated_kernel, [((rows, hidden_width), BF)], keep, x_pair(last))

    pair = jnp.stack([hidden, x_pair(hidden)])
    ups, downs = [pair], [pair]
    for _ in range(3):
        up, down = ring(ups[-1], downs[-1])
        ups.append(up)
        downs.append(down)
    up, down = ring(ups[-1][:1], downs[-1][1:])
    blocks = [pair, downs[1], downs[2], downs[3], ups[3], ups[2], ups[1], up, down]
    send, keep = project_down(place, blocks, down_weight)
    held = local(add_core_kernel, [(keep.shape, BF)], keep, core_pair(send))
    parts = over_plane(held)
    return pl.pallas_call(
        finish_kernel,
        out_shape=jax.ShapeDtypeStruct((rows, width), BF),
        in_specs=[VMEM, VMEM],
        out_specs=VMEM,
        compiler_params=PARAMS,
    )(own, parts)


def solution(mesh):
    return jax.shard_map(
        body,
        mesh=mesh,
        in_specs=(
            P("batch", None),
            P("batch", "mp"),
            P("batch", None),
            P("batch", None),
            P("batch"),
            P(),
            P(),
            P("batch", "mp"),
            P("batch", "mp"),
            P("mp", "batch"),
        ),
        out_specs=P("mp", "batch"),
        check_vma=False,
    )
```

```python
import jax
import jax.numpy as jnp
from jax import lax
from jax.experimental import pallas as pl
from jax.experimental.pallas import tpu as pltpu
from jax.sharding import PartitionSpec as P

HEADS = 128
KV_HEADS = 8
HEAD_DIM = 128
PREFIX = 24
ROWS_DEV = 32
ZN = 8
LANE = 128
BF = jnp.bfloat16
F32 = jnp.float32
PLANE = [[2 * i + core for i in range(8)] for core in range(2)]
VMEM = pl.BlockSpec(memory_space=pltpu.VMEM)
SMEM = pl.BlockSpec(memory_space=pltpu.SMEM)
ANY = pl.BlockSpec(memory_space=pl.ANY)
HBM = pl.BlockSpec(memory_space=pltpu.HBM)
PARAMS = pltpu.CompilerParams(vmem_limit_bytes=24 * 2**20)


def permute(value, axis, target, count=16):
    return lax.ppermute(value, axis, [(i, target(i)) for i in range(count)])


def along_z(value, step):
    return permute(value, "batch", lambda i: (i + 2 * step) % 16)


def x_pair(value):
    return permute(value, "batch", lambda i: i ^ 1)


def core_pair(value):
    return permute(value, "mp", lambda i: i ^ 1)


def transpose_mesh(value):
    return lax.ppermute(
        value,
        ("batch", "mp"),
        [(b * 16 + m, m * 16 + b) for b in range(16) for m in range(16)],
    )


def over_plane(value):
    return lax.all_to_all(value, "mp", 0, 0, axis_index_groups=PLANE, tiled=True)


def together(*pairs):
    values = lax.optimization_barrier(tuple(value for value, _ in pairs))
    sent = tuple(move(value) for value, (_, move) in zip(values, pairs))
    return lax.optimization_barrier(sent)


def in_vmem(*shapes):
    made = tuple(pltpu.VMEM(shape, dtype) for shape, dtype in shapes)
    return made if len(made) > 1 else made[0]


def in_hbm(value):
    return pltpu.with_memory_space_constraint(value, pltpu.HBM)


def softmax(scores, seen):
    scores = jnp.where(seen, scores * F32(HEAD_DIM**-0.5), F32(-1e30))
    exponent = jnp.exp(scores - jnp.max(scores, axis=1, keepdims=True))
    return (exponent / jnp.sum(exponent, axis=1, keepdims=True)).astype(BF)


def scored(queries, keys):
    return lax.dot_general(queries, keys, (((1,), (1,)), ((), ())), preferred_element_type=F32)


def prepare_kernel(length_ref, question_ref, queries_ref, hidden_ref, key_ref, value_ref, out_ref, queries, hidden, pair, sems):
    width = queries.shape[1]
    heads = width // HEAD_DIM
    batch_index, mp_index = lax.axis_index("batch"), lax.axis_index("mp")
    head = pl.ds(pl.multiple_of((mp_index >> 1) * HEAD_DIM, HEAD_DIM), HEAD_DIM)
    at = pl.ds(pl.multiple_of(mp_index * width, width), width)
    copies = [
        pltpu.make_async_copy(source, target, sems.at[i])
        for i, (source, target) in enumerate(
            [
                (key_ref.at[:, head], pair.at[:, :HEAD_DIM]),
                (queries_ref, queries),
                (value_ref.at[:, head], pair.at[:, HEAD_DIM:]),
                (hidden_ref.at[:, at], hidden),
            ]
        )
    ]
    for copy in copies:
        copy.start()
    shape = (ROWS_DEV, ROWS_DEV)
    row = lax.broadcasted_iota(jnp.int32, shape, 0)
    key = lax.broadcasted_iota(jnp.int32, shape, 1)
    seen = (key <= row) & (key < length_ref[batch_index])
    seen = jnp.concatenate([seen.astype(F32)] * heads, axis=0) > 0
    shape = (16, LANE)
    option = lax.broadcasted_iota(jnp.int32, shape, 0) & (ROWS_DEV - PREFIX - 1)
    asked = jnp.zeros(shape, jnp.int32)
    for i in range(ROWS_DEV - PREFIX):
        asked = jnp.where(option == i, question_ref[i], asked)
    out_ref[32:, width:] = asked.astype(F32).astype(BF)
    out_ref[:32, width:] = jnp.zeros((ROWS_DEV, LANE), BF)
    copies[0].wait()
    copies[1].wait()
    stacked = jnp.concatenate(
        [queries[:, h * HEAD_DIM : (h + 1) * HEAD_DIM] for h in range(heads)], axis=0
    )
    attention = softmax(scored(stacked, pair[:, :HEAD_DIM]), seen)
    copies[2].wait()
    context = jnp.dot(attention, pair[:, HEAD_DIM:], preferred_element_type=F32).astype(BF)
    out_ref[32:, : 2 * HEAD_DIM] = pair[:16]
    out_ref[32:, 2 * HEAD_DIM : 4 * HEAD_DIM] = pair[16:]
    last = queries[16:].astype(F32)[PREFIX - 16 :]
    half = width // 2
    out_ref[32:, half:width] = jnp.concatenate([last[:, :half], last[:, half:]], axis=0).astype(BF)
    copies[3].wait()
    prefix = lax.broadcasted_iota(jnp.int32, (ROWS_DEV, HEAD_DIM), 0) < PREFIX
    for h in range(heads):
        columns = slice(h * HEAD_DIM, (h + 1) * HEAD_DIM)
        mine = context[h * ROWS_DEV : (h + 1) * ROWS_DEV].astype(F32)
        mine = jnp.where(prefix, mine, F32(0))
        out_ref[:32, columns] = (hidden[:, columns].astype(F32) + mine).astype(BF)


def prepare(prefix_len, question, queries, hidden_in, key_cache, value_cache):
    rows, width = queries.shape
    return pl.pallas_call(
        prepare_kernel,
        out_shape=in_vmem(((rows + 16, width + LANE), BF)),
        in_specs=[SMEM, SMEM, HBM, HBM, HBM, HBM],
        out_specs=VMEM,
        scratch_shapes=[
            pltpu.VMEM((rows, width), BF),
            pltpu.VMEM((rows, width), BF),
            pltpu.VMEM((rows, 2 * HEAD_DIM), BF),
            pltpu.SemaphoreType.DMA((4,)),
        ],
        compiler_params=PARAMS,
    )(prefix_len, question, in_hbm(queries), in_hbm(hidden_in), in_hbm(key_cache), in_hbm(value_cache))


FAR = 4


def project_kernel(tiles, early, length_ref, gain_ref, mine_ref, theirs_ref, gate_ref, up_ref, *refs):
    own_ref, give, kept, far_low, far_high = refs[0], refs[1:6], refs[6:13], refs[13], refs[14]
    residual, rows, squares, gain, sem = refs[15:]
    n = ROWS_DEV
    width = own_ref.shape[1]
    half = width // 2
    wide = 2 * tiles + 1
    batch_index, mp_index = lax.axis_index("batch"), lax.axis_index("mp")
    z, core = batch_index >> 1, mp_index & 1
    flip = (batch_index & 1) ^ core
    fetch = pltpu.make_async_copy(gain_ref.at[pl.ds(batch_index * width, width)], gain, sem)
    fetch.start()

    def put(s, j, tile, value):
        lanes = slice(tile * LANE, (tile + 1) * LANE)
        if tile < early:
            if j == 1 and s in (0, FAR):
                give[s][:, lanes] = value
            elif j == 1:
                give[min(s, ZN - s)][0 if s < FAR else 1, :, lanes] = value
            elif s == FAR:
                far_low[:, lanes] = value
            else:
                kept[s if s < FAR else s - 1][:, lanes] = value
        else:
            late = tile - early + j * (wide - early)
            if s == FAR:
                far_high[:, late * LANE : (late + 1) * LANE] = value
            else:
                late += early
                kept[s if s < FAR else s - 1][:, late * LANE : (late + 1) * LANE] = value

    blocks = [(ref, i) for ref in (mine_ref, theirs_ref) for i in range(ZN)]
    options = ROWS_DEV - PREFIX

    def gathered(lanes):
        return jnp.concatenate([ref[i, n:, lanes] for ref, i in blocks], axis=0)

    def unfolded(first):
        low, high = slice(first, first + HEAD_DIM), slice(first + 2 * HEAD_DIM, first + 3 * HEAD_DIM)
        return jnp.concatenate(
            [ref[i, n:, lanes] for ref, i in blocks for lanes in (low, high)], axis=0
        )

    keys, values = unfolded(0), unfolded(HEAD_DIM)
    shape = (16 * len(blocks), n * len(blocks))
    asked = gathered(slice(width, width + LANE)).astype(F32).astype(jnp.int32)
    asked = jnp.concatenate([asked] * (shape[1] // LANE), axis=1)
    place = lax.broadcasted_iota(jnp.int32, shape, 1)
    order = place >> 5
    row = lax.broadcasted_iota(jnp.int32, shape, 0)
    owner = ((order & (ZN - 1)) << 1) + ((order >> 3) ^ core)
    live = jnp.zeros(shape, jnp.int32)
    for i in range(len(blocks)):
        live = jnp.where(order == i, length_ref[((i & (ZN - 1)) << 1) + ((i >> 3) ^ core)], live)
    seen = (owner == asked) & ((place & (n - 1)) < live)
    seen = seen | (place == (row >> 4) * n + PREFIX + (row & (options - 1)))
    contexts = []
    for h in range(half // HEAD_DIM):
        queries = gathered(slice(half + h * HEAD_DIM, half + (h + 1) * HEAD_DIM))
        attention = softmax(scored(queries, keys), seen)
        context = jnp.dot(attention, values, preferred_element_type=F32)
        contexts.append(context.astype(BF).astype(F32))
    fetch.wait()
    scale = gain[...].reshape(1, width)
    for k, (ref, i) in enumerate(blocks):
        at = k * 16
        added = jnp.concatenate(
            [context[at : at + options] for context in contexts]
            + [context[at + options : at + 16] for context in contexts],
            axis=1,
        )
        added = jnp.concatenate([jnp.zeros((16 - options, width), F32), added], axis=0)
        first = ref[i, :16, :width]
        last = (ref[i, 16:n, :width].astype(F32) + added).astype(BF)
        if ref is mine_ref:
            residual[i, :16] = first
            residual[i, 16:] = last
        s = (i - z) & (ZN - 1)
        j = flip if ref is mine_ref else 1 - flip
        at = pl.multiple_of(s * 2 * n + j * n, n)
        for part, offset in ((first, 0), (last, 16)):
            x = part.astype(F32)
            into = pl.ds(pl.multiple_of(at + offset, 16), 16)
            rows[into, :] = (x * scale).astype(BF)
            square = x * x
            total = square[:, :LANE]
            for lane in range(1, width // LANE):
                total = total + square[:, lane * LANE : (lane + 1) * LANE]
            squares[into, :] = total.astype(BF)
    own_ref[...] = residual[mp_index >> 1]

    for first, ref, at in [
        (base + t, ref, t) for base, ref in ((0, gate_ref), (tiles, up_ref)) for t in range(0, tiles, 2)
    ] + [(wide - 1, None, 0)]:
        if ref is None:
            product = squares[...]
        else:
            lanes = slice(at * LANE, min(at + 2, tiles) * LANE)
            product = jnp.dot(rows[...], ref[:, lanes], preferred_element_type=F32).astype(BF)
        for t in range(product.shape[1] // LANE):
            for s in range(ZN):
                for j in range(2):
                    begin = (2 * s + j) * n
                    put(s, j, first + t, product[begin : begin + n, t * LANE : (t + 1) * LANE])


EARLY = 16


def project(prefix_len, norm_gain, mine, theirs, gate_weight, up_weight):
    width, hidden_width = gate_weight.shape
    tiles = hidden_width // LANE
    n = ROWS_DEV
    low = (n, EARLY * LANE)
    high = (n, 2 * (2 * tiles + 1 - EARLY) * LANE)
    whole = (n, low[1] + high[1])
    own = (n, width)
    refs = pl.pallas_call(
        lambda *refs: project_kernel(tiles, EARLY, *refs),
        out_shape=in_vmem(
            (own, BF), (low, BF), *[((2, *low), BF)] * 3, (low, BF), *[(whole, BF)] * 7, (low, BF), (high, BF)
        ),
        in_specs=[SMEM, HBM] + [VMEM] * 4,
        out_specs=(VMEM,) * 15,
        scratch_shapes=[
            pltpu.VMEM((ZN, n, width), BF),
            pltpu.VMEM((2 * ZN * n, width), BF),
            pltpu.VMEM((2 * ZN * n, LANE), BF),
            pltpu.VMEM((width,), F32),
            pltpu.SemaphoreType.DMA(()),
        ],
        compiler_params=PARAMS,
    )(prefix_len, in_hbm(norm_gain), mine, theirs, gate_weight, up_weight)
    kept = list(refs[6:13])
    return refs[0], refs[1:6], kept[:4] + [None] + kept[4:], refs[13], refs[14]


def add_first_kernel(low_ref, x_ref, out_ref):
    out_ref[...] = (low_ref[...].astype(F32) + x_ref[...].astype(F32)).astype(BF)


def add_far_kernel(mine_up, mine_down, x, up, down, out_up, out_down):
    low = x.shape[2]
    out_up[:, :low] = (
        mine_up[:, :low].astype(F32) + x[0].astype(F32) + up[...].astype(F32)
    ).astype(BF)
    out_up[:, low:] = mine_up[:, low:]
    out_down[:, :low] = (mine_down[:, :low].astype(F32) + x[1].astype(F32)).astype(BF)
    out_down[:, low:] = (mine_down[:, low:].astype(F32) + down[...].astype(F32)).astype(BF)


def add_ring_kernel(mine_up, mine_down, x, up, down, out_up, out_down):
    low = x.shape[2]
    for mine, i, come, out in ((mine_up, 0, up, out_up), (mine_down, 1, down, out_down)):
        out[:, :low] = (
            mine[:, :low].astype(F32) + x[i].astype(F32) + come[:, :low].astype(F32)
        ).astype(BF)
        out[:, low:] = (mine[:, low:].astype(F32) + come[:, low:].astype(F32)).astype(BF)


def add_last_kernel(mine, x, up, down, keep, give):
    low, wide = x.shape[1], keep.shape[1]
    keep[:, :low] = (
        mine[:, :low].astype(F32)
        + x[...].astype(F32)
        + up[:, :low].astype(F32)
        + down[:, :low].astype(F32)
    )
    keep[:, low:] = (
        mine[:, low:wide].astype(F32) + up[:, low:wide].astype(F32) + down[:, low:wide].astype(F32)
    )
    give[...] = (
        mine[:, wide:].astype(F32) + up[:, wide:].astype(F32) + down[:, wide:].astype(F32)
    ).astype(BF)


def local(kernel, shapes, *args):
    return pl.pallas_call(
        kernel,
        out_shape=in_vmem(*shapes),
        in_specs=[VMEM] * len(args),
        out_specs=(VMEM,) * len(shapes) if len(shapes) > 1 else VMEM,
        compiler_params=PARAMS,
    )(*args)


def gated_kernel(keep, x, out):
    hidden_width = out.shape[1]
    wide = keep.shape[1]
    low = wide - x.shape[1]
    late = keep[:, low:] + x[...].astype(F32)
    squares = late[:, 2 * hidden_width - low :]
    scale = lax.rsqrt(jnp.sum(squares, axis=1, keepdims=True) * F32(1 / 16384) + 1e-05)
    gate = keep[:, :hidden_width] * scale
    lift = jnp.concatenate([keep[:, hidden_width:low], late[:, : 2 * hidden_width - low]], axis=1) * scale
    out[...] = (gate / (1 + jnp.exp(-gate)) * lift).astype(BF)


def down_kernel(*refs):
    blocks, down_ref, give, keep, rows = refs[:9], refs[9], refs[10], refs[11], refs[12]
    n = ROWS_DEV
    batch_index, mp_index = lax.axis_index("batch"), lax.axis_index("mp")
    z, flip = batch_index >> 1, (batch_index ^ mp_index) & 1
    for s in range(ZN):
        for j in range(2):
            if s == FAR:
                value = blocks[7 + j][0]
            else:
                value = blocks[s if s < FAR else s - 1][j]
            target = (z + s) & (ZN - 1)
            other = (flip + j) & 1
            at = (1 - other) * ZN * n + target * n
            rows[pl.ds(pl.multiple_of(at, n), n), :] = value
    step = 2 * LANE
    for i in range(0, down_ref.shape[1], step):
        lanes = slice(i, i + step)
        product = jnp.dot(rows[...], down_ref[:, lanes], preferred_element_type=F32)
        for target in range(ZN):
            give[target, :, lanes] = product[target * n : (target + 1) * n].astype(BF)
            at = (ZN + target) * n
            keep[target, :, lanes] = product[at : at + n]


def project_down(blocks, down_weight):
    hidden_width, width = down_weight.shape
    shape = (ZN, ROWS_DEV, width)
    return pl.pallas_call(
        down_kernel,
        out_shape=in_vmem((shape, BF), (shape, F32)),
        in_specs=[VMEM] * 10,
        out_specs=(VMEM, VMEM),
        scratch_shapes=[pltpu.VMEM((2 * ZN * ROWS_DEV, hidden_width), BF)],
        compiler_params=PARAMS,
    )(*blocks, down_weight)


def add_core_kernel(keep, come, out):
    out[...] = (keep[...] + come[...].astype(F32)).astype(BF)


def finish_kernel(own, parts, out):
    total = own[...].astype(F32)
    for i in range(parts.shape[0]):
        total = total + parts[i].astype(F32)
    out[...] = total.astype(BF)


def ring(up, down, *more):
    return together(
        (up, lambda v: along_z(v, 1)), (down, lambda v: along_z(v, -1)), *more
    )


def body(
    hidden_in,
    queries,
    key_cache,
    value_cache,
    question,
    prefix_len,
    norm_gain,
    gate_weight,
    up_weight,
    down_weight,
):
    rows, width = queries.shape
    hidden_width = gate_weight.shape[1]

    sent = prepare(prefix_len, question, queries, hidden_in, key_cache, value_cache)
    came = transpose_mesh(sent)
    mine = over_plane(jnp.broadcast_to(came[None], (ZN, *came.shape)))
    theirs = core_pair(mine)
    own, give, kept, far_low, far_high = project(
        prefix_len, norm_gain, mine, theirs, gate_weight, up_weight
    )
    low, whole = far_low.shape, kept[0].shape

    (x,) = together((give[4], x_pair))
    up = local(add_first_kernel, [(low, BF)], far_low, x)
    up, down, x = ring(up, far_high, (give[3], x_pair))
    up, down = local(add_far_kernel, [(whole, BF)] * 2, kept[3], kept[5], x, up, down)
    up, down, x = ring(up, down, (give[2], x_pair))
    up, down = local(add_ring_kernel, [(whole, BF)] * 2, kept[2], kept[6], x, up, down)
    up, down, x = ring(up, down, (give[1], x_pair))
    up, down = local(add_ring_kernel, [(whole, BF)] * 2, kept[1], kept[7], x, up, down)
    up, down, x = ring(up, down, (give[0], x_pair))
    late = whole[1] - 2 * hidden_width - LANE
    keep, last = local(
        add_last_kernel,
        [((rows, 2 * hidden_width + LANE), F32), ((rows, late), BF)],
        kept[0],
        x,
        up,
        down,
    )
    hidden = local(gated_kernel, [((rows, hidden_width), BF)], keep, x_pair(last))

    pair = jnp.stack([hidden, x_pair(hidden)])
    ups, downs = [pair], [pair]
    for _ in range(3):
        up, down = ring(ups[-1], downs[-1])
        ups.append(up)
        downs.append(down)
    up, down = ring(ups[-1][:1], downs[-1][1:])
    blocks = [pair, downs[1], downs[2], downs[3], ups[3], ups[2], ups[1], up, down]
    send, keep = project_down(blocks, down_weight)
    held = local(add_core_kernel, [(keep.shape, BF)], keep, core_pair(send))
    parts = over_plane(held)
    return pl.pallas_call(
        finish_kernel,
        out_shape=jax.ShapeDtypeStruct((rows, width), BF),
        in_specs=[VMEM, VMEM],
        out_specs=VMEM,
        compiler_params=PARAMS,
    )(own, parts)


def solution(mesh):
    return jax.shard_map(
        body,
        mesh=mesh,
        in_specs=(
            P("batch", None),
            P("batch", "mp"),
            P("batch", None),
            P("batch", None),
            P("batch"),
            P(),
            P(),
            P("batch", "mp"),
            P("batch", "mp"),
            P("mp", "batch"),
        ),
        out_specs=P("mp", "batch"),
        check_vma=False,
    )
```

```python
import jax
import jax.numpy as jnp
from jax import lax
from jax.experimental import pallas as pl
from jax.experimental.pallas import tpu as pltpu
from jax.sharding import PartitionSpec as P

HEADS = 128
KV_HEADS = 8
HEAD_DIM = 128
PREFIX = 24
ROWS_DEV = 32
ZN = 8
LANE = 128
BF = jnp.bfloat16
F32 = jnp.float32
PLANE = [[2 * i + core for i in range(8)] for core in range(2)]
VMEM = pl.BlockSpec(memory_space=pltpu.VMEM)
SMEM = pl.BlockSpec(memory_space=pltpu.SMEM)
ANY = pl.BlockSpec(memory_space=pl.ANY)
HBM = pl.BlockSpec(memory_space=pltpu.HBM)
PARAMS = pltpu.CompilerParams(vmem_limit_bytes=28 * 2**20)


def permute(value, axis, target, count=16):
    return lax.ppermute(value, axis, [(i, target(i)) for i in range(count)])


def along_z(value, step):
    return permute(value, "batch", lambda i: (i + 2 * step) % 16)


def x_pair(value):
    return permute(value, "batch", lambda i: i ^ 1)


def core_pair(value):
    return permute(value, "mp", lambda i: i ^ 1)


def transpose_mesh(value):
    return lax.ppermute(
        value,
        ("batch", "mp"),
        [(b * 16 + m, m * 16 + b) for b in range(16) for m in range(16)],
    )


def over_plane(value):
    return lax.all_to_all(value, "mp", 0, 0, axis_index_groups=PLANE, tiled=True)


def in_vmem(*shapes):
    made = tuple(pltpu.VMEM(shape, dtype) for shape, dtype in shapes)
    return made if len(made) > 1 else made[0]


def in_hbm(value):
    return pltpu.with_memory_space_constraint(value, pltpu.HBM)


def softmax(scores, seen):
    scores = jnp.where(seen, scores * F32(HEAD_DIM**-0.5), F32(-1e30))
    exponent = jnp.exp(scores - jnp.max(scores, axis=1, keepdims=True))
    return (exponent / jnp.sum(exponent, axis=1, keepdims=True)).astype(BF)


def scored(queries, keys):
    return lax.dot_general(queries, keys, (((1,), (1,)), ((), ())), preferred_element_type=F32)


def prepare_kernel(lengths, questions, queries_ref, hidden_ref, key_ref, value_ref, out_ref, queries, hidden, pair, length_ref, question_ref, sems):
    width = queries.shape[1]
    heads = width // HEAD_DIM
    batch_index, mp_index = lax.axis_index("batch"), lax.axis_index("mp")
    head = pl.ds(pl.multiple_of((mp_index >> 1) * HEAD_DIM, HEAD_DIM), HEAD_DIM)
    at = pl.ds(pl.multiple_of(mp_index * width, width), width)
    copies = [
        pltpu.make_async_copy(source, target, sems.at[i])
        for i, (source, target) in enumerate(
            [
                (key_ref.at[:, head], pair.at[:, :HEAD_DIM]),
                (queries_ref, queries),
                (value_ref.at[:, head], pair.at[:, HEAD_DIM:]),
                (hidden_ref.at[:, at], hidden),
                (lengths, length_ref),
                (questions, question_ref),
            ]
        )
    ]
    for copy in copies:
        copy.start()
    copies[4].wait()
    copies[5].wait()
    shape = (ROWS_DEV, ROWS_DEV)
    row = lax.broadcasted_iota(jnp.int32, shape, 0)
    key = lax.broadcasted_iota(jnp.int32, shape, 1)
    seen = (key <= row) & (key < length_ref[batch_index])
    seen = jnp.concatenate([seen.astype(F32)] * heads, axis=0) > 0
    shape = (16, LANE)
    option = lax.broadcasted_iota(jnp.int32, shape, 0) & (ROWS_DEV - PREFIX - 1)
    asked = jnp.zeros(shape, jnp.int32)
    for i in range(ROWS_DEV - PREFIX):
        asked = jnp.where(option == i, question_ref[i], asked)
    out_ref[32:, width:] = asked.astype(F32).astype(BF)
    out_ref[:32, width:] = jnp.zeros((ROWS_DEV, LANE), BF)
    copies[0].wait()
    copies[1].wait()
    stacked = jnp.concatenate(
        [queries[:, h * HEAD_DIM : (h + 1) * HEAD_DIM] for h in range(heads)], axis=0
    )
    attention = softmax(scored(stacked, pair[:, :HEAD_DIM]), seen)
    copies[2].wait()
    context = jnp.dot(attention, pair[:, HEAD_DIM:], preferred_element_type=F32).astype(BF)
    out_ref[32:, : 2 * HEAD_DIM] = pair[:16]
    out_ref[32:, 2 * HEAD_DIM : 4 * HEAD_DIM] = pair[16:]
    last = queries[16:].astype(F32)[PREFIX - 16 :]
    half = width // 2
    out_ref[32:, half:width] = jnp.concatenate([last[:, :half], last[:, half:]], axis=0).astype(BF)
    copies[3].wait()
    prefix = lax.broadcasted_iota(jnp.int32, (ROWS_DEV, HEAD_DIM), 0) < PREFIX
    for h in range(heads):
        columns = slice(h * HEAD_DIM, (h + 1) * HEAD_DIM)
        mine = context[h * ROWS_DEV : (h + 1) * ROWS_DEV].astype(F32)
        mine = jnp.where(prefix, mine, F32(0))
        out_ref[:32, columns] = (hidden[:, columns].astype(F32) + mine).astype(BF)


def prepare(prefix_len, question, queries, hidden_in, key_cache, value_cache):
    rows, width = queries.shape
    return pl.pallas_call(
        prepare_kernel,
        out_shape=in_vmem(((rows + 16, width + LANE), BF)),
        in_specs=[HBM] * 6,
        out_specs=VMEM,
        scratch_shapes=[
            pltpu.VMEM((rows, width), BF),
            pltpu.VMEM((rows, width), BF),
            pltpu.VMEM((rows, 2 * HEAD_DIM), BF),
            pltpu.SMEM(prefix_len.shape, jnp.int32),
            pltpu.SMEM(question.shape, jnp.int32),
            pltpu.SemaphoreType.DMA((6,)),
        ],
        compiler_params=PARAMS,
    )(*map(in_hbm, (prefix_len, question, queries, hidden_in, key_cache, value_cache)))


FAR = 4


def project_kernel(tiles, early, length_ref, gain_ref, mine_ref, theirs_ref, gate_hbm, up_hbm, *refs):
    own_ref, give, kept, far_low, far_high = refs[0], refs[1:6], refs[6:13], refs[13], refs[14]
    residual, rows, squares, gain, gate_ref, up_ref, sems = refs[15:]
    n = ROWS_DEV
    width = own_ref.shape[1]
    half = width // 2
    wide = 2 * tiles + 1
    batch_index, mp_index = lax.axis_index("batch"), lax.axis_index("mp")
    z, core = batch_index >> 1, mp_index & 1
    flip = (batch_index & 1) ^ core
    fetch = pltpu.make_async_copy(gain_ref.at[pl.ds(batch_index * width, width)], gain, sems.at[0])
    fetch_gate = pltpu.make_async_copy(gate_hbm, gate_ref, sems.at[1])
    fetch_up = pltpu.make_async_copy(up_hbm, up_ref, sems.at[2])
    fetch.start()
    fetch_gate.start()
    fetch_up.start()

    def put(s, j, tile, value):
        lanes = slice(tile * LANE, (tile + 1) * LANE)
        if tile < early:
            if j == 1 and s in (0, FAR):
                give[s][:, lanes] = value
            elif j == 1:
                give[min(s, ZN - s)][0 if s < FAR else 1, :, lanes] = value
            elif s == FAR:
                far_low[:, lanes] = value
            else:
                kept[s if s < FAR else s - 1][:, lanes] = value
        else:
            late = tile - early + j * (wide - early)
            if s == FAR:
                far_high[:, late * LANE : (late + 1) * LANE] = value
            else:
                late += early
                kept[s if s < FAR else s - 1][:, late * LANE : (late + 1) * LANE] = value

    blocks = [(ref, i) for ref in (mine_ref, theirs_ref) for i in range(ZN)]
    options = ROWS_DEV - PREFIX

    def gathered(lanes):
        return jnp.concatenate([ref[i, n:, lanes] for ref, i in blocks], axis=0)

    def unfolded(first):
        low, high = slice(first, first + HEAD_DIM), slice(first + 2 * HEAD_DIM, first + 3 * HEAD_DIM)
        return jnp.concatenate(
            [ref[i, n:, lanes] for ref, i in blocks for lanes in (low, high)], axis=0
        )

    keys, values = unfolded(0), unfolded(HEAD_DIM)
    shape = (16 * len(blocks), n * len(blocks))
    asked = gathered(slice(width, width + LANE)).astype(F32).astype(jnp.int32)
    asked = jnp.concatenate([asked] * (shape[1] // LANE), axis=1)
    place = lax.broadcasted_iota(jnp.int32, shape, 1)
    order = place >> 5
    row = lax.broadcasted_iota(jnp.int32, shape, 0)
    owner = ((order & (ZN - 1)) << 1) + ((order >> 3) ^ core)
    live = jnp.zeros(shape, jnp.int32)
    for i in range(len(blocks)):
        live = jnp.where(order == i, length_ref[((i & (ZN - 1)) << 1) + ((i >> 3) ^ core)], live)
    seen = (owner == asked) & ((place & (n - 1)) < live)
    seen = seen | (place == (row >> 4) * n + PREFIX + (row & (options - 1)))
    contexts = []
    for h in range(half // HEAD_DIM):
        queries = gathered(slice(half + h * HEAD_DIM, half + (h + 1) * HEAD_DIM))
        attention = softmax(scored(queries, keys), seen)
        context = jnp.dot(attention, values, preferred_element_type=F32)
        contexts.append(context.astype(BF).astype(F32))
    fetch.wait()
    scale = gain[...].reshape(1, width)
    for k, (ref, i) in enumerate(blocks):
        at = k * 16
        added = jnp.concatenate(
            [context[at : at + options] for context in contexts]
            + [context[at + options : at + 16] for context in contexts],
            axis=1,
        )
        added = jnp.concatenate([jnp.zeros((16 - options, width), F32), added], axis=0)
        first = ref[i, :16, :width]
        last = (ref[i, 16:n, :width].astype(F32) + added).astype(BF)
        if ref is mine_ref:
            residual[i, :16] = first
            residual[i, 16:] = last
        s = (i - z) & (ZN - 1)
        j = flip if ref is mine_ref else 1 - flip
        at = pl.multiple_of(s * 2 * n + j * n, n)
        for part, offset in ((first, 0), (last, 16)):
            x = part.astype(F32)
            into = pl.ds(pl.multiple_of(at + offset, 16), 16)
            rows[into, :] = (x * scale).astype(BF)
            square = x * x
            total = square[:, :LANE]
            for lane in range(1, width // LANE):
                total = total + square[:, lane * LANE : (lane + 1) * LANE]
            squares[into, :] = total.astype(BF)
    own_ref[...] = residual[mp_index >> 1]

    for first, ref, at in [
        (base + t, ref, t) for base, ref in ((0, gate_ref), (tiles, up_ref)) for t in range(0, tiles, 2)
    ] + [(wide - 1, None, 0)]:
        if at == 0 and ref is not None:
            (fetch_gate if ref is gate_ref else fetch_up).wait()
        if ref is None:
            product = squares[...]
        else:
            lanes = slice(at * LANE, min(at + 2, tiles) * LANE)
            product = jnp.dot(rows[...], ref[:, lanes], preferred_element_type=F32).astype(BF)
        for t in range(product.shape[1] // LANE):
            for s in range(ZN):
                for j in range(2):
                    begin = (2 * s + j) * n
                    put(s, j, first + t, product[begin : begin + n, t * LANE : (t + 1) * LANE])


EARLY = 22


def project(prefix_len, norm_gain, mine, theirs, gate_weight, up_weight):
    width, hidden_width = gate_weight.shape
    tiles = hidden_width // LANE
    n = ROWS_DEV
    low = (n, EARLY * LANE)
    high = (n, 2 * (2 * tiles + 1 - EARLY) * LANE)
    whole = (n, low[1] + high[1])
    own = (n, width)
    refs = pl.pallas_call(
        lambda *refs: project_kernel(tiles, EARLY, *refs),
        out_shape=in_vmem(
            (own, BF), (low, BF), *[((2, *low), BF)] * 3, (low, BF), *[(whole, BF)] * 7, (low, BF), (high, BF)
        ),
        in_specs=[SMEM, HBM, VMEM, VMEM, HBM, HBM],
        out_specs=(VMEM,) * 15,
        scratch_shapes=[
            pltpu.VMEM((ZN, n, width), BF),
            pltpu.VMEM((2 * ZN * n, width), BF),
            pltpu.VMEM((2 * ZN * n, LANE), BF),
            pltpu.VMEM((width,), F32),
            pltpu.VMEM(gate_weight.shape, BF),
            pltpu.VMEM(up_weight.shape, BF),
            pltpu.SemaphoreType.DMA((3,)),
        ],
        compiler_params=PARAMS,
    )(prefix_len, in_hbm(norm_gain), mine, theirs, in_hbm(gate_weight), in_hbm(up_weight))
    kept = list(refs[6:13])
    return refs[0], refs[1:6], kept[:4] + [None] + kept[4:], refs[13], refs[14]


def add_first_kernel(low_ref, x_ref, out_ref):
    out_ref[...] = (low_ref[...].astype(F32) + x_ref[...].astype(F32)).astype(BF)


def add_far_kernel(mine_up, mine_down, x, up, down, out_up, out_down):
    low = x.shape[2]
    out_up[:, :low] = (
        mine_up[:, :low].astype(F32) + x[0].astype(F32) + up[...].astype(F32)
    ).astype(BF)
    out_up[:, low:] = mine_up[:, low:]
    out_down[:, :low] = (mine_down[:, :low].astype(F32) + x[1].astype(F32)).astype(BF)
    out_down[:, low:] = (mine_down[:, low:].astype(F32) + down[...].astype(F32)).astype(BF)


def add_ring_kernel(mine_up, mine_down, x, up, down, out_up, out_down):
    low = x.shape[2]
    for mine, i, come, out in ((mine_up, 0, up, out_up), (mine_down, 1, down, out_down)):
        out[:, :low] = (
            mine[:, :low].astype(F32) + x[i].astype(F32) + come[:, :low].astype(F32)
        ).astype(BF)
        out[:, low:] = (mine[:, low:].astype(F32) + come[:, low:].astype(F32)).astype(BF)


def add_last_kernel(mine, x, up, down, keep, give):
    low, wide = x.shape[1], keep.shape[1]
    keep[:, :low] = (
        mine[:, :low].astype(F32)
        + x[...].astype(F32)
        + up[:, :low].astype(F32)
        + down[:, :low].astype(F32)
    )
    keep[:, low:] = (
        mine[:, low:wide].astype(F32) + up[:, low:wide].astype(F32) + down[:, low:wide].astype(F32)
    )
    give[...] = (
        mine[:, wide:].astype(F32) + up[:, wide:].astype(F32) + down[:, wide:].astype(F32)
    ).astype(BF)


def local(kernel, shapes, *args):
    return pl.pallas_call(
        kernel,
        out_shape=in_vmem(*shapes),
        in_specs=[VMEM] * len(args),
        out_specs=(VMEM,) * len(shapes) if len(shapes) > 1 else VMEM,
        compiler_params=PARAMS,
    )(*args)


def gated_kernel(keep, x, out):
    hidden_width = out.shape[1]
    wide = keep.shape[1]
    low = wide - x.shape[1]
    late = keep[:, low:] + x[...].astype(F32)
    squares = late[:, 2 * hidden_width - low :]
    scale = lax.rsqrt(jnp.sum(squares, axis=1, keepdims=True) * F32(1 / 16384) + 1e-05)
    gate = keep[:, :hidden_width] * scale
    lift = jnp.concatenate([keep[:, hidden_width:low], late[:, : 2 * hidden_width - low]], axis=1) * scale
    out[...] = (gate / (1 + jnp.exp(-gate)) * lift).astype(BF)


def down_kernel(*refs):
    own, up1, down1, up2, down2, up3, down3, up4, down4, x0, x1, x2, x3, x4, down_ref = refs[:15]
    give, keep, rows = refs[15:]
    n = ROWS_DEV
    batch_index, mp_index = lax.axis_index("batch"), lax.axis_index("mp")
    z, flip = batch_index >> 1, (batch_index ^ mp_index) & 1
    ours = {0: own, 1: down1, 2: down2, 3: down3, 5: up3, 6: up2, 7: up1}
    partners = {0: x0, 7: x1.at[0], 1: x1.at[1], 6: x2.at[0], 2: x2.at[1], 5: x3.at[0], 3: x3.at[1], FAR: x4}
    for s in range(ZN):
        for j, found in enumerate((ours, partners)):
            target = (z + s) & (ZN - 1)
            other = (flip + j) & 1
            at = pl.ds(pl.multiple_of((1 - other) * ZN * n + target * n, n), n)
            if s in found:
                rows[at, :] = found[s][...]
            else:
                rows[at, : up4.shape[1]] = up4[...]
                rows[at, up4.shape[1] :] = down4[...]
    step = 2 * LANE
    for i in range(0, down_ref.shape[1], step):
        lanes = slice(i, i + step)
        product = jnp.dot(rows[...], down_ref[:, lanes], preferred_element_type=F32)
        for target in range(ZN):
            give[target, :, lanes] = product[target * n : (target + 1) * n].astype(BF)
            at = (ZN + target) * n
            keep[target, :, lanes] = product[at : at + n]


def project_down(blocks, down_weight):
    hidden_width, width = down_weight.shape
    shape = (ZN, ROWS_DEV, width)
    return pl.pallas_call(
        down_kernel,
        out_shape=in_vmem((shape, BF), (shape, F32)),
        in_specs=[VMEM] * (len(blocks) + 1),
        out_specs=(VMEM, VMEM),
        scratch_shapes=[pltpu.VMEM((2 * ZN * ROWS_DEV, hidden_width), BF)],
        compiler_params=PARAMS,
    )(*blocks, down_weight)


def add_core_kernel(keep, come, out):
    out[...] = (keep[...] + come[...].astype(F32)).astype(BF)


def finish_kernel(own, parts, out):
    total = own[...].astype(F32)
    for i in range(parts.shape[0]):
        total = total + parts[i].astype(F32)
    out[...] = total.astype(BF)


def after(*values):
    return lax.optimization_barrier(values)


def body(
    hidden_in,
    queries,
    key_cache,
    value_cache,
    question,
    prefix_len,
    norm_gain,
    gate_weight,
    up_weight,
    down_weight,
):
    rows, width = queries.shape
    hidden_width = gate_weight.shape[1]

    sent = prepare(prefix_len, question, queries, hidden_in, key_cache, value_cache)
    came = transpose_mesh(sent)
    mine = over_plane(jnp.broadcast_to(came[None], (ZN, *came.shape)))
    theirs = core_pair(mine)
    own, give, kept, far_low, far_high = project(
        prefix_len, norm_gain, mine, theirs, gate_weight, up_weight
    )
    low, whole = far_low.shape, kept[0].shape

    far, ahead = after(give[4], give[3])
    far, x = x_pair(far), x_pair(ahead)
    up, down, ahead = after(local(add_first_kernel, [(low, BF)], far_low, far), far_high, give[2])
    up, down, following = along_z(up, 1), along_z(down, -1), x_pair(ahead)
    up, down, x = after(up, down, x)
    up, down = local(add_far_kernel, [(whole, BF)] * 2, kept[3], kept[5], x, up, down)
    for step in (2, 1):
        up, down, ahead = after(up, down, give[step - 1])
        x = following
        up, down, following = along_z(up, 1), along_z(down, -1), x_pair(ahead)
        up, down, x = after(up, down, x)
        up, down = local(
            add_ring_kernel, [(whole, BF)] * 2, kept[step], kept[ZN - step], x, up, down
        )
    up, down = after(up, down)
    up, down, x = after(along_z(up, 1), along_z(down, -1), following)
    late = whole[1] - 2 * hidden_width - LANE
    keep, last = local(
        add_last_kernel,
        [((rows, 2 * hidden_width + LANE), F32), ((rows, late), BF)],
        kept[0],
        x,
        up,
        down,
    )
    hidden = local(gated_kernel, [((rows, hidden_width), BF)], keep, x_pair(last))

    up, down, across = hidden, hidden, hidden
    blocks, partners = [hidden], []
    for step in range(3):
        up, down, across = after(up, down, across)
        up, down, came = along_z(up, 1), along_z(down, -1), x_pair(across)
        up, down = after(up, down)
        partners.append(came)
        blocks += [up, down]
        across = jnp.stack([up, down])
    half = (hidden_width // LANE + 1) // 2 * LANE
    up, down, across = after(up[:, :half], down[:, half:], across)
    up, down, came = along_z(up, 1), along_z(down, -1), x_pair(across)
    up, down = after(up, down)
    partners += [came, x_pair(jnp.concatenate([up, down], axis=1))]
    blocks += [up, down, *partners]
    send, keep = project_down(blocks, down_weight)
    held = local(add_core_kernel, [(keep.shape, BF)], keep, core_pair(send))
    parts = over_plane(held)
    return pl.pallas_call(
        finish_kernel,
        out_shape=jax.ShapeDtypeStruct((rows, width), BF),
        in_specs=[VMEM, VMEM],
        out_specs=VMEM,
        compiler_params=PARAMS,
    )(own, parts)


def solution(mesh):
    return jax.shard_map(
        body,
        mesh=mesh,
        in_specs=(
            P("batch", None),
            P("batch", "mp"),
            P("batch", None),
            P("batch", None),
            P("batch"),
            P(),
            P(),
            P("batch", "mp"),
            P("batch", "mp"),
            P("mp", "batch"),
        ),
        out_specs=P("mp", "batch"),
        check_vma=False,
    )
```

```python
import jax
import jax.numpy as jnp
from jax import lax
from jax.experimental import pallas as pl
from jax.experimental.pallas import tpu as pltpu
from jax.sharding import PartitionSpec as P

HEADS = 128
KV_HEADS = 8
HEAD_DIM = 128
PREFIX = 24
ROWS_DEV = 32
ZN = 8
LANE = 128
BF = jnp.bfloat16
F32 = jnp.float32
PLANE = [[2 * i + core for i in range(8)] for core in range(2)]
VMEM = pl.BlockSpec(memory_space=pltpu.VMEM)
SMEM = pl.BlockSpec(memory_space=pltpu.SMEM)
ANY = pl.BlockSpec(memory_space=pl.ANY)
HBM = pl.BlockSpec(memory_space=pltpu.HBM)
PARAMS = pltpu.CompilerParams(vmem_limit_bytes=28 * 2**20)


def permute(value, axis, target, count=16):
    return lax.ppermute(value, axis, [(i, target(i)) for i in range(count)])


def along_z(value, step):
    return permute(value, "batch", lambda i: (i + 2 * step) % 16)


def x_pair(value):
    return permute(value, "batch", lambda i: i ^ 1)


def core_pair(value):
    return permute(value, "mp", lambda i: i ^ 1)


def transpose_mesh(value):
    return lax.ppermute(
        value,
        ("batch", "mp"),
        [(b * 16 + m, m * 16 + b) for b in range(16) for m in range(16)],
    )


def over_plane(value):
    return lax.all_to_all(value, "mp", 0, 0, axis_index_groups=PLANE, tiled=True)


def in_vmem(*shapes):
    made = tuple(pltpu.VMEM(shape, dtype) for shape, dtype in shapes)
    return made if len(made) > 1 else made[0]


def in_hbm(value):
    return pltpu.with_memory_space_constraint(value, pltpu.HBM)


def softmax(scores, seen):
    scores = jnp.where(seen, scores * F32(HEAD_DIM**-0.5), F32(-1e30))
    exponent = jnp.exp(scores - jnp.max(scores, axis=1, keepdims=True))
    return (exponent / jnp.sum(exponent, axis=1, keepdims=True)).astype(BF)


def scored(queries, keys):
    return lax.dot_general(queries, keys, (((1,), (1,)), ((), ())), preferred_element_type=F32)


def prepare_kernel(lengths, questions, queries_ref, hidden_ref, key_ref, value_ref, out_ref, queries, hidden, pair, length_ref, question_ref, sems):
    width = queries.shape[1]
    heads = width // HEAD_DIM
    batch_index, mp_index = lax.axis_index("batch"), lax.axis_index("mp")
    head = pl.ds(pl.multiple_of((mp_index >> 1) * HEAD_DIM, HEAD_DIM), HEAD_DIM)
    at = pl.ds(pl.multiple_of(mp_index * width, width), width)
    copies = [
        pltpu.make_async_copy(source, target, sems.at[i])
        for i, (source, target) in enumerate(
            [
                (key_ref.at[:, head], pair.at[:, :HEAD_DIM]),
                (queries_ref, queries),
                (value_ref.at[:, head], pair.at[:, HEAD_DIM:]),
                (hidden_ref.at[:, at], hidden),
                (lengths, length_ref),
                (questions, question_ref),
            ]
        )
    ]
    for copy in copies:
        copy.start()
    copies[4].wait()
    copies[5].wait()
    shape = (ROWS_DEV, ROWS_DEV)
    row = lax.broadcasted_iota(jnp.int32, shape, 0)
    key = lax.broadcasted_iota(jnp.int32, shape, 1)
    seen = (key <= row) & (key < length_ref[batch_index])
    seen = jnp.concatenate([seen.astype(F32)] * heads, axis=0) > 0
    shape = (16, LANE)
    option = lax.broadcasted_iota(jnp.int32, shape, 0) & (ROWS_DEV - PREFIX - 1)
    asked = jnp.zeros(shape, jnp.int32)
    for i in range(ROWS_DEV - PREFIX):
        asked = jnp.where(option == i, question_ref[i], asked)
    out_ref[32:, width:] = asked.astype(F32).astype(BF)
    out_ref[:32, width:] = jnp.zeros((ROWS_DEV, LANE), BF)
    copies[0].wait()
    copies[1].wait()
    stacked = jnp.concatenate(
        [queries[:, h * HEAD_DIM : (h + 1) * HEAD_DIM] for h in range(heads)], axis=0
    )
    attention = softmax(scored(stacked, pair[:, :HEAD_DIM]), seen)
    copies[2].wait()
    context = jnp.dot(attention, pair[:, HEAD_DIM:], preferred_element_type=F32).astype(BF)
    out_ref[32:, : 2 * HEAD_DIM] = pair[:16]
    out_ref[32:, 2 * HEAD_DIM : 4 * HEAD_DIM] = pair[16:]
    last = queries[16:].astype(F32)[PREFIX - 16 :]
    half = width // 2
    out_ref[32:, half:width] = jnp.concatenate([last[:, :half], last[:, half:]], axis=0).astype(BF)
    copies[3].wait()
    prefix = lax.broadcasted_iota(jnp.int32, (ROWS_DEV, HEAD_DIM), 0) < PREFIX
    for h in range(heads):
        columns = slice(h * HEAD_DIM, (h + 1) * HEAD_DIM)
        mine = context[h * ROWS_DEV : (h + 1) * ROWS_DEV].astype(F32)
        mine = jnp.where(prefix, mine, F32(0))
        out_ref[:32, columns] = (hidden[:, columns].astype(F32) + mine).astype(BF)


def prepare(prefix_len, question, queries, hidden_in, key_cache, value_cache):
    rows, width = queries.shape
    return pl.pallas_call(
        prepare_kernel,
        out_shape=in_vmem(((rows + 16, width + LANE), BF)),
        in_specs=[HBM] * 6,
        out_specs=VMEM,
        scratch_shapes=[
            pltpu.VMEM((rows, width), BF),
            pltpu.VMEM((rows, width), BF),
            pltpu.VMEM((rows, 2 * HEAD_DIM), BF),
            pltpu.SMEM(prefix_len.shape, jnp.int32),
            pltpu.SMEM(question.shape, jnp.int32),
            pltpu.SemaphoreType.DMA((6,)),
        ],
        compiler_params=PARAMS,
    )(*map(in_hbm, (prefix_len, question, queries, hidden_in, key_cache, value_cache)))


FAR = 4


def project_kernel(tiles, early, length_ref, gain_ref, mine_ref, theirs_ref, gate_hbm, up_hbm, *refs):
    own_ref, give, kept, far_low, far_high = refs[0], refs[1:6], refs[6:13], refs[13], refs[14]
    residual, rows, squares, gain, gate_ref, up_ref, sems = refs[15:]
    n = ROWS_DEV
    width = own_ref.shape[1]
    half = width // 2
    wide = 2 * tiles + 1
    batch_index, mp_index = lax.axis_index("batch"), lax.axis_index("mp")
    z, core = batch_index >> 1, mp_index & 1
    flip = (batch_index & 1) ^ core
    fetch = pltpu.make_async_copy(gain_ref.at[pl.ds(batch_index * width, width)], gain, sems.at[0])
    fetch_gate = pltpu.make_async_copy(gate_hbm, gate_ref, sems.at[1])
    fetch_up = pltpu.make_async_copy(up_hbm, up_ref, sems.at[2])
    fetch.start()
    fetch_gate.start()
    fetch_up.start()

    def put(s, j, tile, value):
        lanes = slice(tile * LANE, (tile + 1) * LANE)
        if tile < early:
            if j == 1 and s in (0, FAR):
                give[s][:, lanes] = value
            elif j == 1:
                give[min(s, ZN - s)][0 if s < FAR else 1, :, lanes] = value
            elif s == FAR:
                far_low[:, lanes] = value
            else:
                kept[s if s < FAR else s - 1][:, lanes] = value
        else:
            late = tile - early + j * (wide - early)
            if s == FAR:
                far_high[:, late * LANE : (late + 1) * LANE] = value
            else:
                late += early
                kept[s if s < FAR else s - 1][:, late * LANE : (late + 1) * LANE] = value

    blocks = [(ref, i) for ref in (mine_ref, theirs_ref) for i in range(ZN)]
    options = ROWS_DEV - PREFIX

    def gathered(lanes):
        return jnp.concatenate([ref[i, n:, lanes] for ref, i in blocks], axis=0)

    def unfolded(first):
        low, high = slice(first, first + HEAD_DIM), slice(first + 2 * HEAD_DIM, first + 3 * HEAD_DIM)
        return jnp.concatenate(
            [ref[i, n:, lanes] for ref, i in blocks for lanes in (low, high)], axis=0
        )

    keys, values = unfolded(0), unfolded(HEAD_DIM)
    shape = (16 * len(blocks), n * len(blocks))
    asked = gathered(slice(width, width + LANE)).astype(F32).astype(jnp.int32)
    asked = jnp.concatenate([asked] * (shape[1] // LANE), axis=1)
    place = lax.broadcasted_iota(jnp.int32, shape, 1)
    order = place >> 5
    row = lax.broadcasted_iota(jnp.int32, shape, 0)
    owner = ((order & (ZN - 1)) << 1) + ((order >> 3) ^ core)
    live = jnp.zeros(shape, jnp.int32)
    for i in range(len(blocks)):
        live = jnp.where(order == i, length_ref[((i & (ZN - 1)) << 1) + ((i >> 3) ^ core)], live)
    seen = (owner == asked) & ((place & (n - 1)) < live)
    seen = seen | (place == (row >> 4) * n + PREFIX + (row & (options - 1)))
    contexts = []
    for h in range(half // HEAD_DIM):
        queries = gathered(slice(half + h * HEAD_DIM, half + (h + 1) * HEAD_DIM))
        attention = softmax(scored(queries, keys), seen)
        context = jnp.dot(attention, values, preferred_element_type=F32)
        contexts.append(context.astype(BF).astype(F32))
    fetch.wait()
    scale = gain[...].reshape(1, width)
    for k, (ref, i) in enumerate(blocks):
        at = k * 16
        added = jnp.concatenate(
            [context[at : at + options] for context in contexts]
            + [context[at + options : at + 16] for context in contexts],
            axis=1,
        )
        added = jnp.concatenate([jnp.zeros((16 - options, width), F32), added], axis=0)
        first = ref[i, :16, :width]
        last = (ref[i, 16:n, :width].astype(F32) + added).astype(BF)
        if ref is mine_ref:
            residual[i, :16] = first
            residual[i, 16:] = last
        s = (i - z) & (ZN - 1)
        j = flip if ref is mine_ref else 1 - flip
        at = pl.multiple_of(s * 2 * n + j * n, n)
        for part, offset in ((first, 0), (last, 16)):
            x = part.astype(F32)
            into = pl.ds(pl.multiple_of(at + offset, 16), 16)
            rows[into, :] = (x * scale).astype(BF)
            square = x * x
            total = square[:, :LANE]
            for lane in range(1, width // LANE):
                total = total + square[:, lane * LANE : (lane + 1) * LANE]
            squares[into, :] = total.astype(BF)
    own_ref[...] = residual[mp_index >> 1]

    for first, ref, at in [
        (base + t, ref, t) for base, ref in ((0, gate_ref), (tiles, up_ref)) for t in range(0, tiles, 2)
    ] + [(wide - 1, None, 0)]:
        if at == 0 and ref is not None:
            (fetch_gate if ref is gate_ref else fetch_up).wait()
        if ref is None:
            product = squares[...]
        else:
            lanes = slice(at * LANE, min(at + 2, tiles) * LANE)
            product = jnp.dot(rows[...], ref[:, lanes], preferred_element_type=F32).astype(BF)
        for t in range(product.shape[1] // LANE):
            for s in range(ZN):
                for j in range(2):
                    begin = (2 * s + j) * n
                    put(s, j, first + t, product[begin : begin + n, t * LANE : (t + 1) * LANE])


EARLY = 22


def project(prefix_len, norm_gain, mine, theirs, gate_weight, up_weight):
    width, hidden_width = gate_weight.shape
    tiles = hidden_width // LANE
    n = ROWS_DEV
    low = (n, EARLY * LANE)
    high = (n, 2 * (2 * tiles + 1 - EARLY) * LANE)
    whole = (n, low[1] + high[1])
    own = (n, width)
    refs = pl.pallas_call(
        lambda *refs: project_kernel(tiles, EARLY, *refs),
        out_shape=in_vmem(
            (own, BF), (low, BF), *[((2, *low), BF)] * 3, (low, BF), *[(whole, BF)] * 7, (low, BF), (high, BF)
        ),
        in_specs=[SMEM, HBM, VMEM, VMEM, HBM, HBM],
        out_specs=(VMEM,) * 15,
        scratch_shapes=[
            pltpu.VMEM((ZN, n, width), BF),
            pltpu.VMEM((2 * ZN * n, width), BF),
            pltpu.VMEM((2 * ZN * n, LANE), BF),
            pltpu.VMEM((width,), F32),
            pltpu.VMEM(gate_weight.shape, BF),
            pltpu.VMEM(up_weight.shape, BF),
            pltpu.SemaphoreType.DMA((3,)),
        ],
        compiler_params=PARAMS,
    )(prefix_len, in_hbm(norm_gain), mine, theirs, in_hbm(gate_weight), in_hbm(up_weight))
    kept = list(refs[6:13])
    return refs[0], refs[1:6], kept[:4] + [None] + kept[4:], refs[13], refs[14]


def add_first_kernel(low_ref, x_ref, out_ref):
    out_ref[...] = (low_ref[...].astype(F32) + x_ref[...].astype(F32)).astype(BF)


def add_far_kernel(mine_up, mine_down, x, up, down, out_up, out_down):
    low = x.shape[2]
    out_up[:, :low] = (
        mine_up[:, :low].astype(F32) + x[0].astype(F32) + up[...].astype(F32)
    ).astype(BF)
    out_up[:, low:] = mine_up[:, low:]
    out_down[:, :low] = (mine_down[:, :low].astype(F32) + x[1].astype(F32)).astype(BF)
    out_down[:, low:] = (mine_down[:, low:].astype(F32) + down[...].astype(F32)).astype(BF)


def add_ring_kernel(mine_up, mine_down, x, up, down, out_up, out_down):
    low = x.shape[2]
    for mine, i, come, out in ((mine_up, 0, up, out_up), (mine_down, 1, down, out_down)):
        out[:, :low] = (
            mine[:, :low].astype(F32) + x[i].astype(F32) + come[:, :low].astype(F32)
        ).astype(BF)
        out[:, low:] = (mine[:, low:].astype(F32) + come[:, low:].astype(F32)).astype(BF)


def add_last_kernel(mine, x, up, down, keep, give):
    low, wide = x.shape[1], keep.shape[1]
    keep[:, :low] = (
        mine[:, :low].astype(F32)
        + x[...].astype(F32)
        + up[:, :low].astype(F32)
        + down[:, :low].astype(F32)
    )
    keep[:, low:] = (
        mine[:, low:wide].astype(F32) + up[:, low:wide].astype(F32) + down[:, low:wide].astype(F32)
    )
    give[...] = (
        mine[:, wide:].astype(F32) + up[:, wide:].astype(F32) + down[:, wide:].astype(F32)
    ).astype(BF)


def local(kernel, shapes, *args):
    return pl.pallas_call(
        kernel,
        out_shape=in_vmem(*shapes),
        in_specs=[VMEM] * len(args),
        out_specs=(VMEM,) * len(shapes) if len(shapes) > 1 else VMEM,
        compiler_params=PARAMS,
    )(*args)


def gated_kernel(keep, x, out):
    hidden_width = out.shape[1]
    wide = keep.shape[1]
    low = wide - x.shape[1]
    late = keep[:, low:] + x[...].astype(F32)
    squares = late[:, 2 * hidden_width - low :]
    scale = lax.rsqrt(jnp.sum(squares, axis=1, keepdims=True) * F32(1 / 16384) + 1e-05)
    gate = keep[:, :hidden_width] * scale
    lift = jnp.concatenate([keep[:, hidden_width:low], late[:, : 2 * hidden_width - low]], axis=1) * scale
    out[...] = (gate / (1 + jnp.exp(-gate)) * lift).astype(BF)


def down_kernel(*refs):
    own, up1, down1, up2, down2, up3, down3, up4, down4, x0, x1, x2, x3, x4, down_ref = refs[:15]
    give, keep, rows = refs[15:]
    n = ROWS_DEV
    batch_index, mp_index = lax.axis_index("batch"), lax.axis_index("mp")
    z, flip = batch_index >> 1, (batch_index ^ mp_index) & 1
    ours = {0: own, 1: down1, 2: down2, 3: down3, 5: up3, 6: up2, 7: up1}
    partners = {0: x0, 7: x1.at[0], 1: x1.at[1], 6: x2.at[0], 2: x2.at[1], 5: x3.at[0], 3: x3.at[1], FAR: x4}
    for s in range(ZN):
        for j, found in enumerate((ours, partners)):
            target = (z + s) & (ZN - 1)
            other = (flip + j) & 1
            at = pl.ds(pl.multiple_of((1 - other) * ZN * n + target * n, n), n)
            if s in found:
                rows[at, :] = found[s][...]
            else:
                rows[at, : up4.shape[1]] = up4[...]
                rows[at, up4.shape[1] :] = down4[...]
    step = 2 * LANE
    for i in range(0, down_ref.shape[1], step):
        lanes = slice(i, i + step)
        product = jnp.dot(rows[...], down_ref[:, lanes], preferred_element_type=F32)
        for target in range(ZN):
            give[target, :, lanes] = product[target * n : (target + 1) * n].astype(BF)
            at = (ZN + target) * n
            keep[target, :, lanes] = product[at : at + n]


def project_down(blocks, down_weight):
    hidden_width, width = down_weight.shape
    shape = (ZN, ROWS_DEV, width)
    return pl.pallas_call(
        down_kernel,
        out_shape=in_vmem((shape, BF), (shape, F32)),
        in_specs=[VMEM] * (len(blocks) + 1),
        out_specs=(VMEM, VMEM),
        scratch_shapes=[pltpu.VMEM((2 * ZN * ROWS_DEV, hidden_width), BF)],
        compiler_params=PARAMS,
    )(*blocks, down_weight)


def add_core_kernel(keep, come, out):
    out[...] = (keep[...] + come[...].astype(F32)).astype(BF)


def finish_kernel(own, parts, out):
    total = own[...].astype(F32)
    for i in range(parts.shape[0]):
        total = total + parts[i].astype(F32)
    out[...] = total.astype(BF)


def after(*values):
    return lax.optimization_barrier(values)


def body(
    hidden_in,
    queries,
    key_cache,
    value_cache,
    question,
    prefix_len,
    norm_gain,
    gate_weight,
    up_weight,
    down_weight,
):
    rows, width = queries.shape
    hidden_width = gate_weight.shape[1]

    sent = prepare(prefix_len, question, queries, hidden_in, key_cache, value_cache)
    came = transpose_mesh(sent)
    mine = over_plane(jnp.broadcast_to(came[None], (ZN, *came.shape)))
    theirs = core_pair(mine)
    own, give, kept, far_low, far_high = project(
        prefix_len, norm_gain, mine, theirs, gate_weight, up_weight
    )
    low, whole = far_low.shape, kept[0].shape

    far, ahead = after(give[4], give[3])
    far, x = x_pair(far), x_pair(ahead)
    up, down, ahead = after(local(add_first_kernel, [(low, BF)], far_low, far), far_high, give[2])
    up, down, following = along_z(up, 1), along_z(down, -1), x_pair(ahead)
    up, down, x = after(up, down, x)
    up, down = local(add_far_kernel, [(whole, BF)] * 2, kept[3], kept[5], x, up, down)
    for step in (2, 1):
        up, down, ahead = after(up, down, give[step - 1])
        x = following
        up, down, following = along_z(up, 1), along_z(down, -1), x_pair(ahead)
        up, down, x = after(up, down, x)
        up, down = local(
            add_ring_kernel, [(whole, BF)] * 2, kept[step], kept[ZN - step], x, up, down
        )
    up, down = after(up, down)
    up, down, x = after(along_z(up, 1), along_z(down, -1), following)
    late = whole[1] - 2 * hidden_width - LANE
    keep, last = local(
        add_last_kernel,
        [((rows, 2 * hidden_width + LANE), F32), ((rows, late), BF)],
        kept[0],
        x,
        up,
        down,
    )
    hidden = local(gated_kernel, [((rows, hidden_width), BF)], keep, x_pair(last))

    up, down, across = hidden, hidden, hidden
    blocks, partners = [hidden], []
    for step in range(3):
        up, down, across = after(up, down, across)
        up, down, came = along_z(up, 1), along_z(down, -1), x_pair(across)
        if partners:
            up, down, partners[-1] = after(up, down, partners[-1])
        else:
            up, down = after(up, down)
        partners.append(came)
        blocks += [up, down]
        across = jnp.stack([up, down])
    half = (hidden_width // LANE + 1) // 2 * LANE
    up, down, across = after(up[:, :half], down[:, half:], across)
    up, down, came = along_z(up, 1), along_z(down, -1), x_pair(across)
    up, down, partners[-1] = after(up, down, partners[-1])
    partners += [came, x_pair(jnp.concatenate([up, down], axis=1))]
    blocks += [up, down, *partners]
    send, keep = project_down(blocks, down_weight)
    held = local(add_core_kernel, [(keep.shape, BF)], keep, core_pair(send))
    parts = over_plane(held)
    return pl.pallas_call(
        finish_kernel,
        out_shape=jax.ShapeDtypeStruct((rows, width), BF),
        in_specs=[VMEM, VMEM],
        out_specs=VMEM,
        compiler_params=PARAMS,
    )(own, parts)


def solution(mesh):
    return jax.shard_map(
        body,
        mesh=mesh,
        in_specs=(
            P("batch", None),
            P("batch", "mp"),
            P("batch", None),
            P("batch", None),
            P("batch"),
            P(),
            P(),
            P("batch", "mp"),
            P("batch", "mp"),
            P("mp", "batch"),
        ),
        out_specs=P("mp", "batch"),
        check_vma=False,
    )
```

```python
import jax
import jax.numpy as jnp
from jax import lax
from jax.experimental import pallas as pl
from jax.experimental.pallas import tpu as pltpu
from jax.sharding import PartitionSpec as P

HEADS = 128
KV_HEADS = 8
HEAD_DIM = 128
PREFIX = 24
ROWS_DEV = 32
ZN = 8
LANE = 128
BF = jnp.bfloat16
F32 = jnp.float32
PLANE = [[2 * i + core for i in range(8)] for core in range(2)]
VMEM = pl.BlockSpec(memory_space=pltpu.VMEM)
SMEM = pl.BlockSpec(memory_space=pltpu.SMEM)
ANY = pl.BlockSpec(memory_space=pl.ANY)
HBM = pl.BlockSpec(memory_space=pltpu.HBM)
PARAMS = pltpu.CompilerParams(vmem_limit_bytes=28 * 2**20)


def permute(value, axis, target, count=16):
    return lax.ppermute(value, axis, [(i, target(i)) for i in range(count)])


def along_z(value, step):
    return permute(value, "batch", lambda i: (i + 2 * step) % 16)


def x_pair(value):
    return permute(value, "batch", lambda i: i ^ 1)


def core_pair(value):
    return permute(value, "mp", lambda i: i ^ 1)


def transpose_mesh(value):
    return lax.ppermute(
        value,
        ("batch", "mp"),
        [(b * 16 + m, m * 16 + b) for b in range(16) for m in range(16)],
    )


def over_plane(value):
    return lax.all_to_all(value, "mp", 0, 0, axis_index_groups=PLANE, tiled=True)


def in_vmem(*shapes):
    made = tuple(pltpu.VMEM(shape, dtype) for shape, dtype in shapes)
    return made if len(made) > 1 else made[0]


def in_hbm(value):
    return pltpu.with_memory_space_constraint(value, pltpu.HBM)


def softmax(scores, seen):
    scores = jnp.where(seen, scores * F32(HEAD_DIM**-0.5), F32(-1e30))
    exponent = jnp.exp(scores - jnp.max(scores, axis=1, keepdims=True))
    return (exponent / jnp.sum(exponent, axis=1, keepdims=True)).astype(BF)


def scored(queries, keys):
    return lax.dot_general(queries, keys, (((1,), (1,)), ((), ())), preferred_element_type=F32)


def head_copies(key_ref, value_ref, pair, sems):
    at = pl.ds(pl.multiple_of((lax.axis_index("mp") >> 1) * HEAD_DIM, HEAD_DIM), HEAD_DIM)
    return (
        pltpu.make_async_copy(key_ref.at[:, at], pair.at[:, :HEAD_DIM], sems.at[0]),
        pltpu.make_async_copy(value_ref.at[:, at], pair.at[:, HEAD_DIM:], sems.at[1]),
    )


def option_kernel(questions, queries_ref, key_ref, value_ref, out_ref, queries, pair, question_ref, sems):
    width = queries.shape[1]
    copies = (
        *head_copies(key_ref, value_ref, pair, sems),
        pltpu.make_async_copy(queries_ref.at[16:], queries, sems.at[2]),
        pltpu.make_async_copy(questions, question_ref, sems.at[3]),
    )
    for copy in copies:
        copy.start()
    for copy in copies:
        copy.wait()
    shape = (16, LANE)
    option = lax.broadcasted_iota(jnp.int32, shape, 0) & (ROWS_DEV - PREFIX - 1)
    asked = jnp.zeros(shape, jnp.int32)
    for i in range(ROWS_DEV - PREFIX):
        asked = jnp.where(option == i, question_ref[i], asked)
    out_ref[:, width:] = asked.astype(F32).astype(BF)
    out_ref[:, : 2 * HEAD_DIM] = pair[:16]
    out_ref[:, 2 * HEAD_DIM : 4 * HEAD_DIM] = pair[16:]
    last = queries[...].astype(F32)[PREFIX - 16 :]
    half = width // 2
    out_ref[:, half:width] = jnp.concatenate([last[:, :half], last[:, half:]], axis=0).astype(BF)


def prepare_options(question, queries, key_cache, value_cache):
    rows, width = queries.shape
    return pl.pallas_call(
        option_kernel,
        out_shape=in_vmem(((16, width + LANE), BF)),
        in_specs=[HBM] * 4,
        out_specs=VMEM,
        scratch_shapes=[
            pltpu.VMEM((16, width), BF),
            pltpu.VMEM((rows, 2 * HEAD_DIM), BF),
            pltpu.SMEM(question.shape, jnp.int32),
            pltpu.SemaphoreType.DMA((4,)),
        ],
        compiler_params=PARAMS,
    )(*map(in_hbm, (question, queries, key_cache, value_cache)))


def prefix_kernel(lengths, queries_ref, hidden_ref, key_ref, value_ref, out_ref, queries, hidden, pair, length_ref, sems):
    width = queries.shape[1]
    heads = width // HEAD_DIM
    at = pl.ds(pl.multiple_of(lax.axis_index("mp") * width, width), width)
    copies = (
        *head_copies(key_ref, value_ref, pair, sems),
        pltpu.make_async_copy(queries_ref, queries, sems.at[2]),
        pltpu.make_async_copy(lengths, length_ref, sems.at[3]),
        pltpu.make_async_copy(hidden_ref.at[:, at], hidden, sems.at[4]),
    )
    for copy in copies:
        copy.start()
    for copy in copies:
        copy.wait()
    shape = (ROWS_DEV, ROWS_DEV)
    row = lax.broadcasted_iota(jnp.int32, shape, 0)
    key = lax.broadcasted_iota(jnp.int32, shape, 1)
    seen = (key <= row) & (key < length_ref[lax.axis_index("batch")])
    seen = jnp.concatenate([seen.astype(F32)] * heads, axis=0) > 0
    stacked = jnp.concatenate(
        [queries[:, h * HEAD_DIM : (h + 1) * HEAD_DIM] for h in range(heads)], axis=0
    )
    attention = softmax(scored(stacked, pair[:, :HEAD_DIM]), seen)
    context = jnp.dot(attention, pair[:, HEAD_DIM:], preferred_element_type=F32).astype(BF)
    prefix = lax.broadcasted_iota(jnp.int32, (ROWS_DEV, HEAD_DIM), 0) < PREFIX
    for h in range(heads):
        columns = slice(h * HEAD_DIM, (h + 1) * HEAD_DIM)
        mine = context[h * ROWS_DEV : (h + 1) * ROWS_DEV].astype(F32)
        mine = jnp.where(prefix, mine, F32(0))
        out_ref[:, columns] = (hidden[:, columns].astype(F32) + mine).astype(BF)


def prepare_rows(prefix_len, queries, hidden_in, key_cache, value_cache):
    rows, width = queries.shape
    return pl.pallas_call(
        prefix_kernel,
        out_shape=in_vmem(((rows, width), BF)),
        in_specs=[HBM] * 5,
        out_specs=VMEM,
        scratch_shapes=[
            pltpu.VMEM((rows, width), BF),
            pltpu.VMEM((rows, width), BF),
            pltpu.VMEM((rows, 2 * HEAD_DIM), BF),
            pltpu.SMEM(prefix_len.shape, jnp.int32),
            pltpu.SemaphoreType.DMA((5,)),
        ],
        compiler_params=PARAMS,
    )(*map(in_hbm, (prefix_len, queries, hidden_in, key_cache, value_cache)))


FAR = 4


ORDER = (0, 1, 2, 3, 5, 6, 7, FAR)


def products(rows, squares, gate_ref, up_ref, ready):
    tiles = gate_ref.shape[1] // LANE
    for base, ref in ((0, gate_ref), (tiles, up_ref)):
        ready(ref)
        for t in range(0, tiles, 2):
            lanes = slice(t * LANE, min(t + 2, tiles) * LANE)
            product = jnp.dot(rows[...], ref[:, lanes], preferred_element_type=F32).astype(BF)
            for i in range(product.shape[1] // LANE):
                yield base + t + i, product[:, i * LANE : (i + 1) * LANE]
    yield 2 * tiles, squares[...]


def far_kernel(early, length_ref, gain_ref, options, their_options, mine_ref, theirs_ref, gate_hbm, up_hbm, *refs):
    own_ref, rows, squares, gate_ref, up_ref, give, low, high, residual, gain, sems = refs
    n = ROWS_DEV
    width = own_ref.shape[1]
    half = width // 2
    wide = 2 * (gate_ref.shape[1] // LANE) + 1
    batch_index, mp_index = lax.axis_index("batch"), lax.axis_index("mp")
    z, core = batch_index >> 1, mp_index & 1
    flip = (batch_index & 1) ^ core
    fetch = pltpu.make_async_copy(gain_ref.at[pl.ds(batch_index * width, width)], gain, sems.at[0])
    fetch_gate = pltpu.make_async_copy(gate_hbm, gate_ref, sems.at[1])
    fetch_up = pltpu.make_async_copy(up_hbm, up_ref, sems.at[2])
    fetch.start()
    fetch_gate.start()
    fetch_up.start()

    blocks = [(ref, i) for ref in (options, their_options) for i in range(ZN)]
    count = ROWS_DEV - PREFIX

    def gathered(lanes):
        return jnp.concatenate([ref[i, :, lanes] for ref, i in blocks], axis=0)

    def unfolded(first):
        lower, upper = slice(first, first + HEAD_DIM), slice(first + 2 * HEAD_DIM, first + 3 * HEAD_DIM)
        return jnp.concatenate([ref[i, :, lanes] for ref, i in blocks for lanes in (lower, upper)], axis=0)

    keys, values = unfolded(0), unfolded(HEAD_DIM)
    shape = (16 * len(blocks), n * len(blocks))
    asked = gathered(slice(width, width + LANE)).astype(F32).astype(jnp.int32)
    asked = jnp.concatenate([asked] * (shape[1] // LANE), axis=1)
    place = lax.broadcasted_iota(jnp.int32, shape, 1)
    order = place >> 5
    row = lax.broadcasted_iota(jnp.int32, shape, 0)
    owner = ((order & (ZN - 1)) << 1) + ((order >> 3) ^ core)
    live = jnp.zeros(shape, jnp.int32)
    for i in range(len(blocks)):
        live = jnp.where(order == i, length_ref[((i & (ZN - 1)) << 1) + ((i >> 3) ^ core)], live)
    seen = (owner == asked) & ((place & (n - 1)) < live)
    seen = seen | (place == (row >> 4) * n + PREFIX + (row & (count - 1)))
    contexts = []
    for h in range(half // HEAD_DIM):
        queries = gathered(slice(half + h * HEAD_DIM, half + (h + 1) * HEAD_DIM))
        attention = softmax(scored(queries, keys), seen)
        context = jnp.dot(attention, values, preferred_element_type=F32)
        contexts.append(context.astype(BF).astype(F32))
    fetch.wait()
    scale = gain[...].reshape(1, width)
    for k, (ref, i) in enumerate((ref, i) for ref in (mine_ref, theirs_ref) for i in range(ZN)):
        at = k * 16
        added = jnp.concatenate(
            [context[at : at + count] for context in contexts]
            + [context[at + count : at + 16] for context in contexts],
            axis=1,
        )
        added = jnp.concatenate([jnp.zeros((16 - count, width), F32), added], axis=0)
        first = ref[i, :16, :]
        last = (ref[i, 16:, :].astype(F32) + added).astype(BF)
        if ref is mine_ref:
            residual[i, :16] = first
            residual[i, 16:] = last
        s = (i - z) & (ZN - 1)
        j = flip if ref is mine_ref else 1 - flip
        position = jnp.where(s == FAR, ZN - 1, s - (s > FAR).astype(jnp.int32))
        at = pl.multiple_of(position * 2 * n + j * n, n)
        for part, offset in ((first, 0), (last, 16)):
            x = part.astype(F32)
            into = pl.ds(pl.multiple_of(at + offset, 16), 16)
            rows[into, :] = (x * scale).astype(BF)
            square = x * x
            total = square[:, :LANE]
            for lane in range(1, width // LANE):
                total = total + square[:, lane * LANE : (lane + 1) * LANE]
            squares[into, :] = total.astype(BF)
    own_ref[...] = residual[mp_index >> 1]

    begin = (ZN - 1) * 2 * n
    far = slice(begin, begin + 2 * n)
    ready = lambda ref: (fetch_gate if ref is gate_ref else fetch_up).wait()
    for tile, value in products(rows.at[far], squares.at[far], gate_ref, up_ref, ready):
        if tile < early:
            low[:, tile * LANE : (tile + 1) * LANE] = value[:n]
            give[:, tile * LANE : (tile + 1) * LANE] = value[n:]
        else:
            for j in range(2):
                late = tile - early + j * (wide - early)
                high[:, late * LANE : (late + 1) * LANE] = value[j * n : (j + 1) * n]


def near_kernel(early, rows, squares, gate_ref, up_ref, *refs):
    give, kept = refs[:4], refs[4:]
    n = ROWS_DEV
    wide = 2 * (gate_ref.shape[1] // LANE) + 1
    near = slice(0, (ZN - 1) * 2 * n)
    for tile, value in products(rows.at[near], squares.at[near], gate_ref, up_ref, lambda ref: None):
        for k, s in enumerate(ORDER[:-1]):
            for j in range(2):
                part = value[(2 * k + j) * n : (2 * k + j + 1) * n]
                if tile >= early:
                    late = tile + j * (wide - early)
                    kept[k][:, late * LANE : (late + 1) * LANE] = part
                elif j == 0:
                    kept[k][:, tile * LANE : (tile + 1) * LANE] = part
                elif s == 0:
                    give[0][:, tile * LANE : (tile + 1) * LANE] = part
                else:
                    into = give[min(s, ZN - s)]
                    into[0 if s < FAR else 1, :, tile * LANE : (tile + 1) * LANE] = part


EARLY = 22


def project(prefix_len, norm_gain, options, mine, gate_weight, up_weight):
    width, hidden_width = gate_weight.shape
    wide = 2 * (hidden_width // LANE) + 1
    n = ROWS_DEV
    low = (n, EARLY * LANE)
    high = (n, 2 * (wide - EARLY) * LANE)
    whole = (n, low[1] + high[1])
    all_rows = 2 * ZN * n
    own, rows, squares, gate, up, far_give, far_low, far_high = pl.pallas_call(
        lambda *refs: far_kernel(EARLY, *refs),
        out_shape=in_vmem(
            ((n, width), BF),
            ((all_rows, width), BF),
            ((all_rows, LANE), BF),
            (gate_weight.shape, BF),
            (up_weight.shape, BF),
            (low, BF),
            (low, BF),
            (high, BF),
        ),
        in_specs=[SMEM, HBM] + [VMEM] * 4 + [HBM, HBM],
        out_specs=(VMEM,) * 8,
        scratch_shapes=[
            pltpu.VMEM((ZN, n, width), BF),
            pltpu.VMEM((width,), F32),
            pltpu.SemaphoreType.DMA((3,)),
        ],
        compiler_params=PARAMS,
    )(prefix_len, in_hbm(norm_gain), *options, *mine, in_hbm(gate_weight), in_hbm(up_weight))
    refs = local(
        lambda *refs: near_kernel(EARLY, *refs),
        [(low, BF), *[((2, *low), BF)] * 3, *[(whole, BF)] * 7],
        rows,
        squares,
        gate,
        up,
    )
    kept = list(refs[4:])
    return own, [*refs[:4], far_give], kept[:4] + [None] + kept[4:], far_low, far_high


def add_first_kernel(low_ref, x_ref, out_ref):
    out_ref[...] = (low_ref[...].astype(F32) + x_ref[...].astype(F32)).astype(BF)


def add_far_kernel(mine_up, mine_down, x, up, down, out_up, out_down):
    low = x.shape[2]
    out_up[:, :low] = (
        mine_up[:, :low].astype(F32) + x[0].astype(F32) + up[...].astype(F32)
    ).astype(BF)
    out_up[:, low:] = mine_up[:, low:]
    out_down[:, :low] = (mine_down[:, :low].astype(F32) + x[1].astype(F32)).astype(BF)
    out_down[:, low:] = (mine_down[:, low:].astype(F32) + down[...].astype(F32)).astype(BF)


def add_ring_kernel(mine_up, mine_down, x, up, down, out_up, out_down):
    low = x.shape[2]
    for mine, i, come, out in ((mine_up, 0, up, out_up), (mine_down, 1, down, out_down)):
        out[:, :low] = (
            mine[:, :low].astype(F32) + x[i].astype(F32) + come[:, :low].astype(F32)
        ).astype(BF)
        out[:, low:] = (mine[:, low:].astype(F32) + come[:, low:].astype(F32)).astype(BF)


def add_last_kernel(mine, x, up, down, keep, give):
    low, wide = x.shape[1], keep.shape[1]
    keep[:, :low] = (
        mine[:, :low].astype(F32)
        + x[...].astype(F32)
        + up[:, :low].astype(F32)
        + down[:, :low].astype(F32)
    )
    keep[:, low:] = (
        mine[:, low:wide].astype(F32) + up[:, low:wide].astype(F32) + down[:, low:wide].astype(F32)
    )
    give[...] = (
        mine[:, wide:].astype(F32) + up[:, wide:].astype(F32) + down[:, wide:].astype(F32)
    ).astype(BF)


def local(kernel, shapes, *args):
    return pl.pallas_call(
        kernel,
        out_shape=in_vmem(*shapes),
        in_specs=[VMEM] * len(args),
        out_specs=(VMEM,) * len(shapes) if len(shapes) > 1 else VMEM,
        compiler_params=PARAMS,
    )(*args)


def gated_kernel(keep, x, out):
    hidden_width = out.shape[1]
    wide = keep.shape[1]
    low = wide - x.shape[1]
    late = keep[:, low:] + x[...].astype(F32)
    squares = late[:, 2 * hidden_width - low :]
    scale = lax.rsqrt(jnp.sum(squares, axis=1, keepdims=True) * F32(1 / 16384) + 1e-05)
    gate = keep[:, :hidden_width] * scale
    lift = jnp.concatenate([keep[:, hidden_width:low], late[:, : 2 * hidden_width - low]], axis=1) * scale
    out[...] = (gate / (1 + jnp.exp(-gate)) * lift).astype(BF)


def down_kernel(*refs):
    own, up1, down1, up2, down2, up3, down3, up4, down4, x0, x1, x2, x3, x4, down_ref = refs[:15]
    give, keep, rows = refs[15:]
    n = ROWS_DEV
    batch_index, mp_index = lax.axis_index("batch"), lax.axis_index("mp")
    z, flip = batch_index >> 1, (batch_index ^ mp_index) & 1
    ours = {0: own, 1: down1, 2: down2, 3: down3, 5: up3, 6: up2, 7: up1}
    partners = {0: x0, 7: x1.at[0], 1: x1.at[1], 6: x2.at[0], 2: x2.at[1], 5: x3.at[0], 3: x3.at[1], FAR: x4}
    for s in range(ZN):
        for j, found in enumerate((ours, partners)):
            target = (z + s) & (ZN - 1)
            other = (flip + j) & 1
            at = pl.ds(pl.multiple_of((1 - other) * ZN * n + target * n, n), n)
            if s in found:
                rows[at, :] = found[s][...]
            else:
                rows[at, : up4.shape[1]] = up4[...]
                rows[at, up4.shape[1] :] = down4[...]
    step = 2 * LANE
    for i in range(0, down_ref.shape[1], step):
        lanes = slice(i, i + step)
        product = jnp.dot(rows[...], down_ref[:, lanes], preferred_element_type=F32)
        for target in range(ZN):
            give[target, :, lanes] = product[target * n : (target + 1) * n].astype(BF)
            at = (ZN + target) * n
            keep[target, :, lanes] = product[at : at + n]


def project_down(blocks, down_weight):
    hidden_width, width = down_weight.shape
    shape = (ZN, ROWS_DEV, width)
    return pl.pallas_call(
        down_kernel,
        out_shape=in_vmem((shape, BF), (shape, F32)),
        in_specs=[VMEM] * (len(blocks) + 1),
        out_specs=(VMEM, VMEM),
        scratch_shapes=[pltpu.VMEM((2 * ZN * ROWS_DEV, hidden_width), BF)],
        compiler_params=PARAMS,
    )(*blocks, down_weight)


def add_core_kernel(keep, come, out):
    out[...] = (keep[...] + come[...].astype(F32)).astype(BF)


def finish_kernel(own, parts, out):
    total = own[...].astype(F32)
    for i in range(parts.shape[0]):
        total = total + parts[i].astype(F32)
    out[...] = total.astype(BF)


def after(*values):
    return lax.optimization_barrier(values)


def body(
    hidden_in,
    queries,
    key_cache,
    value_cache,
    question,
    prefix_len,
    norm_gain,
    gate_weight,
    up_weight,
    down_weight,
):
    rows, width = queries.shape
    hidden_width = gate_weight.shape[1]

    options = transpose_mesh(prepare_options(question, queries, key_cache, value_cache))
    mine = transpose_mesh(prepare_rows(prefix_len, queries, hidden_in, key_cache, value_cache))
    options = over_plane(jnp.broadcast_to(options[None], (ZN, *options.shape)))
    options, mine = after(options, mine)
    mine = over_plane(jnp.broadcast_to(mine[None], (ZN, *mine.shape)))
    own, give, kept, far_low, far_high = project(
        prefix_len,
        norm_gain,
        (options, core_pair(options)),
        (mine, core_pair(mine)),
        gate_weight,
        up_weight,
    )
    low, whole = far_low.shape, kept[0].shape

    up = local(add_first_kernel, [(low, BF)], far_low, x_pair(give[4]))
    up, down, x = after(up, far_high, give[3])
    x, up, down = x_pair(x), along_z(up, 1), along_z(down, -1)
    up, down, x, ahead = after(up, down, x, give[2])
    following = x_pair(ahead)
    up, down = local(add_far_kernel, [(whole, BF)] * 2, kept[3], kept[5], x, up, down)
    for step in (2, 1):
        up, down, ahead = after(up, down, give[step - 1])
        x = following
        up, down, following = along_z(up, 1), along_z(down, -1), x_pair(ahead)
        up, down, x = after(up, down, x)
        up, down = local(
            add_ring_kernel, [(whole, BF)] * 2, kept[step], kept[ZN - step], x, up, down
        )
    up, down = after(up, down)
    up, down, x = after(along_z(up, 1), along_z(down, -1), following)
    late = whole[1] - 2 * hidden_width - LANE
    keep, last = local(
        add_last_kernel,
        [((rows, 2 * hidden_width + LANE), F32), ((rows, late), BF)],
        kept[0],
        x,
        up,
        down,
    )
    hidden = local(gated_kernel, [((rows, hidden_width), BF)], keep, x_pair(last))

    up, down, across = hidden, hidden, hidden
    blocks, partners = [hidden], []
    for step in range(3):
        up, down, across = after(up, down, across)
        up, down, came = along_z(up, 1), along_z(down, -1), x_pair(across)
        if partners:
            up, down, partners[-1] = after(up, down, partners[-1])
        else:
            up, down = after(up, down)
        partners.append(came)
        blocks += [up, down]
        across = jnp.stack([up, down])
    half = (hidden_width // LANE + 1) // 2 * LANE
    up, down, across = after(up[:, :half], down[:, half:], across)
    up, down, came = along_z(up, 1), along_z(down, -1), x_pair(across)
    up, down, partners[-1] = after(up, down, partners[-1])
    partners += [came, x_pair(jnp.concatenate([up, down], axis=1))]
    blocks += [up, down, *partners]
    send, keep = project_down(blocks, down_weight)
    held = local(add_core_kernel, [(keep.shape, BF)], keep, core_pair(send))
    parts = over_plane(held)
    return pl.pallas_call(
        finish_kernel,
        out_shape=jax.ShapeDtypeStruct((rows, width), BF),
        in_specs=[VMEM, VMEM],
        out_specs=VMEM,
        compiler_params=PARAMS,
    )(own, parts)


def solution(mesh):
    return jax.shard_map(
        body,
        mesh=mesh,
        in_specs=(
            P("batch", None),
            P("batch", "mp"),
            P("batch", None),
            P("batch", None),
            P("batch"),
            P(),
            P(),
            P("batch", "mp"),
            P("batch", "mp"),
            P("mp", "batch"),
        ),
        out_specs=P("mp", "batch"),
        check_vma=False,
    )
```

```python
import jax
import jax.numpy as jnp
from jax import lax
from jax.experimental import pallas as pl
from jax.experimental.pallas import tpu as pltpu
from jax.sharding import PartitionSpec as P

HEADS = 128
KV_HEADS = 8
HEAD_DIM = 128
PREFIX = 24
ROWS_DEV = 32
ZN = 8
LANE = 128
BF = jnp.bfloat16
F32 = jnp.float32
PLANE = [[2 * i + core for i in range(8)] for core in range(2)]
VMEM = pl.BlockSpec(memory_space=pltpu.VMEM)
SMEM = pl.BlockSpec(memory_space=pltpu.SMEM)
ANY = pl.BlockSpec(memory_space=pl.ANY)
HBM = pl.BlockSpec(memory_space=pltpu.HBM)
PARAMS = pltpu.CompilerParams(vmem_limit_bytes=28 * 2**20)


def permute(value, axis, target, count=16):
    return lax.ppermute(value, axis, [(i, target(i)) for i in range(count)])


def along_z(value, step):
    return permute(value, "batch", lambda i: (i + 2 * step) % 16)


def x_pair(value):
    return permute(value, "batch", lambda i: i ^ 1)


def core_pair(value):
    return permute(value, "mp", lambda i: i ^ 1)


def by_core(value, target, cores):
    return lax.ppermute(
        value,
        ("batch", "mp"),
        [(b * 16 + m, target(b, m % 2) * 16 + m) for b in range(16) for m in range(16) if m % 2 in cores],
    )


def transpose_mesh(value):
    return lax.ppermute(
        value,
        ("batch", "mp"),
        [(b * 16 + m, m * 16 + b) for b in range(16) for m in range(16)],
    )


def over_plane(value):
    return lax.all_to_all(value, "mp", 0, 0, axis_index_groups=PLANE, tiled=True)


def in_vmem(*shapes):
    made = tuple(pltpu.VMEM(shape, dtype) for shape, dtype in shapes)
    return made if len(made) > 1 else made[0]


def in_hbm(value):
    return pltpu.with_memory_space_constraint(value, pltpu.HBM)


def softmax(scores, seen):
    scores = jnp.where(seen, scores * F32(HEAD_DIM**-0.5), F32(-1e30))
    exponent = jnp.exp(scores - jnp.max(scores, axis=1, keepdims=True))
    return (exponent / jnp.sum(exponent, axis=1, keepdims=True)).astype(BF)


def scored(queries, keys):
    return lax.dot_general(queries, keys, (((1,), (1,)), ((), ())), preferred_element_type=F32)


def prepare_kernel(lengths, questions, queries_ref, hidden_ref, key_ref, value_ref, out_ref, queries, hidden, pair, length_ref, question_ref, sems):
    width = queries.shape[1]
    heads = width // HEAD_DIM
    batch_index, mp_index = lax.axis_index("batch"), lax.axis_index("mp")
    head = pl.ds(pl.multiple_of((mp_index >> 1) * HEAD_DIM, HEAD_DIM), HEAD_DIM)
    at = pl.ds(pl.multiple_of(mp_index * width, width), width)
    copies = [
        pltpu.make_async_copy(source, target, sems.at[i])
        for i, (source, target) in enumerate(
            [
                (key_ref.at[:, head], pair.at[:, :HEAD_DIM]),
                (queries_ref, queries),
                (value_ref.at[:, head], pair.at[:, HEAD_DIM:]),
                (hidden_ref.at[:, at], hidden),
                (lengths, length_ref),
                (questions, question_ref),
            ]
        )
    ]
    for copy in copies:
        copy.start()
    copies[4].wait()
    copies[5].wait()
    shape = (ROWS_DEV, ROWS_DEV)
    row = lax.broadcasted_iota(jnp.int32, shape, 0)
    key = lax.broadcasted_iota(jnp.int32, shape, 1)
    seen = (key <= row) & (key < length_ref[batch_index])
    seen = jnp.concatenate([seen.astype(F32)] * heads, axis=0) > 0
    shape = (16, LANE)
    option = lax.broadcasted_iota(jnp.int32, shape, 0) & (ROWS_DEV - PREFIX - 1)
    asked = jnp.zeros(shape, jnp.int32)
    for i in range(ROWS_DEV - PREFIX):
        asked = jnp.where(option == i, question_ref[i], asked)
    out_ref[32:, width:] = asked.astype(F32).astype(BF)
    out_ref[:32, width:] = jnp.zeros((ROWS_DEV, LANE), BF)
    copies[0].wait()
    copies[1].wait()
    stacked = jnp.concatenate(
        [queries[:, h * HEAD_DIM : (h + 1) * HEAD_DIM] for h in range(heads)], axis=0
    )
    attention = softmax(scored(stacked, pair[:, :HEAD_DIM]), seen)
    copies[2].wait()
    context = jnp.dot(attention, pair[:, HEAD_DIM:], preferred_element_type=F32).astype(BF)
    out_ref[32:, : 2 * HEAD_DIM] = pair[:16]
    out_ref[32:, 2 * HEAD_DIM : 4 * HEAD_DIM] = pair[16:]
    last = queries[16:].astype(F32)[PREFIX - 16 :]
    half = width // 2
    out_ref[32:, half:width] = jnp.concatenate([last[:, :half], last[:, half:]], axis=0).astype(BF)
    copies[3].wait()
    prefix = lax.broadcasted_iota(jnp.int32, (ROWS_DEV, HEAD_DIM), 0) < PREFIX
    for h in range(heads):
        columns = slice(h * HEAD_DIM, (h + 1) * HEAD_DIM)
        mine = context[h * ROWS_DEV : (h + 1) * ROWS_DEV].astype(F32)
        mine = jnp.where(prefix, mine, F32(0))
        out_ref[:32, columns] = (hidden[:, columns].astype(F32) + mine).astype(BF)


def prepare(prefix_len, question, queries, hidden_in, key_cache, value_cache):
    rows, width = queries.shape
    return pl.pallas_call(
        prepare_kernel,
        out_shape=in_vmem(((rows + 16, width + LANE), BF)),
        in_specs=[HBM] * 6,
        out_specs=VMEM,
        scratch_shapes=[
            pltpu.VMEM((rows, width), BF),
            pltpu.VMEM((rows, width), BF),
            pltpu.VMEM((rows, 2 * HEAD_DIM), BF),
            pltpu.SMEM(prefix_len.shape, jnp.int32),
            pltpu.SMEM(question.shape, jnp.int32),
            pltpu.SemaphoreType.DMA((6,)),
        ],
        compiler_params=PARAMS,
    )(*map(in_hbm, (prefix_len, question, queries, hidden_in, key_cache, value_cache)))


FAR = 4


def project_kernel(tiles, early, length_ref, gain_ref, mine_ref, theirs_ref, gate_hbm, up_hbm, *refs):
    own_ref, give, kept, far_low, far_high = refs[0], refs[1:6], refs[6:13], refs[13], refs[14]
    residual, rows, squares, gain, gate_ref, up_ref, sems = refs[15:]
    n = ROWS_DEV
    width = own_ref.shape[1]
    half = width // 2
    wide = 2 * tiles + 1
    batch_index, mp_index = lax.axis_index("batch"), lax.axis_index("mp")
    z, core = batch_index >> 1, mp_index & 1
    flip = (batch_index & 1) ^ core
    fetch = pltpu.make_async_copy(gain_ref.at[pl.ds(batch_index * width, width)], gain, sems.at[0])
    fetch_gate = pltpu.make_async_copy(gate_hbm, gate_ref, sems.at[1])
    fetch_up = pltpu.make_async_copy(up_hbm, up_ref, sems.at[2])
    fetch.start()
    fetch_gate.start()
    fetch_up.start()

    def put(s, j, tile, value):
        lanes = slice(tile * LANE, (tile + 1) * LANE)
        if tile < early:
            if j == 1 and s in (0, FAR):
                give[s][:, lanes] = value
            elif j == 1:
                give[min(s, ZN - s)][0 if s < FAR else 1, :, lanes] = value
            elif s == FAR:
                far_low[:, lanes] = value
            else:
                kept[s if s < FAR else s - 1][:, lanes] = value
        else:
            late = tile - early + j * (wide - early)
            if s == FAR:
                far_high[:, late * LANE : (late + 1) * LANE] = value
            else:
                late += early
                kept[s if s < FAR else s - 1][:, late * LANE : (late + 1) * LANE] = value

    blocks = [(ref, i) for ref in (mine_ref, theirs_ref) for i in range(ZN)]
    options = ROWS_DEV - PREFIX

    def gathered(lanes):
        return jnp.concatenate([ref[i, n:, lanes] for ref, i in blocks], axis=0)

    def unfolded(first):
        low, high = slice(first, first + HEAD_DIM), slice(first + 2 * HEAD_DIM, first + 3 * HEAD_DIM)
        return jnp.concatenate(
            [ref[i, n:, lanes] for ref, i in blocks for lanes in (low, high)], axis=0
        )

    keys, values = unfolded(0), unfolded(HEAD_DIM)
    shape = (16 * len(blocks), n * len(blocks))
    asked = gathered(slice(width, width + LANE)).astype(F32).astype(jnp.int32)
    asked = jnp.concatenate([asked] * (shape[1] // LANE), axis=1)
    place = lax.broadcasted_iota(jnp.int32, shape, 1)
    order = place >> 5
    row = lax.broadcasted_iota(jnp.int32, shape, 0)
    owner = ((order & (ZN - 1)) << 1) + ((order >> 3) ^ core)
    live = jnp.zeros(shape, jnp.int32)
    for i in range(len(blocks)):
        live = jnp.where(order == i, length_ref[((i & (ZN - 1)) << 1) + ((i >> 3) ^ core)], live)
    seen = (owner == asked) & ((place & (n - 1)) < live)
    seen = seen | (place == (row >> 4) * n + PREFIX + (row & (options - 1)))
    contexts = []
    for h in range(half // HEAD_DIM):
        queries = gathered(slice(half + h * HEAD_DIM, half + (h + 1) * HEAD_DIM))
        attention = softmax(scored(queries, keys), seen)
        context = jnp.dot(attention, values, preferred_element_type=F32)
        contexts.append(context.astype(BF).astype(F32))
    fetch.wait()
    scale = gain[...].reshape(1, width)
    for k, (ref, i) in enumerate(blocks):
        at = k * 16
        added = jnp.concatenate(
            [context[at : at + options] for context in contexts]
            + [context[at + options : at + 16] for context in contexts],
            axis=1,
        )
        added = jnp.concatenate([jnp.zeros((16 - options, width), F32), added], axis=0)
        first = ref[i, :16, :width]
        last = (ref[i, 16:n, :width].astype(F32) + added).astype(BF)
        if ref is mine_ref:
            residual[i, :16] = first
            residual[i, 16:] = last
        s = (i - z) & (ZN - 1)
        j = flip if ref is mine_ref else 1 - flip
        at = pl.multiple_of(s * 2 * n + j * n, n)
        for part, offset in ((first, 0), (last, 16)):
            x = part.astype(F32)
            into = pl.ds(pl.multiple_of(at + offset, 16), 16)
            rows[into, :] = (x * scale).astype(BF)
            square = x * x
            total = square[:, :LANE]
            for lane in range(1, width // LANE):
                total = total + square[:, lane * LANE : (lane + 1) * LANE]
            squares[into, :] = total.astype(BF)
    own_ref[...] = residual[mp_index >> 1]

    for first, ref, at in [
        (base + t, ref, t) for base, ref in ((0, gate_ref), (tiles, up_ref)) for t in range(0, tiles, 2)
    ] + [(wide - 1, None, 0)]:
        if at == 0 and ref is not None:
            (fetch_gate if ref is gate_ref else fetch_up).wait()
        if ref is None:
            product = squares[...]
        else:
            lanes = slice(at * LANE, min(at + 2, tiles) * LANE)
            product = jnp.dot(rows[...], ref[:, lanes], preferred_element_type=F32).astype(BF)
        for t in range(product.shape[1] // LANE):
            for s in range(ZN):
                for j in range(2):
                    begin = (2 * s + j) * n
                    put(s, j, first + t, product[begin : begin + n, t * LANE : (t + 1) * LANE])


EARLY = 22


def project(prefix_len, norm_gain, mine, theirs, gate_weight, up_weight):
    width, hidden_width = gate_weight.shape
    tiles = hidden_width // LANE
    n = ROWS_DEV
    low = (n, EARLY * LANE)
    high = (n, 2 * (2 * tiles + 1 - EARLY) * LANE)
    whole = (n, low[1] + high[1])
    own = (n, width)
    refs = pl.pallas_call(
        lambda *refs: project_kernel(tiles, EARLY, *refs),
        out_shape=in_vmem(
            (own, BF), (low, BF), *[((2, *low), BF)] * 3, (low, BF), *[(whole, BF)] * 7, (low, BF), (high, BF)
        ),
        in_specs=[SMEM, HBM, VMEM, VMEM, HBM, HBM],
        out_specs=(VMEM,) * 15,
        scratch_shapes=[
            pltpu.VMEM((ZN, n, width), BF),
            pltpu.VMEM((2 * ZN * n, width), BF),
            pltpu.VMEM((2 * ZN * n, LANE), BF),
            pltpu.VMEM((width,), F32),
            pltpu.VMEM(gate_weight.shape, BF),
            pltpu.VMEM(up_weight.shape, BF),
            pltpu.SemaphoreType.DMA((3,)),
        ],
        compiler_params=PARAMS,
    )(prefix_len, in_hbm(norm_gain), mine, theirs, in_hbm(gate_weight), in_hbm(up_weight))
    kept = list(refs[6:13])
    return refs[0], refs[1:6], kept[:4] + [None] + kept[4:], refs[13], refs[14]


def add_first_kernel(low_ref, x_ref, out_ref):
    out_ref[...] = (low_ref[...].astype(F32) + x_ref[...].astype(F32)).astype(BF)


def add_far_kernel(mine_up, mine_down, x, up, down, out_up, out_down):
    low = x.shape[2]
    out_up[:, :low] = (
        mine_up[:, :low].astype(F32) + x[0].astype(F32) + up[...].astype(F32)
    ).astype(BF)
    out_up[:, low:] = mine_up[:, low:]
    out_down[:, :low] = (mine_down[:, :low].astype(F32) + x[1].astype(F32)).astype(BF)
    out_down[:, low:] = (mine_down[:, low:].astype(F32) + down[...].astype(F32)).astype(BF)


def add_ring_kernel(mine_up, mine_down, x, up, down, out_up, out_down):
    low = x.shape[2]
    for mine, i, come, out in ((mine_up, 0, up, out_up), (mine_down, 1, down, out_down)):
        out[:, :low] = (
            mine[:, :low].astype(F32) + x[i].astype(F32) + come[:, :low].astype(F32)
        ).astype(BF)
        out[:, low:] = (mine[:, low:].astype(F32) + come[:, low:].astype(F32)).astype(BF)


def add_last_kernel(mine, x, up, down, keep, give):
    low, wide = x.shape[1], keep.shape[1]
    keep[:, :low] = (
        mine[:, :low].astype(F32)
        + x[...].astype(F32)
        + up[:, :low].astype(F32)
        + down[:, :low].astype(F32)
    )
    keep[:, low:] = (
        mine[:, low:wide].astype(F32) + up[:, low:wide].astype(F32) + down[:, low:wide].astype(F32)
    )
    give[...] = (
        mine[:, wide:].astype(F32) + up[:, wide:].astype(F32) + down[:, wide:].astype(F32)
    ).astype(BF)


def local(kernel, shapes, *args):
    return pl.pallas_call(
        kernel,
        out_shape=in_vmem(*shapes),
        in_specs=[VMEM] * len(args),
        out_specs=(VMEM,) * len(shapes) if len(shapes) > 1 else VMEM,
        compiler_params=PARAMS,
    )(*args)


def gated_kernel(keep, x, out):
    hidden_width = out.shape[1]
    wide = keep.shape[1]
    low = wide - x.shape[1]
    late = keep[:, low:] + x[...].astype(F32)
    squares = late[:, 2 * hidden_width - low :]
    scale = lax.rsqrt(jnp.sum(squares, axis=1, keepdims=True) * F32(1 / 16384) + 1e-05)
    gate = keep[:, :hidden_width] * scale
    lift = jnp.concatenate([keep[:, hidden_width:low], late[:, : 2 * hidden_width - low]], axis=1) * scale
    out[...] = (gate / (1 + jnp.exp(-gate)) * lift).astype(BF)


def down_kernel(own, near1, near2, near3, far, x0, x1, x2, x3, x4, down_ref, their_down, give, keep, rows):
    n = ROWS_DEV
    width = down_ref.shape[0]
    batch_index, mp_index = lax.axis_index("batch"), lax.axis_index("mp")
    core = mp_index & 1
    flip = (batch_index & 1) ^ core
    for j, found in enumerate(((near1, near2, near3, far, own), (x1, x2, x3, x4, x0))):
        first = ((flip + j) & 1) * 4 * n
        for i in range(3):
            rows[pl.ds(pl.multiple_of(first + i * n, n), n), :] = found[i][...]
        last = pl.ds(pl.multiple_of(first + 3 * n, n), n)

        @pl.when(core == 0)
        def _():
            rows[last, :] = found[3][...]

        @pl.when(core == 1)
        def _():
            rows[last, :] = found[4][...]

    step = 2 * LANE
    for i in range(0, down_ref.shape[1], step):
        lanes = slice(i, i + step)
        product = jnp.dot(rows[:, :width], down_ref[:, lanes], preferred_element_type=F32)
        product = product + jnp.dot(rows[:, width:], their_down[:, lanes], preferred_element_type=F32)
        product = product.astype(BF)
        for k in range(4):
            keep[k, :, lanes] = product[k * n : (k + 1) * n]
            give[k, :, lanes] = product[(4 + k) * n : (5 + k) * n]


def place_kernel(keep, come, out):
    z, core = lax.axis_index("batch") >> 1, lax.axis_index("mp") & 1
    for parts, side in ((keep, core), (come, 1 - core)):
        sign = 2 * side - 1
        for k in range(4):
            distance = sign * (k + 1) if k < 3 else (1 - side) * FAR
            out[(z + distance) & (ZN - 1)] = parts[k]


def finish_kernel(own, parts, out):
    total = own[...].astype(F32)
    for i in range(parts.shape[0]):
        total = total + parts[i].astype(F32)
    out[...] = total.astype(BF)


def after(*values):
    return lax.optimization_barrier(values)


def body(
    hidden_in,
    queries,
    key_cache,
    value_cache,
    question,
    prefix_len,
    norm_gain,
    gate_weight,
    up_weight,
    down_weight,
):
    rows, width = queries.shape
    hidden_width = gate_weight.shape[1]

    sent = prepare(prefix_len, question, queries, hidden_in, key_cache, value_cache)
    sent, down_weight = after(sent, down_weight)
    their_down = core_pair(down_weight)
    came, their_down = after(transpose_mesh(sent), their_down)
    mine = over_plane(jnp.broadcast_to(came[None], (ZN, *came.shape)))
    theirs = core_pair(mine)
    own, give, kept, far_low, far_high = project(
        prefix_len, norm_gain, mine, theirs, gate_weight, up_weight
    )
    low, whole = far_low.shape, kept[0].shape

    far, ahead = after(give[4], give[3])
    far, x = x_pair(far), x_pair(ahead)
    up, down, ahead = after(local(add_first_kernel, [(low, BF)], far_low, far), far_high, give[2])
    up, down, following = along_z(up, 1), along_z(down, -1), x_pair(ahead)
    up, down, x = after(up, down, x)
    up, down = local(add_far_kernel, [(whole, BF)] * 2, kept[3], kept[5], x, up, down)
    for step in (2, 1):
        up, down, ahead = after(up, down, give[step - 1])
        x = following
        up, down, following = along_z(up, 1), along_z(down, -1), x_pair(ahead)
        up, down, x = after(up, down, x)
        up, down = local(
            add_ring_kernel, [(whole, BF)] * 2, kept[step], kept[ZN - step], x, up, down
        )
    up, down = after(up, down)
    up, down, x = after(along_z(up, 1), along_z(down, -1), following)
    late = whole[1] - 2 * hidden_width - LANE
    keep, last = local(
        add_last_kernel,
        [((rows, 2 * hidden_width + LANE), F32), ((rows, late), BF)],
        kept[0],
        x,
        up,
        down,
    )
    hidden = local(gated_kernel, [((rows, hidden_width), BF)], keep, x_pair(last))

    near = jnp.concatenate([hidden, core_pair(hidden)], axis=1)
    blocks, partners = [near], []
    for step in range(4):
        across = blocks[-1]
        near, across = after(across, across)
        near = by_core(near, lambda i, core: (i + 2 - 4 * core) % 16, (0,) if step == 3 else (0, 1))
        came = by_core(across, lambda i, core: i ^ 1, (1,) if step == 0 else (0, 1))
        if partners:
            near, partners[-1] = after(near, partners[-1])
        partners.append(came)
        blocks.append(near)
    partners.append(by_core(near, lambda i, core: i ^ 1, (0,)))
    shape = (4, rows, width)
    keep, send = pl.pallas_call(
        lambda *refs: down_kernel(*refs[:12], refs[13], refs[12], refs[14]),
        out_shape=in_vmem((shape, BF), (shape, BF)),
        in_specs=[VMEM] * 12,
        out_specs=(VMEM, VMEM),
        scratch_shapes=[pltpu.VMEM((8 * rows, 2 * hidden_width), BF)],
        compiler_params=PARAMS,
    )(*blocks, *partners, down_weight, their_down)
    held = local(place_kernel, [((ZN, rows, width), BF)], keep, core_pair(send))
    parts = over_plane(held)
    return pl.pallas_call(
        finish_kernel,
        out_shape=jax.ShapeDtypeStruct((rows, width), BF),
        in_specs=[VMEM, VMEM],
        out_specs=VMEM,
        compiler_params=PARAMS,
    )(own, parts)


def solution(mesh):
    return jax.shard_map(
        body,
        mesh=mesh,
        in_specs=(
            P("batch", None),
            P("batch", "mp"),
            P("batch", None),
            P("batch", None),
            P("batch"),
            P(),
            P(),
            P("batch", "mp"),
            P("batch", "mp"),
            P("mp", "batch"),
        ),
        out_specs=P("mp", "batch"),
        check_vma=False,
    )
```

```python
import jax
import jax.numpy as jnp
from jax import lax
from jax.experimental import pallas as pl
from jax.experimental.pallas import tpu as pltpu
from jax.sharding import PartitionSpec as P

HEADS = 128
KV_HEADS = 8
HEAD_DIM = 128
PREFIX = 24
ROWS_DEV = 32
ZN = 8
LANE = 128
BF = jnp.bfloat16
F32 = jnp.float32
PLANE = [[2 * i + core for i in range(8)] for core in range(2)]
VMEM = pl.BlockSpec(memory_space=pltpu.VMEM)
SMEM = pl.BlockSpec(memory_space=pltpu.SMEM)
ANY = pl.BlockSpec(memory_space=pl.ANY)
HBM = pl.BlockSpec(memory_space=pltpu.HBM)
PARAMS = pltpu.CompilerParams(vmem_limit_bytes=28 * 2**20)


def permute(value, axis, target, count=16):
    return lax.ppermute(value, axis, [(i, target(i)) for i in range(count)])


def along_z(value, step):
    return permute(value, "batch", lambda i: (i + 2 * step) % 16)


def x_pair(value):
    return permute(value, "batch", lambda i: i ^ 1)


def core_pair(value):
    return permute(value, "mp", lambda i: i ^ 1)


def transpose_mesh(value):
    return lax.ppermute(
        value,
        ("batch", "mp"),
        [(b * 16 + m, m * 16 + b) for b in range(16) for m in range(16)],
    )


def over_plane(value):
    return lax.all_to_all(value, "mp", 0, 0, axis_index_groups=PLANE, tiled=True)


def in_vmem(*shapes):
    made = tuple(pltpu.VMEM(shape, dtype) for shape, dtype in shapes)
    return made if len(made) > 1 else made[0]


def in_hbm(value):
    return pltpu.with_memory_space_constraint(value, pltpu.HBM)


def softmax(scores, seen):
    scores = jnp.where(seen, scores * F32(HEAD_DIM**-0.5), F32(-1e30))
    exponent = jnp.exp(scores - jnp.max(scores, axis=1, keepdims=True))
    return (exponent / jnp.sum(exponent, axis=1, keepdims=True)).astype(BF)


def scored(queries, keys):
    return lax.dot_general(queries, keys, (((1,), (1,)), ((), ())), preferred_element_type=F32)


def prepare_kernel(lengths, questions, queries_ref, hidden_ref, key_ref, value_ref, out_ref, queries, hidden, pair, length_ref, question_ref, sems):
    width = queries.shape[1]
    heads = width // HEAD_DIM
    batch_index, mp_index = lax.axis_index("batch"), lax.axis_index("mp")
    head = pl.ds(pl.multiple_of((mp_index >> 1) * HEAD_DIM, HEAD_DIM), HEAD_DIM)
    at = pl.ds(pl.multiple_of(mp_index * width, width), width)
    copies = [
        pltpu.make_async_copy(source, target, sems.at[i])
        for i, (source, target) in enumerate(
            [
                (key_ref.at[:, head], pair.at[:, :HEAD_DIM]),
                (queries_ref, queries),
                (value_ref.at[:, head], pair.at[:, HEAD_DIM:]),
                (hidden_ref.at[:, at], hidden),
                (lengths, length_ref),
                (questions, question_ref),
            ]
        )
    ]
    for copy in copies:
        copy.start()
    copies[4].wait()
    copies[5].wait()
    shape = (ROWS_DEV, ROWS_DEV)
    row = lax.broadcasted_iota(jnp.int32, shape, 0)
    key = lax.broadcasted_iota(jnp.int32, shape, 1)
    seen = (key <= row) & (key < length_ref[batch_index])
    seen = jnp.concatenate([seen.astype(F32)] * heads, axis=0) > 0
    shape = (16, LANE)
    option = lax.broadcasted_iota(jnp.int32, shape, 0) & (ROWS_DEV - PREFIX - 1)
    asked = jnp.zeros(shape, jnp.int32)
    for i in range(ROWS_DEV - PREFIX):
        asked = jnp.where(option == i, question_ref[i], asked)
    out_ref[32:, width:] = asked.astype(F32).astype(BF)
    out_ref[:32, width:] = jnp.zeros((ROWS_DEV, LANE), BF)
    copies[0].wait()
    copies[1].wait()
    stacked = jnp.concatenate(
        [queries[:, h * HEAD_DIM : (h + 1) * HEAD_DIM] for h in range(heads)], axis=0
    )
    attention = softmax(scored(stacked, pair[:, :HEAD_DIM]), seen)
    copies[2].wait()
    context = jnp.dot(attention, pair[:, HEAD_DIM:], preferred_element_type=F32).astype(BF)
    out_ref[32:, : 2 * HEAD_DIM] = pair[:16]
    out_ref[32:, 2 * HEAD_DIM : 4 * HEAD_DIM] = pair[16:]
    last = queries[16:].astype(F32)[PREFIX - 16 :]
    half = width // 2
    out_ref[32:, half:width] = jnp.concatenate([last[:, :half], last[:, half:]], axis=0).astype(BF)
    copies[3].wait()
    prefix = lax.broadcasted_iota(jnp.int32, (ROWS_DEV, HEAD_DIM), 0) < PREFIX
    for h in range(heads):
        columns = slice(h * HEAD_DIM, (h + 1) * HEAD_DIM)
        mine = context[h * ROWS_DEV : (h + 1) * ROWS_DEV].astype(F32)
        mine = jnp.where(prefix, mine, F32(0))
        out_ref[:32, columns] = (hidden[:, columns].astype(F32) + mine).astype(BF)


def prepare(prefix_len, question, queries, hidden_in, key_cache, value_cache):
    rows, width = queries.shape
    return pl.pallas_call(
        prepare_kernel,
        out_shape=in_vmem(((rows + 16, width + LANE), BF)),
        in_specs=[HBM] * 6,
        out_specs=VMEM,
        scratch_shapes=[
            pltpu.VMEM((rows, width), BF),
            pltpu.VMEM((rows, width), BF),
            pltpu.VMEM((rows, 2 * HEAD_DIM), BF),
            pltpu.SMEM(prefix_len.shape, jnp.int32),
            pltpu.SMEM(question.shape, jnp.int32),
            pltpu.SemaphoreType.DMA((6,)),
        ],
        compiler_params=PARAMS,
    )(*map(in_hbm, (prefix_len, question, queries, hidden_in, key_cache, value_cache)))


FAR = 4


ORDER = [(s, 1) for s in (FAR, 3, 5, 2, 6, 1, 7, 0)] + [(s, 0) for s in range(ZN)]
FIRST = 3


def products(rows, squares, gate_ref, up_ref, ready):
    tiles = gate_ref.shape[1] // LANE
    for base, ref in ((0, gate_ref), (tiles, up_ref)):
        ready(ref)
        for t in range(0, tiles, 2):
            lanes = slice(t * LANE, min(t + 2, tiles) * LANE)
            product = jnp.dot(rows[...], ref[:, lanes], preferred_element_type=F32).astype(BF)
            yield slice((base + t) * LANE, (base + t) * LANE + product.shape[1]), product
    yield slice(2 * tiles * LANE, (2 * tiles + 1) * LANE), squares[...]


def first_kernel(length_ref, gain_ref, mine_ref, theirs_ref, gate_hbm, up_hbm, *refs):
    own_ref, rows, squares, gate_ref, up_ref, far_ref, next_ref, residual, gain, sems = refs
    n = ROWS_DEV
    width = own_ref.shape[1]
    half = width // 2
    batch_index, mp_index = lax.axis_index("batch"), lax.axis_index("mp")
    z, core = batch_index >> 1, mp_index & 1
    flip = (batch_index & 1) ^ core
    fetch = pltpu.make_async_copy(gain_ref.at[pl.ds(batch_index * width, width)], gain, sems.at[0])
    fetch_gate = pltpu.make_async_copy(gate_hbm, gate_ref, sems.at[1])
    fetch_up = pltpu.make_async_copy(up_hbm, up_ref, sems.at[2])
    fetch.start()
    fetch_gate.start()
    fetch_up.start()

    blocks = [(ref, i) for ref in (mine_ref, theirs_ref) for i in range(ZN)]
    options = ROWS_DEV - PREFIX

    def gathered(lanes):
        return jnp.concatenate([ref[i, n:, lanes] for ref, i in blocks], axis=0)

    def unfolded(first):
        low, high = slice(first, first + HEAD_DIM), slice(first + 2 * HEAD_DIM, first + 3 * HEAD_DIM)
        return jnp.concatenate(
            [ref[i, n:, lanes] for ref, i in blocks for lanes in (low, high)], axis=0
        )

    keys, values = unfolded(0), unfolded(HEAD_DIM)
    shape = (16 * len(blocks), n * len(blocks))
    asked = gathered(slice(width, width + LANE)).astype(F32).astype(jnp.int32)
    asked = jnp.concatenate([asked] * (shape[1] // LANE), axis=1)
    place = lax.broadcasted_iota(jnp.int32, shape, 1)
    order = place >> 5
    row = lax.broadcasted_iota(jnp.int32, shape, 0)
    owner = ((order & (ZN - 1)) << 1) + ((order >> 3) ^ core)
    live = jnp.zeros(shape, jnp.int32)
    for i in range(len(blocks)):
        live = jnp.where(order == i, length_ref[((i & (ZN - 1)) << 1) + ((i >> 3) ^ core)], live)
    seen = (owner == asked) & ((place & (n - 1)) < live)
    seen = seen | (place == (row >> 4) * n + PREFIX + (row & (options - 1)))
    contexts = []
    for h in range(half // HEAD_DIM):
        queries = gathered(slice(half + h * HEAD_DIM, half + (h + 1) * HEAD_DIM))
        attention = softmax(scored(queries, keys), seen)
        context = jnp.dot(attention, values, preferred_element_type=F32)
        contexts.append(context.astype(BF).astype(F32))
    fetch.wait()
    scale = gain[...].reshape(1, width)
    for k, (ref, i) in enumerate(blocks):
        at = k * 16
        added = jnp.concatenate(
            [context[at : at + options] for context in contexts]
            + [context[at + options : at + 16] for context in contexts],
            axis=1,
        )
        added = jnp.concatenate([jnp.zeros((16 - options, width), F32), added], axis=0)
        first = ref[i, :16, :width]
        last = (ref[i, 16:n, :width].astype(F32) + added).astype(BF)
        if ref is mine_ref:
            residual[i, :16] = first
            residual[i, 16:] = last
        s = (i - z) & (ZN - 1)
        j = flip if ref is mine_ref else 1 - flip
        position = ZN + s
        for index, (target, _) in enumerate(ORDER[:ZN]):
            position = jnp.where((s == target) & (j == 1), index, position)
        at = pl.multiple_of(position * n, n)
        for part, offset in ((first, 0), (last, 16)):
            x = part.astype(F32)
            into = pl.ds(pl.multiple_of(at + offset, 16), 16)
            rows[into, :] = (x * scale).astype(BF)
            square = x * x
            total = square[:, :LANE]
            for lane in range(1, width // LANE):
                total = total + square[:, lane * LANE : (lane + 1) * LANE]
            squares[into, :] = total.astype(BF)
    own_ref[...] = residual[mp_index >> 1]
    early = slice(0, FIRST * n)
    ready = lambda ref: (fetch_gate if ref is gate_ref else fetch_up).wait()
    for lanes, value in products(rows.at[early], squares.at[early], gate_ref, up_ref, ready):
        far_ref[:, lanes] = value[:n]
        next_ref[0, :, lanes] = value[n : 2 * n]
        next_ref[1, :, lanes] = value[2 * n :]


def rest_kernel(rows, squares, gate_ref, up_ref, give2, give1, give0, *kept):
    n = ROWS_DEV
    into = [give2.at[0], give2.at[1], give1.at[0], give1.at[1], give0, *kept]
    late = slice(FIRST * n, len(ORDER) * n)
    for lanes, value in products(rows.at[late], squares.at[late], gate_ref, up_ref, lambda ref: None):
        for i, ref in enumerate(into):
            ref[:, lanes] = value[i * n : (i + 1) * n]


def project(prefix_len, norm_gain, mine, theirs, gate_weight, up_weight):
    width, hidden_width = gate_weight.shape
    n = ROWS_DEV
    part = (n, 2 * hidden_width + LANE)
    all_rows = len(ORDER) * n
    own, rows, squares, gate, up, far, following = pl.pallas_call(
        first_kernel,
        out_shape=in_vmem(
            ((n, width), BF),
            ((all_rows, width), BF),
            ((all_rows, LANE), BF),
            (gate_weight.shape, BF),
            (up_weight.shape, BF),
            (part, BF),
            ((2, *part), BF),
        ),
        in_specs=[SMEM, HBM, VMEM, VMEM, HBM, HBM],
        out_specs=(VMEM,) * 7,
        scratch_shapes=[
            pltpu.VMEM((ZN, n, width), BF),
            pltpu.VMEM((width,), F32),
            pltpu.SemaphoreType.DMA((3,)),
        ],
        compiler_params=PARAMS,
    )(prefix_len, in_hbm(norm_gain), mine, theirs, in_hbm(gate_weight), in_hbm(up_weight))
    give2, give1, give0, *kept = local(
        rest_kernel,
        [((2, *part), BF)] * 2 + [(part, BF)] * 9,
        rows,
        squares,
        gate,
        up,
        cost=cost((len(ORDER) - FIRST) * n, width, part[1]),
    )
    return own, [give0, give1, give2, following, far], kept


def summed(*refs):
    total = refs[0].astype(F32)
    for ref in refs[1:]:
        total = total + ref.astype(F32)
    return total.astype(BF)


def add_first_kernel(mine, x, out_up, out_down):
    low = out_up.shape[1]
    out_up[...] = summed(mine[:, :low], x[:, :low])
    out_down[...] = summed(mine[:, low:], x[:, low:])


def add_far_kernel(mine_up, mine_down, x, up, down, out_up, out_down):
    low = up.shape[1]
    out_up[:, :low] = summed(mine_up[:, :low], x[0, :, :low], up[...])
    out_up[:, low:] = summed(mine_up[:, low:], x[0, :, low:])
    out_down[:, :low] = summed(mine_down[:, :low], x[1, :, :low])
    out_down[:, low:] = summed(mine_down[:, low:], x[1, :, low:], down[...])


def add_ring_kernel(mine_up, mine_down, x, up, down, out_up, out_down):
    out_up[...] = summed(mine_up[...], x[0], up[...])
    out_down[...] = summed(mine_down[...], x[1], down[...])


def gated_kernel(mine, x, up, down, out):
    width = out.shape[1]

    def total(lanes):
        parts = [ref[:, lanes].astype(F32) for ref in (mine, x, up, down)]
        return (parts[0] + parts[1]) + (parts[2] + parts[3])

    squares = total(slice(2 * width, 2 * width + LANE))
    scale = lax.rsqrt(jnp.sum(squares, axis=1, keepdims=True) * F32(1 / 16384) + 1e-05)
    gate = total(slice(0, width)) * scale
    lift = total(slice(width, 2 * width)) * scale
    out[...] = (gate / (1 + jnp.exp(-gate)) * lift).astype(BF)


def cost(rows, depth, columns):
    return pl.CostEstimate(
        flops=2 * rows * depth * columns, bytes_accessed=2 * depth * columns, transcendentals=0
    )


def local(kernel, shapes, *args, cost=None):
    return pl.pallas_call(
        kernel,
        out_shape=in_vmem(*shapes),
        in_specs=[VMEM] * len(args),
        out_specs=(VMEM,) * len(shapes) if len(shapes) > 1 else VMEM,
        compiler_params=PARAMS,
        cost_estimate=cost,
    )(*args)


def down_kernel(*refs):
    own, up1, down1, up2, down2, up3, down3, up4, down4, x0, x1, x2, x3, x4, down_ref = refs[:15]
    give, keep, rows = refs[15:]
    n = ROWS_DEV
    batch_index, mp_index = lax.axis_index("batch"), lax.axis_index("mp")
    z, flip = batch_index >> 1, (batch_index ^ mp_index) & 1
    ours = {0: own, 1: down1, 2: down2, 3: down3, 5: up3, 6: up2, 7: up1}
    partners = {0: x0, 7: x1.at[0], 1: x1.at[1], 6: x2.at[0], 2: x2.at[1], 5: x3.at[0], 3: x3.at[1], FAR: x4}
    for s in range(ZN):
        for j, found in enumerate((ours, partners)):
            target = (z + s) & (ZN - 1)
            other = (flip + j) & 1
            at = pl.ds(pl.multiple_of((1 - other) * ZN * n + target * n, n), n)
            if s in found:
                rows[at, :] = found[s][...]
            else:
                rows[at, : up4.shape[1]] = up4[...]
                rows[at, up4.shape[1] :] = down4[...]
    step = 2 * LANE
    for i in range(0, down_ref.shape[1], step):
        lanes = slice(i, i + step)
        product = jnp.dot(rows[...], down_ref[:, lanes], preferred_element_type=F32)
        for target in range(ZN):
            give[target, :, lanes] = product[target * n : (target + 1) * n].astype(BF)
            at = (ZN + target) * n
            keep[target, :, lanes] = product[at : at + n]


def project_down(blocks, down_weight):
    hidden_width, width = down_weight.shape
    shape = (ZN, ROWS_DEV, width)
    return pl.pallas_call(
        down_kernel,
        out_shape=in_vmem((shape, BF), (shape, F32)),
        in_specs=[VMEM] * (len(blocks) + 1),
        out_specs=(VMEM, VMEM),
        scratch_shapes=[pltpu.VMEM((2 * ZN * ROWS_DEV, hidden_width), BF)],
        compiler_params=PARAMS,
    )(*blocks, down_weight)


def add_core_kernel(keep, come, out):
    out[...] = (keep[...] + come[...].astype(F32)).astype(BF)


def finish_kernel(own, parts, out):
    total = own[...].astype(F32)
    for i in range(parts.shape[0]):
        total = total + parts[i].astype(F32)
    out[...] = total.astype(BF)


def after(*values):
    return lax.optimization_barrier(values)


def body(
    hidden_in,
    queries,
    key_cache,
    value_cache,
    question,
    prefix_len,
    norm_gain,
    gate_weight,
    up_weight,
    down_weight,
):
    rows, width = queries.shape
    hidden_width = gate_weight.shape[1]

    sent = prepare(prefix_len, question, queries, hidden_in, key_cache, value_cache)
    came = transpose_mesh(sent)
    mine = over_plane(jnp.broadcast_to(came[None], (ZN, *came.shape)))
    theirs = core_pair(mine)
    own, give, kept = project(prefix_len, norm_gain, mine, theirs, gate_weight, up_weight)
    part = kept[0].shape
    half = (part[1] // LANE) // 2 * LANE
    ends = [((rows, half), BF), ((rows, part[1] - half), BF)]

    far, ahead = after(give[4], give[3])
    far, following = x_pair(far), x_pair(ahead)
    up, down = local(add_first_kernel, ends, kept[4], far)
    for step in (4, 3, 2, 1):
        up, down, ahead = after(up, down, give[step - 2] if step > 1 else give[0])
        x = following
        if step > 1:
            following = x_pair(ahead)
        up, down = along_z(up, 1), along_z(down, -1)
        up, down, x = after(up, down, x)
        if step > 1:
            up, down = local(
                add_far_kernel if step == 4 else add_ring_kernel,
                [(part, BF)] * 2,
                kept[step - 1],
                kept[ZN + 1 - step],
                x,
                up,
                down,
            )
    hidden = local(gated_kernel, [((rows, hidden_width), BF)], kept[0], x, up, down)

    up, down, across = hidden, hidden, hidden
    blocks, partners = [hidden], []
    for step in range(3):
        up, down, across = after(up, down, across)
        up, down, came = along_z(up, 1), along_z(down, -1), x_pair(across)
        if partners:
            up, down, partners[-1] = after(up, down, partners[-1])
        else:
            up, down = after(up, down)
        partners.append(came)
        blocks += [up, down]
        across = jnp.stack([up, down])
    half = (hidden_width // LANE + 1) // 2 * LANE
    up, down, across = after(up[:, :half], down[:, half:], across)
    up, down, came = along_z(up, 1), along_z(down, -1), x_pair(across)
    up, down, partners[-1] = after(up, down, partners[-1])
    partners += [came, x_pair(jnp.concatenate([up, down], axis=1))]
    blocks += [up, down, *partners]
    send, keep = project_down(blocks, down_weight)
    held = local(add_core_kernel, [(keep.shape, BF)], keep, core_pair(send))
    parts = over_plane(held)
    return pl.pallas_call(
        finish_kernel,
        out_shape=jax.ShapeDtypeStruct((rows, width), BF),
        in_specs=[VMEM, VMEM],
        out_specs=VMEM,
        compiler_params=PARAMS,
    )(own, parts)


def solution(mesh):
    return jax.shard_map(
        body,
        mesh=mesh,
        in_specs=(
            P("batch", None),
            P("batch", "mp"),
            P("batch", None),
            P("batch", None),
            P("batch"),
            P(),
            P(),
            P("batch", "mp"),
            P("batch", "mp"),
            P("mp", "batch"),
        ),
        out_specs=P("mp", "batch"),
        check_vma=False,
    )
```

```python
import jax
import jax.numpy as jnp
from jax import lax
from jax.experimental import pallas as pl
from jax.experimental.pallas import tpu as pltpu
from jax.sharding import PartitionSpec as P

HEADS = 128
KV_HEADS = 8
HEAD_DIM = 128
PREFIX = 24
ROWS_DEV = 32
ZN = 8
LANE = 128
BF = jnp.bfloat16
F32 = jnp.float32
PLANE = [[2 * i + core for i in range(8)] for core in range(2)]
VMEM = pl.BlockSpec(memory_space=pltpu.VMEM)
SMEM = pl.BlockSpec(memory_space=pltpu.SMEM)
ANY = pl.BlockSpec(memory_space=pl.ANY)
HBM = pl.BlockSpec(memory_space=pltpu.HBM)
PARAMS = pltpu.CompilerParams(vmem_limit_bytes=28 * 2**20)


def permute(value, axis, target, count=16):
    return lax.ppermute(value, axis, [(i, target(i)) for i in range(count)])


def along_z(value, step):
    return permute(value, "batch", lambda i: (i + 2 * step) % 16)


def x_pair(value):
    return permute(value, "batch", lambda i: i ^ 1)


def core_pair(value):
    return permute(value, "mp", lambda i: i ^ 1)


def transpose_mesh(value):
    return lax.ppermute(
        value,
        ("batch", "mp"),
        [(b * 16 + m, m * 16 + b) for b in range(16) for m in range(16)],
    )


def over_plane(value):
    return lax.all_to_all(value, "mp", 0, 0, axis_index_groups=PLANE, tiled=True)


def in_vmem(*shapes):
    made = tuple(pltpu.VMEM(shape, dtype) for shape, dtype in shapes)
    return made if len(made) > 1 else made[0]


def in_hbm(value):
    return pltpu.with_memory_space_constraint(value, pltpu.HBM)


PAIRS = 8 * ROWS_DEV
QUERIES = PAIRS + 4 * 16
ASKED = QUERIES + 4 * 16


def softmax(scores, seen):
    scores = jnp.where(seen, scores * F32(HEAD_DIM**-0.5), F32(-1e30))
    exponent = jnp.exp(scores - jnp.max(scores, axis=1, keepdims=True))
    return (exponent * (F32(1) / jnp.sum(exponent, axis=1, keepdims=True))).astype(BF)


def scored(queries, keys):
    return lax.dot_general(queries, keys, (((1,), (1,)), ((), ())), preferred_element_type=F32)


def prepare_kernel(lengths, questions, queries_ref, hidden_ref, key_ref, value_ref, out_ref, queries, hidden, pair, length_ref, question_ref, sems):
    width = queries.shape[1]
    heads = width // HEAD_DIM
    batch_index, mp_index = lax.axis_index("batch"), lax.axis_index("mp")
    head = pl.ds(pl.multiple_of((mp_index >> 1) * HEAD_DIM, HEAD_DIM), HEAD_DIM)
    at = pl.ds(pl.multiple_of(mp_index * width, width), width)
    copies = [
        pltpu.make_async_copy(source, target, sems.at[i])
        for i, (source, target) in enumerate(
            [
                (key_ref.at[:, head], pair.at[:, :HEAD_DIM]),
                (queries_ref, queries),
                (value_ref.at[:, head], pair.at[:, HEAD_DIM:]),
                (hidden_ref.at[:, at], hidden),
                (lengths, length_ref),
                (questions, question_ref),
            ]
        )
    ]
    for copy in copies:
        copy.start()
    copies[4].wait()
    copies[5].wait()
    shape = (ROWS_DEV, ROWS_DEV)
    row = lax.broadcasted_iota(jnp.int32, shape, 0)
    key = lax.broadcasted_iota(jnp.int32, shape, 1)
    seen = (key <= row) & (key < length_ref[batch_index])
    seen = jnp.concatenate([seen.astype(F32)] * heads, axis=0) > 0
    shape = (16, LANE)
    option = lax.broadcasted_iota(jnp.int32, shape, 0) & (ROWS_DEV - PREFIX - 1)
    asked = jnp.zeros(shape, jnp.int32)
    for i in range(ROWS_DEV - PREFIX):
        asked = jnp.where(option == i, question_ref[i], asked)
    out_ref[ASKED : ASKED + 16, :] = asked.astype(F32).astype(BF)
    copies[0].wait()
    copies[1].wait()
    stacked = jnp.concatenate(
        [queries[:, h * HEAD_DIM : (h + 1) * HEAD_DIM] for h in range(heads)], axis=0
    )
    attention = softmax(scored(stacked, pair[:, :HEAD_DIM]), seen)
    copies[2].wait()
    context = jnp.dot(attention, pair[:, HEAD_DIM:], preferred_element_type=F32).astype(BF)
    for i in range(2):
        for j in range(2):
            at = PAIRS + (2 * i + j) * 16
            out_ref[at : at + 16, :] = pair[16 * i : 16 * i + 16, j * HEAD_DIM : (j + 1) * HEAD_DIM]
    last = queries[16:].astype(F32)[PREFIX - 16 :]
    half = width // 2
    for h in range(heads // 2):
        first = h * HEAD_DIM
        tile = [last[:, at : at + HEAD_DIM] for at in (first, first + half)]
        at = QUERIES + h * 16
        out_ref[at : at + 16, :] = jnp.concatenate(tile, axis=0).astype(BF)
    copies[3].wait()
    prefix = lax.broadcasted_iota(jnp.int32, (ROWS_DEV, HEAD_DIM), 0) < PREFIX
    for h in range(heads):
        columns = slice(h * HEAD_DIM, (h + 1) * HEAD_DIM)
        mine = context[h * ROWS_DEV : (h + 1) * ROWS_DEV].astype(F32)
        mine = jnp.where(prefix, mine, F32(0))
        at = slice(h * ROWS_DEV, (h + 1) * ROWS_DEV)
        out_ref[at, :] = (hidden[:, columns].astype(F32) + mine).astype(BF)


def prepare(prefix_len, question, queries, hidden_in, key_cache, value_cache):
    rows, width = queries.shape
    return pl.pallas_call(
        prepare_kernel,
        out_shape=in_vmem(((ASKED + 16, LANE), BF)),
        in_specs=[HBM] * 6,
        out_specs=VMEM,
        scratch_shapes=[
            pltpu.VMEM((rows, width), BF),
            pltpu.VMEM((rows, width), BF),
            pltpu.VMEM((rows, 2 * HEAD_DIM), BF),
            pltpu.SMEM(prefix_len.shape, jnp.int32),
            pltpu.SMEM(question.shape, jnp.int32),
            pltpu.SemaphoreType.DMA((6,)),
        ],
        compiler_params=PARAMS,
    )(*map(in_hbm, (prefix_len, question, queries, hidden_in, key_cache, value_cache)))


FAR = 4


ORDER = [(s, 1) for s in (FAR, 3, 5, 2, 6, 1, 7, 0)] + [(s, 0) for s in range(ZN)]
FIRST = 3


def products(rows, squares, gate_ref, up_ref, ready):
    tiles = gate_ref.shape[1] // LANE
    for base, ref in ((0, gate_ref), (tiles, up_ref)):
        ready(ref)
        for t in range(0, tiles, 2):
            lanes = slice(t * LANE, min(t + 2, tiles) * LANE)
            product = jnp.dot(rows[...], ref[:, lanes], preferred_element_type=F32).astype(BF)
            yield slice((base + t) * LANE, (base + t) * LANE + product.shape[1]), product
    yield slice(2 * tiles * LANE, (2 * tiles + 1) * LANE), squares[...]


def first_kernel(length_ref, gain_ref, mine_ref, theirs_ref, gate_hbm, up_hbm, *refs):
    own_ref, rows, squares, gate_ref, up_ref, far_ref, next_ref, residual, gain, sems = refs
    n = ROWS_DEV
    width = own_ref.shape[1]
    half = width // 2
    batch_index, mp_index = lax.axis_index("batch"), lax.axis_index("mp")
    z, core = batch_index >> 1, mp_index & 1
    flip = (batch_index & 1) ^ core
    fetch = pltpu.make_async_copy(gain_ref.at[pl.ds(batch_index * width, width)], gain, sems.at[0])
    fetch_gate = pltpu.make_async_copy(gate_hbm, gate_ref, sems.at[1])
    fetch_up = pltpu.make_async_copy(up_hbm, up_ref, sems.at[2])
    fetch.start()
    fetch_gate.start()
    fetch_up.start()

    blocks = [(ref, i) for ref in (mine_ref, theirs_ref) for i in range(ZN)]
    options = ROWS_DEV - PREFIX

    def gathered(*parts):
        return jnp.concatenate([ref[i, at : at + 16, :] for ref, i in blocks for at in parts], axis=0)

    keys, values = gathered(PAIRS, PAIRS + 32), gathered(PAIRS + 16, PAIRS + 48)
    total = n * len(blocks)
    place = lax.broadcasted_iota(jnp.int32, (8, total), 1)
    order = place >> 5
    live = jnp.zeros(place.shape, jnp.int32)
    for i in range(len(blocks)):
        live = jnp.where(order == i, length_ref[((i & (ZN - 1)) << 1) + ((i >> 3) ^ core)], live)
    owner = ((order & (ZN - 1)) << 1) + ((order >> 3) ^ core)
    owner = jnp.where((place & (n - 1)) < live, owner, -1)
    asked = gathered(ASKED).astype(F32).astype(jnp.int32)
    row = lax.broadcasted_iota(jnp.int32, (asked.shape[0], 1), 0)
    itself = (row >> 4) * n + PREFIX + (row & (options - 1))
    seen = (jnp.tile(owner, (asked.shape[0] // 8, 1)) == jnp.tile(asked, (1, total // LANE))) | (
        jnp.tile(place, (asked.shape[0] // 8, 1)) == itself
    )
    contexts = []
    for h in range(half // HEAD_DIM):
        attention = softmax(scored(gathered(QUERIES + h * 16), keys), seen)
        context = jnp.dot(attention, values, preferred_element_type=F32)
        contexts.append(context.astype(BF).astype(F32))
    fetch.wait()
    scale = gain[...].reshape(1, width)
    for k, (ref, i) in enumerate(blocks):
        s = (i - z) & (ZN - 1)
        j = flip if ref is mine_ref else 1 - flip
        position = ZN + s
        for index, (target, _) in enumerate(ORDER[:ZN]):
            position = jnp.where((s == target) & (j == 1), index, position)
        into = pl.ds(pl.multiple_of(position * n, n), n)
        total = jnp.zeros((n, LANE), F32)
        for tile in range(width // LANE):
            lanes = slice(tile * LANE, (tile + 1) * LANE)
            at = k * 16 + tile // len(contexts) * options
            added = contexts[tile % len(contexts)][at : at + options]
            added = jnp.concatenate([jnp.zeros((PREFIX, LANE), F32), added], axis=0)
            part = (ref[i, tile * n : (tile + 1) * n, :].astype(F32) + added).astype(BF)
            if ref is mine_ref:
                residual[i, :, lanes] = part
            x = part.astype(F32)
            rows[into, lanes] = (x * scale[:, lanes]).astype(BF)
            total = total + x * x
        squares[into, :] = total.astype(BF)
    own_ref[...] = residual[mp_index >> 1]
    early = slice(0, FIRST * n)
    ready = lambda ref: (fetch_gate if ref is gate_ref else fetch_up).wait()
    for lanes, value in products(rows.at[early], squares.at[early], gate_ref, up_ref, ready):
        far_ref[:, lanes] = value[:n]
        next_ref[0, :, lanes] = value[n : 2 * n]
        next_ref[1, :, lanes] = value[2 * n :]


def rest_kernel(rows, squares, gate_ref, up_ref, give2, give1, give0, *kept):
    n = ROWS_DEV
    into = [give2.at[0], give2.at[1], give1.at[0], give1.at[1], give0, *kept]
    late = slice(FIRST * n, len(ORDER) * n)
    for lanes, value in products(rows.at[late], squares.at[late], gate_ref, up_ref, lambda ref: None):
        for i, ref in enumerate(into):
            ref[:, lanes] = value[i * n : (i + 1) * n]


def project(prefix_len, norm_gain, mine, theirs, gate_weight, up_weight):
    width, hidden_width = gate_weight.shape
    n = ROWS_DEV
    part = (n, 2 * hidden_width + LANE)
    all_rows = len(ORDER) * n
    own, rows, squares, gate, up, far, following = pl.pallas_call(
        first_kernel,
        out_shape=in_vmem(
            ((n, width), BF),
            ((all_rows, width), BF),
            ((all_rows, LANE), BF),
            (gate_weight.shape, BF),
            (up_weight.shape, BF),
            (part, BF),
            ((2, *part), BF),
        ),
        in_specs=[SMEM, HBM, VMEM, VMEM, HBM, HBM],
        out_specs=(VMEM,) * 7,
        scratch_shapes=[
            pltpu.VMEM((ZN, n, width), BF),
            pltpu.VMEM((width,), F32),
            pltpu.SemaphoreType.DMA((3,)),
        ],
        compiler_params=PARAMS,
    )(prefix_len, in_hbm(norm_gain), mine, theirs, in_hbm(gate_weight), in_hbm(up_weight))
    give2, give1, give0, *kept = local(
        rest_kernel,
        [((2, *part), BF)] * 2 + [(part, BF)] * 9,
        rows,
        squares,
        gate,
        up,
        cost=cost((len(ORDER) - FIRST) * n, width, part[1]),
    )
    return own, [give0, give1, give2, following, far], kept


def summed(*refs):
    total = refs[0].astype(F32)
    for ref in refs[1:]:
        total = total + ref.astype(F32)
    return total.astype(BF)


def add_first_kernel(mine, x, out_up, out_down):
    low = out_up.shape[1]
    out_up[...] = summed(mine[:, :low], x[:, :low])
    out_down[...] = summed(mine[:, low:], x[:, low:])


def add_far_kernel(mine_up, mine_down, x, up, down, out_up, out_down):
    low = up.shape[1]
    out_up[:, :low] = summed(mine_up[:, :low], x[0, :, :low], up[...])
    out_up[:, low:] = summed(mine_up[:, low:], x[0, :, low:])
    out_down[:, :low] = summed(mine_down[:, :low], x[1, :, :low])
    out_down[:, low:] = summed(mine_down[:, low:], x[1, :, low:], down[...])


def add_ring_kernel(mine_up, mine_down, x, up, down, out_up, out_down):
    out_up[...] = summed(mine_up[...], x[0], up[...])
    out_down[...] = summed(mine_down[...], x[1], down[...])


def gated_kernel(mine, x, up, down, out):
    width = out.shape[1]

    def total(lanes):
        parts = [ref[:, lanes].astype(F32) for ref in (mine, x, up, down)]
        return (parts[0] + parts[1]) + (parts[2] + parts[3])

    squares = total(slice(2 * width, 2 * width + LANE))
    scale = lax.rsqrt(jnp.sum(squares, axis=1, keepdims=True) * F32(1 / 16384) + 1e-05)
    gate = total(slice(0, width)) * scale
    lift = total(slice(width, 2 * width)) * scale
    out[...] = (gate / (1 + jnp.exp(-gate)) * lift).astype(BF)


def cost(rows, depth, columns):
    return pl.CostEstimate(
        flops=2 * rows * depth * columns, bytes_accessed=2 * depth * columns, transcendentals=0
    )


def local(kernel, shapes, *args, cost=None):
    return pl.pallas_call(
        kernel,
        out_shape=in_vmem(*shapes),
        in_specs=[VMEM] * len(args),
        out_specs=(VMEM,) * len(shapes) if len(shapes) > 1 else VMEM,
        compiler_params=PARAMS,
        cost_estimate=cost,
    )(*args)


def down_kernel(*refs):
    own, up1, down1, up2, down2, up3, down3, up4, down4, x0, x1, x2, x3, x4, down_ref = refs[:15]
    give, keep, rows = refs[15:]
    n = ROWS_DEV
    batch_index, mp_index = lax.axis_index("batch"), lax.axis_index("mp")
    z, flip = batch_index >> 1, (batch_index ^ mp_index) & 1
    ours = {0: own, 1: down1, 2: down2, 3: down3, 5: up3, 6: up2, 7: up1}
    partners = {0: x0, 7: x1.at[0], 1: x1.at[1], 6: x2.at[0], 2: x2.at[1], 5: x3.at[0], 3: x3.at[1], FAR: x4}
    for s in range(ZN):
        for j, found in enumerate((ours, partners)):
            target = (z + s) & (ZN - 1)
            other = (flip + j) & 1
            at = pl.ds(pl.multiple_of((1 - other) * ZN * n + target * n, n), n)
            if s in found:
                rows[at, :] = found[s][...]
            else:
                rows[at, : up4.shape[1]] = up4[...]
                rows[at, up4.shape[1] :] = down4[...]
    step = 2 * LANE
    for i in range(0, down_ref.shape[1], step):
        lanes = slice(i, i + step)
        product = jnp.dot(rows[...], down_ref[:, lanes], preferred_element_type=F32)
        for target in range(ZN):
            give[target, :, lanes] = product[target * n : (target + 1) * n].astype(BF)
            at = (ZN + target) * n
            keep[target, :, lanes] = product[at : at + n]


def project_down(blocks, down_weight):
    hidden_width, width = down_weight.shape
    shape = (ZN, ROWS_DEV, width)
    return pl.pallas_call(
        down_kernel,
        out_shape=in_vmem((shape, BF), (shape, F32)),
        in_specs=[VMEM] * (len(blocks) + 1),
        out_specs=(VMEM, VMEM),
        scratch_shapes=[pltpu.VMEM((2 * ZN * ROWS_DEV, hidden_width), BF)],
        compiler_params=PARAMS,
    )(*blocks, down_weight)


def add_core_kernel(keep, come, out):
    out[...] = (keep[...] + come[...].astype(F32)).astype(BF)


def finish_kernel(own, parts, out):
    total = own[...].astype(F32)
    for i in range(parts.shape[0]):
        total = total + parts[i].astype(F32)
    out[...] = total.astype(BF)


def after(*values):
    return lax.optimization_barrier(values)


def body(
    hidden_in,
    queries,
    key_cache,
    value_cache,
    question,
    prefix_len,
    norm_gain,
    gate_weight,
    up_weight,
    down_weight,
):
    rows, width = queries.shape
    hidden_width = gate_weight.shape[1]

    sent = prepare(prefix_len, question, queries, hidden_in, key_cache, value_cache)
    came = transpose_mesh(sent)
    mine = over_plane(jnp.broadcast_to(came[None], (ZN, *came.shape)))
    theirs = core_pair(mine)
    own, give, kept = project(prefix_len, norm_gain, mine, theirs, gate_weight, up_weight)
    part = kept[0].shape
    half = (part[1] // LANE) // 2 * LANE
    ends = [((rows, half), BF), ((rows, part[1] - half), BF)]

    far, ahead = after(give[4], give[3])
    far, following = x_pair(far), x_pair(ahead)
    up, down = local(add_first_kernel, ends, kept[4], far)
    for step in (4, 3, 2, 1):
        up, down, ahead = after(up, down, give[step - 2] if step > 1 else give[0])
        x = following
        if step > 1:
            following = x_pair(ahead)
        up, down = along_z(up, 1), along_z(down, -1)
        up, down, x = after(up, down, x)
        if step > 1:
            up, down = local(
                add_far_kernel if step == 4 else add_ring_kernel,
                [(part, BF)] * 2,
                kept[step - 1],
                kept[ZN + 1 - step],
                x,
                up,
                down,
            )
    hidden = local(gated_kernel, [((rows, hidden_width), BF)], kept[0], x, up, down)

    up, down, across = hidden, hidden, hidden
    blocks, partners = [hidden], []
    for step in range(3):
        up, down, across = after(up, down, across)
        up, down, came = along_z(up, 1), along_z(down, -1), x_pair(across)
        if partners:
            up, down, partners[-1] = after(up, down, partners[-1])
        else:
            up, down = after(up, down)
        partners.append(came)
        blocks += [up, down]
        across = jnp.stack([up, down])
    half = (hidden_width // LANE + 1) // 2 * LANE
    up, down, across = after(up[:, :half], down[:, half:], across)
    up, down, came = along_z(up, 1), along_z(down, -1), x_pair(across)
    up, down, partners[-1] = after(up, down, partners[-1])
    partners += [came, x_pair(jnp.concatenate([up, down], axis=1))]
    blocks += [up, down, *partners]
    send, keep = project_down(blocks, down_weight)
    held = local(add_core_kernel, [(keep.shape, BF)], keep, core_pair(send))
    parts = over_plane(held)
    return pl.pallas_call(
        finish_kernel,
        out_shape=jax.ShapeDtypeStruct((rows, width), BF),
        in_specs=[VMEM, VMEM],
        out_specs=VMEM,
        compiler_params=PARAMS,
    )(own, parts)


def solution(mesh):
    return jax.shard_map(
        body,
        mesh=mesh,
        in_specs=(
            P("batch", None),
            P("batch", "mp"),
            P("batch", None),
            P("batch", None),
            P("batch"),
            P(),
            P(),
            P("batch", "mp"),
            P("batch", "mp"),
            P("mp", "batch"),
        ),
        out_specs=P("mp", "batch"),
        check_vma=False,
    )
```

```python
import jax
import jax.numpy as jnp
from jax import lax
from jax.experimental import pallas as pl
from jax.experimental.pallas import tpu as pltpu
from jax.sharding import PartitionSpec as P

HEADS = 128
KV_HEADS = 8
HEAD_DIM = 128
PREFIX = 24
ROWS_DEV = 32
ZN = 8
LANE = 128
BF = jnp.bfloat16
F32 = jnp.float32
PLANE = [[2 * i + core for i in range(8)] for core in range(2)]
VMEM = pl.BlockSpec(memory_space=pltpu.VMEM)
SMEM = pl.BlockSpec(memory_space=pltpu.SMEM)
ANY = pl.BlockSpec(memory_space=pl.ANY)
HBM = pl.BlockSpec(memory_space=pltpu.HBM)
PARAMS = pltpu.CompilerParams(vmem_limit_bytes=28 * 2**20)


def permute(value, axis, target, count=16):
    return lax.ppermute(value, axis, [(i, target(i)) for i in range(count)])


def along_z(value, step):
    return permute(value, "batch", lambda i: (i + 2 * step) % 16)


def x_pair(value):
    return permute(value, "batch", lambda i: i ^ 1)


def core_pair(value):
    return permute(value, "mp", lambda i: i ^ 1)


def transpose_mesh(value):
    return lax.ppermute(
        value,
        ("batch", "mp"),
        [(b * 16 + m, m * 16 + b) for b in range(16) for m in range(16)],
    )


def over_plane(value):
    return lax.all_to_all(value, "mp", 0, 0, axis_index_groups=PLANE, tiled=True)


def in_vmem(*shapes):
    made = tuple(pltpu.VMEM(shape, dtype) for shape, dtype in shapes)
    return made if len(made) > 1 else made[0]


def in_hbm(value):
    return pltpu.with_memory_space_constraint(value, pltpu.HBM)


PAIRS = 8 * ROWS_DEV
QUERIES = PAIRS + 4 * 16
ASKED = QUERIES + 4 * 16


def mixed(scores, seen, values):
    scores = jnp.where(seen, scores * F32(HEAD_DIM**-0.5), F32(-1e30))
    weights = jnp.exp(scores - jnp.max(scores, axis=1, keepdims=True)).astype(BF)
    both = jnp.concatenate([values, jnp.ones(values.shape, BF)], axis=1)
    product = jnp.dot(weights, both, preferred_element_type=F32)
    return (product[:, :HEAD_DIM] / product[:, HEAD_DIM:]).astype(BF)


def scored(queries, keys):
    return lax.dot_general(queries, keys, (((1,), (1,)), ((), ())), preferred_element_type=F32)


def prepare_kernel(lengths, questions, queries_ref, hidden_ref, key_ref, value_ref, out_ref, queries, hidden, pair, length_ref, question_ref, sems):
    width = queries.shape[1]
    heads = width // HEAD_DIM
    batch_index, mp_index = lax.axis_index("batch"), lax.axis_index("mp")
    head = pl.ds(pl.multiple_of((mp_index >> 1) * HEAD_DIM, HEAD_DIM), HEAD_DIM)
    at = pl.ds(pl.multiple_of(mp_index * width, width), width)
    copies = [
        pltpu.make_async_copy(source, target, sems.at[i])
        for i, (source, target) in enumerate(
            [
                (key_ref.at[:, head], pair.at[:, :HEAD_DIM]),
                (queries_ref, queries),
                (value_ref.at[:, head], pair.at[:, HEAD_DIM:]),
                (hidden_ref.at[:, at], hidden),
                (lengths, length_ref),
                (questions, question_ref),
            ]
        )
    ]
    for copy in copies:
        copy.start()
    copies[4].wait()
    copies[5].wait()
    shape = (ROWS_DEV, ROWS_DEV)
    row = lax.broadcasted_iota(jnp.int32, shape, 0)
    key = lax.broadcasted_iota(jnp.int32, shape, 1)
    seen = (key <= row) & (key < length_ref[batch_index])
    seen = jnp.concatenate([seen.astype(F32)] * heads, axis=0) > 0
    shape = (16, LANE)
    option = lax.broadcasted_iota(jnp.int32, shape, 0) & (ROWS_DEV - PREFIX - 1)
    asked = jnp.zeros(shape, jnp.int32)
    for i in range(ROWS_DEV - PREFIX):
        asked = jnp.where(option == i, question_ref[i], asked)
    out_ref[ASKED : ASKED + 16, :] = asked.astype(F32).astype(BF)
    copies[0].wait()
    copies[1].wait()
    stacked = jnp.concatenate(
        [queries[:, h * HEAD_DIM : (h + 1) * HEAD_DIM] for h in range(heads)], axis=0
    )
    copies[2].wait()
    context = mixed(scored(stacked, pair[:, :HEAD_DIM]), seen, pair[:, HEAD_DIM:])
    for i in range(2):
        for j in range(2):
            at = PAIRS + (2 * i + j) * 16
            out_ref[at : at + 16, :] = pair[16 * i : 16 * i + 16, j * HEAD_DIM : (j + 1) * HEAD_DIM]
    last = queries[16:].astype(F32)[PREFIX - 16 :]
    half = width // 2
    for h in range(heads // 2):
        first = h * HEAD_DIM
        tile = [last[:, at : at + HEAD_DIM] for at in (first, first + half)]
        at = QUERIES + h * 16
        out_ref[at : at + 16, :] = jnp.concatenate(tile, axis=0).astype(BF)
    copies[3].wait()
    prefix = lax.broadcasted_iota(jnp.int32, (ROWS_DEV, HEAD_DIM), 0) < PREFIX
    for h in range(heads):
        columns = slice(h * HEAD_DIM, (h + 1) * HEAD_DIM)
        mine = context[h * ROWS_DEV : (h + 1) * ROWS_DEV].astype(F32)
        mine = jnp.where(prefix, mine, F32(0))
        at = slice(h * ROWS_DEV, (h + 1) * ROWS_DEV)
        out_ref[at, :] = (hidden[:, columns].astype(F32) + mine).astype(BF)


def prepare(prefix_len, question, queries, hidden_in, key_cache, value_cache):
    rows, width = queries.shape
    return pl.pallas_call(
        prepare_kernel,
        out_shape=in_vmem(((ASKED + 16, LANE), BF)),
        in_specs=[HBM] * 6,
        out_specs=VMEM,
        scratch_shapes=[
            pltpu.VMEM((rows, width), BF),
            pltpu.VMEM((rows, width), BF),
            pltpu.VMEM((rows, 2 * HEAD_DIM), BF),
            pltpu.SMEM(prefix_len.shape, jnp.int32),
            pltpu.SMEM(question.shape, jnp.int32),
            pltpu.SemaphoreType.DMA((6,)),
        ],
        compiler_params=PARAMS,
    )(*map(in_hbm, (prefix_len, question, queries, hidden_in, key_cache, value_cache)))


FAR = 4


ORDER = [(s, 1) for s in (FAR, 3, 5, 2, 6, 1, 7, 0)] + [(s, 0) for s in range(ZN)]
FIRST = 3


def products(rows, squares, gate_ref, up_ref):
    tiles = gate_ref.shape[1] // LANE
    for base, ref in ((0, gate_ref), (tiles, up_ref)):
        for t in range(0, tiles, 2):
            lanes = slice(t * LANE, min(t + 2, tiles) * LANE)
            product = jnp.dot(rows[...], ref[:, lanes], preferred_element_type=F32).astype(BF)
            yield slice((base + t) * LANE, (base + t) * LANE + product.shape[1]), product
    yield slice(2 * tiles * LANE, (2 * tiles + 1) * LANE), squares[...]


def first_kernel(length_ref, gain_ref, mine_ref, theirs_ref, gate_ref, up_ref, *refs):
    own_ref, rows, squares, far_ref, next_ref, residual, gain, sem = refs
    n = ROWS_DEV
    width = own_ref.shape[1]
    half = width // 2
    batch_index, mp_index = lax.axis_index("batch"), lax.axis_index("mp")
    z, core = batch_index >> 1, mp_index & 1
    flip = (batch_index & 1) ^ core
    fetch = pltpu.make_async_copy(gain_ref.at[pl.ds(batch_index * width, width)], gain, sem)
    fetch.start()

    blocks = [(ref, i) for ref in (mine_ref, theirs_ref) for i in range(ZN)]
    options = ROWS_DEV - PREFIX

    def gathered(*parts):
        return jnp.concatenate([ref[i, at : at + 16, :] for ref, i in blocks for at in parts], axis=0)

    keys, values = gathered(PAIRS, PAIRS + 32), gathered(PAIRS + 16, PAIRS + 48)
    total = n * len(blocks)
    place = lax.broadcasted_iota(jnp.int32, (8, total), 1)
    order = place >> 5
    live = jnp.zeros(place.shape, jnp.int32)
    for i in range(len(blocks)):
        live = jnp.where(order == i, length_ref[((i & (ZN - 1)) << 1) + ((i >> 3) ^ core)], live)
    owner = ((order & (ZN - 1)) << 1) + ((order >> 3) ^ core)
    owner = jnp.where((place & (n - 1)) < live, owner, -1)
    asked = gathered(ASKED).astype(F32).astype(jnp.int32)
    row = lax.broadcasted_iota(jnp.int32, (asked.shape[0], 1), 0)
    itself = (row >> 4) * n + PREFIX + (row & (options - 1))
    seen = (jnp.tile(owner, (asked.shape[0] // 8, 1)) == jnp.tile(asked, (1, total // LANE))) | (
        jnp.tile(place, (asked.shape[0] // 8, 1)) == itself
    )
    contexts = []
    for h in range(half // HEAD_DIM):
        context = mixed(scored(gathered(QUERIES + h * 16), keys), seen, values)
        contexts.append(context.astype(F32))
    fetch.wait()
    scale = gain[...].reshape(1, width)
    for k, (ref, i) in enumerate(blocks):
        s = (i - z) & (ZN - 1)
        j = flip if ref is mine_ref else 1 - flip
        position = ZN + s
        for index, (target, _) in enumerate(ORDER[:ZN]):
            position = jnp.where((s == target) & (j == 1), index, position)
        into = pl.ds(pl.multiple_of(position * n, n), n)
        total = jnp.zeros((n, LANE), F32)
        for tile in range(width // LANE):
            lanes = slice(tile * LANE, (tile + 1) * LANE)
            at = k * 16 + tile // len(contexts) * options
            added = contexts[tile % len(contexts)][at : at + options]
            added = jnp.concatenate([jnp.zeros((PREFIX, LANE), F32), added], axis=0)
            part = (ref[i, tile * n : (tile + 1) * n, :].astype(F32) + added).astype(BF)
            if ref is mine_ref:
                residual[i, :, lanes] = part
            x = part.astype(F32)
            rows[into, lanes] = (x * scale[:, lanes]).astype(BF)
            total = total + x * x
        squares[into, :] = total.astype(BF)
    own_ref[...] = residual[mp_index >> 1]
    early = slice(0, FIRST * n)
    for lanes, value in products(rows.at[early], squares.at[early], gate_ref, up_ref):
        far_ref[:, lanes] = value[:n]
        next_ref[0, :, lanes] = value[n : 2 * n]
        next_ref[1, :, lanes] = value[2 * n :]


def rest_kernel(rows, squares, gate_ref, up_ref, give2, give1, give0, *kept):
    n = ROWS_DEV
    into = [give2.at[0], give2.at[1], give1.at[0], give1.at[1], give0, *kept]
    late = slice(FIRST * n, len(ORDER) * n)
    for lanes, value in products(rows.at[late], squares.at[late], gate_ref, up_ref):
        for i, ref in enumerate(into):
            ref[:, lanes] = value[i * n : (i + 1) * n]


def fetch_kernel(gate_hbm, up_hbm, gate_ref, up_ref, sems):
    copies = (
        pltpu.make_async_copy(gate_hbm, gate_ref, sems.at[0]),
        pltpu.make_async_copy(up_hbm, up_ref, sems.at[1]),
    )
    for copy in copies:
        copy.start()
    for copy in copies:
        copy.wait()


def fetch(gate_weight, up_weight):
    return pl.pallas_call(
        fetch_kernel,
        out_shape=in_vmem((gate_weight.shape, BF), (up_weight.shape, BF)),
        in_specs=[HBM, HBM],
        out_specs=(VMEM, VMEM),
        scratch_shapes=[pltpu.SemaphoreType.DMA((2,))],
        compiler_params=PARAMS,
        cost_estimate=cost(1, *gate_weight.shape),
    )(in_hbm(gate_weight), in_hbm(up_weight))


def project(prefix_len, norm_gain, mine, theirs, gate_weight, up_weight):
    width, hidden_width = gate_weight.shape
    n = ROWS_DEV
    part = (n, 2 * hidden_width + LANE)
    all_rows = len(ORDER) * n
    own, rows, squares, far, following = pl.pallas_call(
        first_kernel,
        out_shape=in_vmem(
            ((n, width), BF),
            ((all_rows, width), BF),
            ((all_rows, LANE), BF),
            (part, BF),
            ((2, *part), BF),
        ),
        in_specs=[SMEM, HBM, VMEM, VMEM, VMEM, VMEM],
        out_specs=(VMEM,) * 5,
        scratch_shapes=[
            pltpu.VMEM((ZN, n, width), BF),
            pltpu.VMEM((width,), F32),
            pltpu.SemaphoreType.DMA(()),
        ],
        compiler_params=PARAMS,
    )(prefix_len, in_hbm(norm_gain), mine, theirs, gate_weight, up_weight)
    give2, give1, give0, *kept = local(
        rest_kernel,
        [((2, *part), BF)] * 2 + [(part, BF)] * 9,
        rows,
        squares,
        gate_weight,
        up_weight,
        cost=cost((len(ORDER) - FIRST) * n, width, part[1]),
    )
    return own, [give0, give1, give2, following, far], kept


def summed(*refs):
    total = refs[0].astype(F32)
    for ref in refs[1:]:
        total = total + ref.astype(F32)
    return total.astype(BF)


def add_first_kernel(mine, x, out_up, out_down):
    low = out_up.shape[1]
    out_up[...] = summed(mine[:, :low], x[:, :low])
    out_down[...] = summed(mine[:, low:], x[:, low:])


def add_far_kernel(mine_up, mine_down, x, up, down, out_up, out_down):
    low = up.shape[1]
    out_up[:, :low] = summed(mine_up[:, :low], x[0, :, :low], up[...])
    out_up[:, low:] = summed(mine_up[:, low:], x[0, :, low:])
    out_down[:, :low] = summed(mine_down[:, :low], x[1, :, :low])
    out_down[:, low:] = summed(mine_down[:, low:], x[1, :, low:], down[...])


def add_ring_kernel(mine_up, mine_down, x, up, down, out_up, out_down):
    out_up[...] = summed(mine_up[...], x[0], up[...])
    out_down[...] = summed(mine_down[...], x[1], down[...])


def gated_kernel(mine, x, up, down, out):
    width = out.shape[1]

    def total(lanes):
        parts = [ref[:, lanes].astype(F32) for ref in (mine, x, up, down)]
        return (parts[0] + parts[1]) + (parts[2] + parts[3])

    squares = total(slice(2 * width, 2 * width + LANE))
    scale = lax.rsqrt(jnp.sum(squares, axis=1, keepdims=True) * F32(1 / 16384) + 1e-05)
    gate = total(slice(0, width)) * scale
    lift = total(slice(width, 2 * width)) * scale
    out[...] = (gate / (1 + jnp.exp(-gate)) * lift).astype(BF)


def cost(rows, depth, columns):
    return pl.CostEstimate(
        flops=2 * rows * depth * columns, bytes_accessed=2 * depth * columns, transcendentals=0
    )


def local(kernel, shapes, *args, cost=None):
    return pl.pallas_call(
        kernel,
        out_shape=in_vmem(*shapes),
        in_specs=[VMEM] * len(args),
        out_specs=(VMEM,) * len(shapes) if len(shapes) > 1 else VMEM,
        compiler_params=PARAMS,
        cost_estimate=cost,
    )(*args)


def down_kernel(*refs):
    own, up1, down1, up2, down2, up3, down3, up4, down4, x0, x1, x2, x3, x4, down_ref = refs[:15]
    give, keep, rows = refs[15:]
    n = ROWS_DEV
    batch_index, mp_index = lax.axis_index("batch"), lax.axis_index("mp")
    z, flip = batch_index >> 1, (batch_index ^ mp_index) & 1
    ours = {0: own, 1: down1, 2: down2, 3: down3, 5: up3, 6: up2, 7: up1}
    partners = {0: x0, 7: x1.at[0], 1: x1.at[1], 6: x2.at[0], 2: x2.at[1], 5: x3.at[0], 3: x3.at[1], FAR: x4}
    for s in range(ZN):
        for j, found in enumerate((ours, partners)):
            target = (z + s) & (ZN - 1)
            other = (flip + j) & 1
            at = pl.ds(pl.multiple_of((1 - other) * ZN * n + target * n, n), n)
            if s in found:
                rows[at, :] = found[s][...]
            else:
                rows[at, : up4.shape[1]] = up4[...]
                rows[at, up4.shape[1] :] = down4[...]
    step = 2 * LANE
    for i in range(0, down_ref.shape[1], step):
        lanes = slice(i, i + step)
        product = jnp.dot(rows[...], down_ref[:, lanes], preferred_element_type=F32)
        for target in range(ZN):
            give[target, :, lanes] = product[target * n : (target + 1) * n].astype(BF)
            at = (ZN + target) * n
            keep[target, :, lanes] = product[at : at + n]


def project_down(blocks, down_weight):
    hidden_width, width = down_weight.shape
    shape = (ZN, ROWS_DEV, width)
    return pl.pallas_call(
        down_kernel,
        out_shape=in_vmem((shape, BF), (shape, F32)),
        in_specs=[VMEM] * (len(blocks) + 1),
        out_specs=(VMEM, VMEM),
        scratch_shapes=[pltpu.VMEM((2 * ZN * ROWS_DEV, hidden_width), BF)],
        compiler_params=PARAMS,
    )(*blocks, down_weight)


def add_core_kernel(keep, come, out):
    out[...] = (keep[...] + come[...].astype(F32)).astype(BF)


def finish_kernel(own, parts, out):
    total = own[...].astype(F32)
    for i in range(parts.shape[0]):
        total = total + parts[i].astype(F32)
    out[...] = total.astype(BF)


def after(*values):
    return lax.optimization_barrier(values)


def body(
    hidden_in,
    queries,
    key_cache,
    value_cache,
    question,
    prefix_len,
    norm_gain,
    gate_weight,
    up_weight,
    down_weight,
):
    rows, width = queries.shape
    hidden_width = gate_weight.shape[1]

    sent = prepare(prefix_len, question, queries, hidden_in, key_cache, value_cache)
    sent, gate_weight, up_weight = after(sent, gate_weight, up_weight)
    came, gate_weight, up_weight = after(transpose_mesh(sent), *fetch(gate_weight, up_weight))
    mine = over_plane(jnp.broadcast_to(came[None], (ZN, *came.shape)))
    theirs = core_pair(mine)
    own, give, kept = project(prefix_len, norm_gain, mine, theirs, gate_weight, up_weight)
    part = kept[0].shape
    half = (part[1] // LANE) // 2 * LANE
    ends = [((rows, half), BF), ((rows, part[1] - half), BF)]

    far, ahead = after(give[4], give[3])
    far, following = x_pair(far), x_pair(ahead)
    up, down = local(add_first_kernel, ends, kept[4], far)
    for step in (4, 3, 2, 1):
        up, down, ahead = after(up, down, give[step - 2] if step > 1 else give[0])
        x = following
        if step > 1:
            following = x_pair(ahead)
        up, down = along_z(up, 1), along_z(down, -1)
        up, down, x = after(up, down, x)
        if step > 1:
            up, down = local(
                add_far_kernel if step == 4 else add_ring_kernel,
                [(part, BF)] * 2,
                kept[step - 1],
                kept[ZN + 1 - step],
                x,
                up,
                down,
            )
    hidden = local(gated_kernel, [((rows, hidden_width), BF)], kept[0], x, up, down)

    up, down, across = hidden, hidden, hidden
    blocks, partners = [hidden], []
    for step in range(3):
        up, down, across = after(up, down, across)
        up, down, came = along_z(up, 1), along_z(down, -1), x_pair(across)
        if partners:
            up, down, partners[-1] = after(up, down, partners[-1])
        else:
            up, down = after(up, down)
        partners.append(came)
        blocks += [up, down]
        across = jnp.stack([up, down])
    half = (hidden_width // LANE + 1) // 2 * LANE
    up, down, across = after(up[:, :half], down[:, half:], across)
    up, down, came = along_z(up, 1), along_z(down, -1), x_pair(across)
    up, down, partners[-1] = after(up, down, partners[-1])
    partners += [came, x_pair(jnp.concatenate([up, down], axis=1))]
    blocks += [up, down, *partners]
    send, keep = project_down(blocks, down_weight)
    held = local(add_core_kernel, [(keep.shape, BF)], keep, core_pair(send))
    parts = over_plane(held)
    return pl.pallas_call(
        finish_kernel,
        out_shape=jax.ShapeDtypeStruct((rows, width), BF),
        in_specs=[VMEM, VMEM],
        out_specs=VMEM,
        compiler_params=PARAMS,
    )(own, parts)


def solution(mesh):
    return jax.shard_map(
        body,
        mesh=mesh,
        in_specs=(
            P("batch", None),
            P("batch", "mp"),
            P("batch", None),
            P("batch", None),
            P("batch"),
            P(),
            P(),
            P("batch", "mp"),
            P("batch", "mp"),
            P("mp", "batch"),
        ),
        out_specs=P("mp", "batch"),
        check_vma=False,
    )
```

```python
import jax
import jax.numpy as jnp
from jax import lax
from jax.experimental import pallas as pl
from jax.experimental.pallas import tpu as pltpu
from jax.sharding import PartitionSpec as P

HEADS = 128
KV_HEADS = 8
HEAD_DIM = 128
PREFIX = 24
ROWS_DEV = 32
ZN = 8
LANE = 128
BF = jnp.bfloat16
F32 = jnp.float32
PLANE = [[2 * i + core for i in range(8)] for core in range(2)]
VMEM = pl.BlockSpec(memory_space=pltpu.VMEM)
SMEM = pl.BlockSpec(memory_space=pltpu.SMEM)
ANY = pl.BlockSpec(memory_space=pl.ANY)
HBM = pl.BlockSpec(memory_space=pltpu.HBM)
PARAMS = pltpu.CompilerParams(vmem_limit_bytes=28 * 2**20)


def permute(value, axis, target, count=16):
    return lax.ppermute(value, axis, [(i, target(i)) for i in range(count)])


def along_z(value, step):
    return permute(value, "batch", lambda i: (i + 2 * step) % 16)


def mirrored(value, step):
    return lax.ppermute(
        value,
        ("batch", "mp"),
        [
            (b * 16 + m, (b + 2 * step * (1 - 2 * (m % 2))) % 16 * 16 + m)
            for b in range(16)
            for m in range(16)
        ],
    )


def x_pair(value):
    return permute(value, "batch", lambda i: i ^ 1)


def core_pair(value):
    return permute(value, "mp", lambda i: i ^ 1)


def transpose_mesh(value):
    return lax.ppermute(
        value,
        ("batch", "mp"),
        [(b * 16 + m, m * 16 + b) for b in range(16) for m in range(16)],
    )


def over_plane(value):
    return lax.all_to_all(value, "mp", 0, 0, axis_index_groups=PLANE, tiled=True)


def in_vmem(*shapes):
    made = tuple(pltpu.VMEM(shape, dtype) for shape, dtype in shapes)
    return made if len(made) > 1 else made[0]


def in_hbm(value):
    return pltpu.with_memory_space_constraint(value, pltpu.HBM)


PAIRS = 8 * ROWS_DEV
QUERIES = PAIRS + 4 * 16
ASKED = QUERIES + 4 * 16


def mixed(scores, seen, values):
    scores = jnp.where(seen, scores * F32(HEAD_DIM**-0.5), F32(-1e30))
    weights = jnp.exp(scores - jnp.max(scores, axis=1, keepdims=True)).astype(BF)
    both = jnp.concatenate([values, jnp.ones(values.shape, BF)], axis=1)
    product = jnp.dot(weights, both, preferred_element_type=F32)
    return (product[:, :HEAD_DIM] / product[:, HEAD_DIM:]).astype(BF)


def scored(queries, keys):
    return lax.dot_general(queries, keys, (((1,), (1,)), ((), ())), preferred_element_type=F32)


def prepare_kernel(lengths, questions, queries_ref, hidden_ref, key_ref, value_ref, out_ref, queries, hidden, pair, length_ref, question_ref, sems):
    width = queries.shape[1]
    heads = width // HEAD_DIM
    batch_index, mp_index = lax.axis_index("batch"), lax.axis_index("mp")
    head = pl.ds(pl.multiple_of((mp_index >> 1) * HEAD_DIM, HEAD_DIM), HEAD_DIM)
    at = pl.ds(pl.multiple_of(mp_index * width, width), width)
    copies = [
        pltpu.make_async_copy(source, target, sems.at[i])
        for i, (source, target) in enumerate(
            [
                (key_ref.at[:, head], pair.at[:, :HEAD_DIM]),
                (queries_ref, queries),
                (value_ref.at[:, head], pair.at[:, HEAD_DIM:]),
                (hidden_ref.at[:, at], hidden),
                (lengths, length_ref),
                (questions, question_ref),
            ]
        )
    ]
    for copy in copies:
        copy.start()
    copies[4].wait()
    copies[5].wait()
    shape = (ROWS_DEV, ROWS_DEV)
    row = lax.broadcasted_iota(jnp.int32, shape, 0)
    key = lax.broadcasted_iota(jnp.int32, shape, 1)
    seen = (key <= row) & (key < length_ref[batch_index])
    seen = jnp.concatenate([seen.astype(F32)] * heads, axis=0) > 0
    shape = (16, LANE)
    option = lax.broadcasted_iota(jnp.int32, shape, 0) & (ROWS_DEV - PREFIX - 1)
    asked = jnp.zeros(shape, jnp.int32)
    for i in range(ROWS_DEV - PREFIX):
        asked = jnp.where(option == i, question_ref[i], asked)
    out_ref[ASKED : ASKED + 16, :] = asked.astype(F32).astype(BF)
    copies[0].wait()
    copies[1].wait()
    stacked = jnp.concatenate(
        [queries[:, h * HEAD_DIM : (h + 1) * HEAD_DIM] for h in range(heads)], axis=0
    )
    copies[2].wait()
    context = mixed(scored(stacked, pair[:, :HEAD_DIM]), seen, pair[:, HEAD_DIM:])
    for i in range(2):
        for j in range(2):
            at = PAIRS + (2 * i + j) * 16
            out_ref[at : at + 16, :] = pair[16 * i : 16 * i + 16, j * HEAD_DIM : (j + 1) * HEAD_DIM]
    last = queries[16:].astype(F32)[PREFIX - 16 :]
    half = width // 2
    for h in range(heads // 2):
        first = h * HEAD_DIM
        tile = [last[:, at : at + HEAD_DIM] for at in (first, first + half)]
        at = QUERIES + h * 16
        out_ref[at : at + 16, :] = jnp.concatenate(tile, axis=0).astype(BF)
    copies[3].wait()
    prefix = lax.broadcasted_iota(jnp.int32, (ROWS_DEV, HEAD_DIM), 0) < PREFIX
    for h in range(heads):
        columns = slice(h * HEAD_DIM, (h + 1) * HEAD_DIM)
        mine = context[h * ROWS_DEV : (h + 1) * ROWS_DEV].astype(F32)
        mine = jnp.where(prefix, mine, F32(0))
        at = slice(h * ROWS_DEV, (h + 1) * ROWS_DEV)
        out_ref[at, :] = (hidden[:, columns].astype(F32) + mine).astype(BF)


def prepare(prefix_len, question, queries, hidden_in, key_cache, value_cache):
    rows, width = queries.shape
    return pl.pallas_call(
        prepare_kernel,
        out_shape=in_vmem(((ASKED + 16, LANE), BF)),
        in_specs=[HBM] * 6,
        out_specs=VMEM,
        scratch_shapes=[
            pltpu.VMEM((rows, width), BF),
            pltpu.VMEM((rows, width), BF),
            pltpu.VMEM((rows, 2 * HEAD_DIM), BF),
            pltpu.SMEM(prefix_len.shape, jnp.int32),
            pltpu.SMEM(question.shape, jnp.int32),
            pltpu.SemaphoreType.DMA((6,)),
        ],
        compiler_params=PARAMS,
    )(*map(in_hbm, (prefix_len, question, queries, hidden_in, key_cache, value_cache)))


FAR = 4


ORDER = [(s, 1) for s in (FAR, 3, 5, 2, 6, 1, 7, 0)] + [(s, 0) for s in range(ZN)]
FIRST = 3


def products(rows, squares, gate_ref, up_ref):
    tiles = gate_ref.shape[1] // LANE
    for base, ref in ((0, gate_ref), (tiles, up_ref)):
        for t in range(0, tiles, 2):
            lanes = slice(t * LANE, min(t + 2, tiles) * LANE)
            product = jnp.dot(rows[...], ref[:, lanes], preferred_element_type=F32).astype(BF)
            yield slice((base + t) * LANE, (base + t) * LANE + product.shape[1]), product
    yield slice(2 * tiles * LANE, (2 * tiles + 1) * LANE), squares[...]


def first_kernel(length_ref, gain_ref, mine_ref, theirs_ref, gate_ref, up_ref, *refs):
    own_ref, rows, squares, far_ref, next_ref, residual, gain, sem = refs
    n = ROWS_DEV
    width = own_ref.shape[1]
    half = width // 2
    batch_index, mp_index = lax.axis_index("batch"), lax.axis_index("mp")
    z, core = batch_index >> 1, mp_index & 1
    flip = (batch_index & 1) ^ core
    fetch = pltpu.make_async_copy(gain_ref.at[pl.ds(batch_index * width, width)], gain, sem)
    fetch.start()

    blocks = [(ref, i) for ref in (mine_ref, theirs_ref) for i in range(ZN)]
    options = ROWS_DEV - PREFIX

    def gathered(*parts):
        return jnp.concatenate([ref[i, at : at + 16, :] for ref, i in blocks for at in parts], axis=0)

    keys, values = gathered(PAIRS, PAIRS + 32), gathered(PAIRS + 16, PAIRS + 48)
    total = n * len(blocks)
    place = lax.broadcasted_iota(jnp.int32, (8, total), 1)
    order = place >> 5
    live = jnp.zeros(place.shape, jnp.int32)
    for i in range(len(blocks)):
        live = jnp.where(order == i, length_ref[((i & (ZN - 1)) << 1) + ((i >> 3) ^ core)], live)
    owner = ((order & (ZN - 1)) << 1) + ((order >> 3) ^ core)
    owner = jnp.where((place & (n - 1)) < live, owner, -1)
    asked = gathered(ASKED).astype(F32).astype(jnp.int32)
    row = lax.broadcasted_iota(jnp.int32, (asked.shape[0], 1), 0)
    itself = (row >> 4) * n + PREFIX + (row & (options - 1))
    seen = (jnp.tile(owner, (asked.shape[0] // 8, 1)) == jnp.tile(asked, (1, total // LANE))) | (
        jnp.tile(place, (asked.shape[0] // 8, 1)) == itself
    )
    contexts = []
    for h in range(half // HEAD_DIM):
        context = mixed(scored(gathered(QUERIES + h * 16), keys), seen, values)
        contexts.append(context.astype(F32))
    fetch.wait()
    scale = gain[...].reshape(1, width)
    for k, (ref, i) in enumerate(blocks):
        s = (i - z) & (ZN - 1)
        j = flip if ref is mine_ref else 1 - flip
        position = ZN + s
        for index, (target, _) in enumerate(ORDER[:ZN]):
            position = jnp.where((s == target) & (j == 1), index, position)
        into = pl.ds(pl.multiple_of(position * n, n), n)
        total = jnp.zeros((n, LANE), F32)
        for tile in range(width // LANE):
            lanes = slice(tile * LANE, (tile + 1) * LANE)
            at = k * 16 + tile // len(contexts) * options
            added = contexts[tile % len(contexts)][at : at + options]
            added = jnp.concatenate([jnp.zeros((PREFIX, LANE), F32), added], axis=0)
            part = (ref[i, tile * n : (tile + 1) * n, :].astype(F32) + added).astype(BF)
            if ref is mine_ref:
                residual[i, :, lanes] = part
            x = part.astype(F32)
            rows[into, lanes] = (x * scale[:, lanes]).astype(BF)
            total = total + x * x
        squares[into, :] = total.astype(BF)
    own_ref[...] = residual[mp_index >> 1]
    early = slice(0, FIRST * n)
    for lanes, value in products(rows.at[early], squares.at[early], gate_ref, up_ref):
        far_ref[:, lanes] = value[:n]
        next_ref[0, :, lanes] = value[n : 2 * n]
        next_ref[1, :, lanes] = value[2 * n :]


def rest_kernel(rows, squares, gate_ref, up_ref, give2, give1, give0, *kept):
    n = ROWS_DEV
    into = [give2.at[0], give2.at[1], give1.at[0], give1.at[1], give0, *kept]
    late = slice(FIRST * n, len(ORDER) * n)
    for lanes, value in products(rows.at[late], squares.at[late], gate_ref, up_ref):
        for i, ref in enumerate(into):
            ref[:, lanes] = value[i * n : (i + 1) * n]


def fetch_kernel(gate_hbm, up_hbm, gate_ref, up_ref, sems):
    copies = (
        pltpu.make_async_copy(gate_hbm, gate_ref, sems.at[0]),
        pltpu.make_async_copy(up_hbm, up_ref, sems.at[1]),
    )
    for copy in copies:
        copy.start()
    for copy in copies:
        copy.wait()


def fetch(gate_weight, up_weight):
    return pl.pallas_call(
        fetch_kernel,
        out_shape=in_vmem((gate_weight.shape, BF), (up_weight.shape, BF)),
        in_specs=[HBM, HBM],
        out_specs=(VMEM, VMEM),
        scratch_shapes=[pltpu.SemaphoreType.DMA((2,))],
        compiler_params=PARAMS,
        cost_estimate=cost(1, *gate_weight.shape),
    )(in_hbm(gate_weight), in_hbm(up_weight))


def project(prefix_len, norm_gain, mine, theirs, gate_weight, up_weight):
    width, hidden_width = gate_weight.shape
    n = ROWS_DEV
    part = (n, 2 * hidden_width + LANE)
    all_rows = len(ORDER) * n
    own, rows, squares, far, following = pl.pallas_call(
        first_kernel,
        out_shape=in_vmem(
            ((n, width), BF),
            ((all_rows, width), BF),
            ((all_rows, LANE), BF),
            (part, BF),
            ((2, *part), BF),
        ),
        in_specs=[SMEM, HBM, VMEM, VMEM, VMEM, VMEM],
        out_specs=(VMEM,) * 5,
        scratch_shapes=[
            pltpu.VMEM((ZN, n, width), BF),
            pltpu.VMEM((width,), F32),
            pltpu.SemaphoreType.DMA(()),
        ],
        compiler_params=PARAMS,
    )(prefix_len, in_hbm(norm_gain), mine, theirs, gate_weight, up_weight)
    give2, give1, give0, *kept = local(
        rest_kernel,
        [((2, *part), BF)] * 2 + [(part, BF)] * 9,
        rows,
        squares,
        gate_weight,
        up_weight,
        cost=cost((len(ORDER) - FIRST) * n, width, part[1]),
    )
    return own, [give0, give1, give2, following, far], kept


def summed(*refs):
    total = refs[0].astype(F32)
    for ref in refs[1:]:
        total = total + ref.astype(F32)
    return total.astype(BF)


def add_first_kernel(mine, x, out_up, out_down):
    low = out_up.shape[1]
    out_up[...] = summed(mine[:, :low], x[:, :low])
    out_down[...] = summed(mine[:, low:], x[:, low:])


def add_far_kernel(mine_up, mine_down, x, up, down, out_up, out_down):
    low = up.shape[1]
    out_up[:, :low] = summed(mine_up[:, :low], x[0, :, :low], up[...])
    out_up[:, low:] = summed(mine_up[:, low:], x[0, :, low:])
    out_down[:, :low] = summed(mine_down[:, :low], x[1, :, :low])
    out_down[:, low:] = summed(mine_down[:, low:], x[1, :, low:], down[...])


def add_ring_kernel(mine_up, mine_down, x, up, down, out_up, out_down):
    out_up[...] = summed(mine_up[...], x[0], up[...])
    out_down[...] = summed(mine_down[...], x[1], down[...])


def gated_kernel(mine, x, up, down, out):
    width = out.shape[1]

    def total(lanes):
        parts = [ref[:, lanes].astype(F32) for ref in (mine, x, up, down)]
        return (parts[0] + parts[1]) + (parts[2] + parts[3])

    squares = total(slice(2 * width, 2 * width + LANE))
    scale = lax.rsqrt(jnp.sum(squares, axis=1, keepdims=True) * F32(1 / 16384) + 1e-05)
    gate = total(slice(0, width)) * scale
    lift = total(slice(width, 2 * width)) * scale
    out[...] = (gate / (1 + jnp.exp(-gate)) * lift).astype(BF)


def cost(rows, depth, columns):
    return pl.CostEstimate(
        flops=2 * rows * depth * columns, bytes_accessed=2 * depth * columns, transcendentals=0
    )


def local(kernel, shapes, *args, cost=None):
    return pl.pallas_call(
        kernel,
        out_shape=in_vmem(*shapes),
        in_specs=[VMEM] * len(args),
        out_specs=(VMEM,) * len(shapes) if len(shapes) > 1 else VMEM,
        compiler_params=PARAMS,
        cost_estimate=cost,
    )(*args)


def down_kernel(*refs):
    own, up1, down1, up2, down2, up3, down3, up4, down4, x0, x1, x2, x3, x4, down_ref = refs[:15]
    give, keep, rows = refs[15:]
    n = ROWS_DEV
    batch_index, mp_index = lax.axis_index("batch"), lax.axis_index("mp")
    z, flip = batch_index >> 1, (batch_index ^ mp_index) & 1
    ours = {0: own, 1: down1, 2: down2, 3: down3, 5: up3, 6: up2, 7: up1}
    partners = {0: x0, 7: x1.at[0], 1: x1.at[1], 6: x2.at[0], 2: x2.at[1], 5: x3.at[0], 3: x3.at[1], FAR: x4}
    for s in range(ZN):
        for j, found in enumerate((ours, partners)):
            target = (z + s * (1 - 2 * (mp_index & 1))) & (ZN - 1)
            other = (flip + j) & 1
            at = pl.ds(pl.multiple_of((1 - other) * ZN * n + target * n, n), n)
            if s in found:
                rows[at, :] = found[s][...]
            else:
                rows[at, : up4.shape[1]] = up4[...]
                rows[at, up4.shape[1] :] = down4[...]
    step = 2 * LANE
    for i in range(0, down_ref.shape[1], step):
        lanes = slice(i, i + step)
        product = jnp.dot(rows[...], down_ref[:, lanes], preferred_element_type=F32)
        for target in range(ZN):
            give[target, :, lanes] = product[target * n : (target + 1) * n].astype(BF)
            at = (ZN + target) * n
            keep[target, :, lanes] = product[at : at + n]


def project_down(blocks, down_weight):
    hidden_width, width = down_weight.shape
    shape = (ZN, ROWS_DEV, width)
    return pl.pallas_call(
        down_kernel,
        out_shape=in_vmem((shape, BF), (shape, F32)),
        in_specs=[VMEM] * (len(blocks) + 1),
        out_specs=(VMEM, VMEM),
        scratch_shapes=[pltpu.VMEM((2 * ZN * ROWS_DEV, hidden_width), BF)],
        compiler_params=PARAMS,
    )(*blocks, down_weight)


def add_core_kernel(keep, come, out):
    out[...] = (keep[...] + come[...].astype(F32)).astype(BF)


def finish_kernel(own, parts, out):
    total = own[...].astype(F32)
    for i in range(parts.shape[0]):
        total = total + parts[i].astype(F32)
    out[...] = total.astype(BF)


def after(*values):
    return lax.optimization_barrier(values)


def body(
    hidden_in,
    queries,
    key_cache,
    value_cache,
    question,
    prefix_len,
    norm_gain,
    gate_weight,
    up_weight,
    down_weight,
):
    rows, width = queries.shape
    hidden_width = gate_weight.shape[1]

    sent = prepare(prefix_len, question, queries, hidden_in, key_cache, value_cache)
    sent, gate_weight, up_weight = after(sent, gate_weight, up_weight)
    came, gate_weight, up_weight = after(transpose_mesh(sent), *fetch(gate_weight, up_weight))
    mine = over_plane(jnp.broadcast_to(came[None], (ZN, *came.shape)))
    theirs = core_pair(mine)
    own, give, kept = project(prefix_len, norm_gain, mine, theirs, gate_weight, up_weight)
    part = kept[0].shape
    half = (part[1] // LANE) // 2 * LANE
    ends = [((rows, half), BF), ((rows, part[1] - half), BF)]

    far, ahead = after(give[4], give[3])
    far, following = x_pair(far), x_pair(ahead)
    up, down = local(add_first_kernel, ends, kept[4], far)
    for step in (4, 3, 2, 1):
        up, down, ahead = after(up, down, give[step - 2] if step > 1 else give[0])
        x = following
        if step > 1:
            following = x_pair(ahead)
        up, down = along_z(up, 1), along_z(down, -1)
        up, down, x = after(up, down, x)
        if step > 1:
            up, down = local(
                add_far_kernel if step == 4 else add_ring_kernel,
                [(part, BF)] * 2,
                kept[step - 1],
                kept[ZN + 1 - step],
                x,
                up,
                down,
            )
    hidden = local(gated_kernel, [((rows, hidden_width), BF)], kept[0], x, up, down)

    up, down, across = hidden, hidden, hidden
    blocks, partners = [hidden], []
    for step in range(3):
        up, down, across = after(up, down, across)
        up, down, came = mirrored(up, 1), mirrored(down, -1), x_pair(across)
        if partners:
            up, down, partners[-1] = after(up, down, partners[-1])
        else:
            up, down = after(up, down)
        partners.append(came)
        blocks += [up, down]
        across = jnp.stack([up, down])
    half = (hidden_width // LANE + 1) // 2 * LANE
    up, down, across = after(up[:, :half], down[:, half:], across)
    up, down, came = mirrored(up, 1), mirrored(down, -1), x_pair(across)
    up, down, partners[-1] = after(up, down, partners[-1])
    partners += [came, x_pair(jnp.concatenate([up, down], axis=1))]
    blocks += [up, down, *partners]
    send, keep = project_down(blocks, down_weight)
    held = local(add_core_kernel, [(keep.shape, BF)], keep, core_pair(send))
    parts = over_plane(held)
    return pl.pallas_call(
        finish_kernel,
        out_shape=jax.ShapeDtypeStruct((rows, width), BF),
        in_specs=[VMEM, VMEM],
        out_specs=VMEM,
        compiler_params=PARAMS,
    )(own, parts)


def solution(mesh):
    return jax.shard_map(
        body,
        mesh=mesh,
        in_specs=(
            P("batch", None),
            P("batch", "mp"),
            P("batch", None),
            P("batch", None),
            P("batch"),
            P(),
            P(),
            P("batch", "mp"),
            P("batch", "mp"),
            P("mp", "batch"),
        ),
        out_specs=P("mp", "batch"),
        check_vma=False,
    )
```

```python
import jax
import jax.numpy as jnp
from jax import lax
from jax.experimental import pallas as pl
from jax.experimental.pallas import tpu as pltpu
from jax.sharding import PartitionSpec as P

HEADS = 128
KV_HEADS = 8
HEAD_DIM = 128
PREFIX = 24
ROWS_DEV = 32
ZN = 8
LANE = 128
BF = jnp.bfloat16
F32 = jnp.float32
PLANE = [[2 * i + core for i in range(8)] for core in range(2)]
VMEM = pl.BlockSpec(memory_space=pltpu.VMEM)
SMEM = pl.BlockSpec(memory_space=pltpu.SMEM)
ANY = pl.BlockSpec(memory_space=pl.ANY)
HBM = pl.BlockSpec(memory_space=pltpu.HBM)
PARAMS = pltpu.CompilerParams(vmem_limit_bytes=28 * 2**20)


def permute(value, axis, target, count=16):
    return lax.ppermute(value, axis, [(i, target(i)) for i in range(count)])


def along_z(value, step):
    return permute(value, "batch", lambda i: (i + 2 * step) % 16)


def mirrored(value, step):
    return lax.ppermute(
        value,
        ("batch", "mp"),
        [
            (b * 16 + m, (b + 2 * step * (1 - 2 * (m % 2))) % 16 * 16 + m)
            for b in range(16)
            for m in range(16)
        ],
    )


def x_pair(value):
    return permute(value, "batch", lambda i: i ^ 1)


def core_pair(value):
    return permute(value, "mp", lambda i: i ^ 1)


def transpose_mesh(value):
    return lax.ppermute(
        value,
        ("batch", "mp"),
        [(b * 16 + m, m * 16 + b) for b in range(16) for m in range(16)],
    )


def over_plane(value):
    return lax.all_to_all(value, "mp", 0, 0, axis_index_groups=PLANE, tiled=True)


def in_vmem(*shapes):
    made = tuple(pltpu.VMEM(shape, dtype) for shape, dtype in shapes)
    return made if len(made) > 1 else made[0]


def in_hbm(value):
    return pltpu.with_memory_space_constraint(value, pltpu.HBM)


PAIRS = 8 * ROWS_DEV
QUERIES = PAIRS + 4 * 16
ASKED = QUERIES + 4 * 16


def mixed(scores, seen, values):
    scores = jnp.where(seen, scores * F32(HEAD_DIM**-0.5), F32(-1e30))
    weights = jnp.exp(scores - jnp.max(scores, axis=1, keepdims=True)).astype(BF)
    both = jnp.concatenate([values, jnp.ones(values.shape, BF)], axis=1)
    product = jnp.dot(weights, both, preferred_element_type=F32)
    return (product[:, :HEAD_DIM] / product[:, HEAD_DIM:]).astype(BF)


def scored(queries, keys):
    return lax.dot_general(queries, keys, (((1,), (1,)), ((), ())), preferred_element_type=F32)


def prepare_kernel(lengths, questions, queries_ref, hidden_ref, key_ref, value_ref, out_ref, queries, hidden, pair, length_ref, question_ref, sems):
    width = queries.shape[1]
    heads = width // HEAD_DIM
    batch_index, mp_index = lax.axis_index("batch"), lax.axis_index("mp")
    head = pl.ds(pl.multiple_of((mp_index >> 1) * HEAD_DIM, HEAD_DIM), HEAD_DIM)
    at = pl.ds(pl.multiple_of(mp_index * width, width), width)
    copies = [
        pltpu.make_async_copy(source, target, sems.at[i])
        for i, (source, target) in enumerate(
            [
                (key_ref.at[:, head], pair.at[:, :HEAD_DIM]),
                (queries_ref, queries),
                (value_ref.at[:, head], pair.at[:, HEAD_DIM:]),
                (hidden_ref.at[:, at], hidden),
                (lengths, length_ref),
                (questions, question_ref),
            ]
        )
    ]
    for copy in copies:
        copy.start()
    copies[4].wait()
    copies[5].wait()
    shape = (ROWS_DEV, ROWS_DEV)
    row = lax.broadcasted_iota(jnp.int32, shape, 0)
    key = lax.broadcasted_iota(jnp.int32, shape, 1)
    seen = (key <= row) & (key < length_ref[batch_index])
    seen = jnp.concatenate([seen.astype(F32)] * heads, axis=0) > 0
    shape = (16, LANE)
    option = lax.broadcasted_iota(jnp.int32, shape, 0) & (ROWS_DEV - PREFIX - 1)
    asked = jnp.zeros(shape, jnp.int32)
    for i in range(ROWS_DEV - PREFIX):
        asked = jnp.where(option == i, question_ref[i], asked)
    out_ref[ASKED : ASKED + 16, :] = asked.astype(F32).astype(BF)
    copies[0].wait()
    copies[1].wait()
    stacked = jnp.concatenate(
        [queries[:, h * HEAD_DIM : (h + 1) * HEAD_DIM] for h in range(heads)], axis=0
    )
    copies[2].wait()
    context = mixed(scored(stacked, pair[:, :HEAD_DIM]), seen, pair[:, HEAD_DIM:])
    for i in range(2):
        for j in range(2):
            at = PAIRS + (2 * i + j) * 16
            out_ref[at : at + 16, :] = pair[16 * i : 16 * i + 16, j * HEAD_DIM : (j + 1) * HEAD_DIM]
    last = queries[16:].astype(F32)[PREFIX - 16 :]
    half = width // 2
    for h in range(heads // 2):
        first = h * HEAD_DIM
        tile = [last[:, at : at + HEAD_DIM] for at in (first, first + half)]
        at = QUERIES + h * 16
        out_ref[at : at + 16, :] = jnp.concatenate(tile, axis=0).astype(BF)
    copies[3].wait()
    prefix = lax.broadcasted_iota(jnp.int32, (ROWS_DEV, HEAD_DIM), 0) < PREFIX
    for h in range(heads):
        columns = slice(h * HEAD_DIM, (h + 1) * HEAD_DIM)
        mine = context[h * ROWS_DEV : (h + 1) * ROWS_DEV].astype(F32)
        mine = jnp.where(prefix, mine, F32(0))
        at = slice(h * ROWS_DEV, (h + 1) * ROWS_DEV)
        out_ref[at, :] = (hidden[:, columns].astype(F32) + mine).astype(BF)


def prepare(prefix_len, question, queries, hidden_in, key_cache, value_cache):
    rows, width = queries.shape
    return pl.pallas_call(
        prepare_kernel,
        out_shape=in_vmem(((ASKED + 16, LANE), BF)),
        in_specs=[HBM] * 6,
        out_specs=VMEM,
        scratch_shapes=[
            pltpu.VMEM((rows, width), BF),
            pltpu.VMEM((rows, width), BF),
            pltpu.VMEM((rows, 2 * HEAD_DIM), BF),
            pltpu.SMEM(prefix_len.shape, jnp.int32),
            pltpu.SMEM(question.shape, jnp.int32),
            pltpu.SemaphoreType.DMA((6,)),
        ],
        compiler_params=PARAMS,
    )(*map(in_hbm, (prefix_len, question, queries, hidden_in, key_cache, value_cache)))


FAR = 4


ORDER = [(s, 1) for s in (FAR, 3, 5, 2, 6, 1, 7, 0)] + [(s, 0) for s in range(ZN)]
FIRST = 3


def products(rows, squares, gate_ref, up_ref):
    tiles = gate_ref.shape[1] // LANE
    for base, ref in ((0, gate_ref), (tiles, up_ref)):
        for t in range(0, tiles, 2):
            lanes = slice(t * LANE, min(t + 2, tiles) * LANE)
            product = jnp.dot(rows[...], ref[:, lanes], preferred_element_type=F32).astype(BF)
            yield slice((base + t) * LANE, (base + t) * LANE + product.shape[1]), product
    yield slice(2 * tiles * LANE, (2 * tiles + 1) * LANE), squares[...]


def first_kernel(length_ref, gain_ref, mine_ref, theirs_ref, gate_ref, up_ref, *refs):
    own_ref, rows, squares, far_ref, next_ref, residual, gain, sem = refs
    n = ROWS_DEV
    width = own_ref.shape[1]
    half = width // 2
    batch_index, mp_index = lax.axis_index("batch"), lax.axis_index("mp")
    z, core = batch_index >> 1, mp_index & 1
    flip = (batch_index & 1) ^ core
    fetch = pltpu.make_async_copy(gain_ref.at[pl.ds(batch_index * width, width)], gain, sem)
    fetch.start()

    blocks = [(ref, i) for ref in (mine_ref, theirs_ref) for i in range(ZN)]
    options = ROWS_DEV - PREFIX

    def gathered(*parts):
        return jnp.concatenate([ref[i, at : at + 16, :] for ref, i in blocks for at in parts], axis=0)

    keys, values = gathered(PAIRS, PAIRS + 32), gathered(PAIRS + 16, PAIRS + 48)
    total = n * len(blocks)
    place = lax.broadcasted_iota(jnp.int32, (8, total), 1)
    order = place >> 5
    live = jnp.zeros(place.shape, jnp.int32)
    for i in range(len(blocks)):
        live = jnp.where(order == i, length_ref[((i & (ZN - 1)) << 1) + ((i >> 3) ^ core)], live)
    owner = ((order & (ZN - 1)) << 1) + ((order >> 3) ^ core)
    owner = jnp.where((place & (n - 1)) < live, owner, -1)
    asked = gathered(ASKED).astype(F32).astype(jnp.int32)
    row = lax.broadcasted_iota(jnp.int32, (asked.shape[0], 1), 0)
    itself = (row >> 4) * n + PREFIX + (row & (options - 1))
    seen = (jnp.tile(owner, (asked.shape[0] // 8, 1)) == jnp.tile(asked, (1, total // LANE))) | (
        jnp.tile(place, (asked.shape[0] // 8, 1)) == itself
    )
    contexts = []
    for h in range(half // HEAD_DIM):
        context = mixed(scored(gathered(QUERIES + h * 16), keys), seen, values)
        contexts.append(context.astype(F32))
    fetch.wait()
    scale = gain[...].reshape(1, width)
    for k, (ref, i) in enumerate(blocks):
        s = (i - z) & (ZN - 1)
        j = flip if ref is mine_ref else 1 - flip
        position = ZN + s
        for index, (target, _) in enumerate(ORDER[:ZN]):
            position = jnp.where((s == target) & (j == 1), index, position)
        into = pl.ds(pl.multiple_of(position * n, n), n)
        total = jnp.zeros((n, LANE), F32)
        for tile in range(width // LANE):
            lanes = slice(tile * LANE, (tile + 1) * LANE)
            at = k * 16 + tile // len(contexts) * options
            added = contexts[tile % len(contexts)][at : at + options]
            added = jnp.concatenate([jnp.zeros((PREFIX, LANE), F32), added], axis=0)
            part = (ref[i, tile * n : (tile + 1) * n, :].astype(F32) + added).astype(BF)
            if ref is mine_ref:
                residual[i, :, lanes] = part
            x = part.astype(F32)
            rows[into, lanes] = (x * scale[:, lanes]).astype(BF)
            total = total + x * x
        squares[into, :] = total.astype(BF)
    own_ref[...] = residual[mp_index >> 1]
    early = slice(0, FIRST * n)
    for lanes, value in products(rows.at[early], squares.at[early], gate_ref, up_ref):
        far_ref[:, lanes] = value[:n]
        next_ref[0, :, lanes] = value[n : 2 * n]
        next_ref[1, :, lanes] = value[2 * n :]


def rest_kernel(rows, squares, gate_ref, up_ref, give2, give1, give0, *kept):
    n = ROWS_DEV
    into = [give2.at[0], give2.at[1], give1.at[0], give1.at[1], give0, *kept]
    late = slice(FIRST * n, len(ORDER) * n)
    for lanes, value in products(rows.at[late], squares.at[late], gate_ref, up_ref):
        for i, ref in enumerate(into):
            ref[:, lanes] = value[i * n : (i + 1) * n]


def fetch_kernel(gate_hbm, up_hbm, gate_ref, up_ref, sems):
    copies = (
        pltpu.make_async_copy(gate_hbm, gate_ref, sems.at[0]),
        pltpu.make_async_copy(up_hbm, up_ref, sems.at[1]),
    )
    for copy in copies:
        copy.start()
    for copy in copies:
        copy.wait()


def fetch(gate_weight, up_weight):
    return pl.pallas_call(
        fetch_kernel,
        out_shape=in_vmem((gate_weight.shape, BF), (up_weight.shape, BF)),
        in_specs=[HBM, HBM],
        out_specs=(VMEM, VMEM),
        scratch_shapes=[pltpu.SemaphoreType.DMA((2,))],
        compiler_params=PARAMS,
        cost_estimate=cost(1, *gate_weight.shape),
    )(in_hbm(gate_weight), in_hbm(up_weight))


def project(prefix_len, norm_gain, mine, theirs, gate_weight, up_weight):
    width, hidden_width = gate_weight.shape
    n = ROWS_DEV
    part = (n, 2 * hidden_width + LANE)
    all_rows = len(ORDER) * n
    own, rows, squares, far, following = pl.pallas_call(
        first_kernel,
        out_shape=in_vmem(
            ((n, width), BF),
            ((all_rows, width), BF),
            ((all_rows, LANE), BF),
            (part, BF),
            ((2, *part), BF),
        ),
        in_specs=[SMEM, HBM, VMEM, VMEM, VMEM, VMEM],
        out_specs=(VMEM,) * 5,
        scratch_shapes=[
            pltpu.VMEM((ZN, n, width), BF),
            pltpu.VMEM((width,), F32),
            pltpu.SemaphoreType.DMA(()),
        ],
        compiler_params=PARAMS,
    )(prefix_len, in_hbm(norm_gain), mine, theirs, gate_weight, up_weight)
    give2, give1, give0, *kept = local(
        rest_kernel,
        [((2, *part), BF)] * 2 + [(part, BF)] * 9,
        rows,
        squares,
        gate_weight,
        up_weight,
        cost=cost((len(ORDER) - FIRST) * n, width, part[1]),
    )
    return own, [give0, give1, give2, following, far], kept


def summed(*refs):
    total = refs[0].astype(F32)
    for ref in refs[1:]:
        total = total + ref.astype(F32)
    return total.astype(BF)


def add_first_kernel(mine, x, out_up, out_down):
    low = out_up.shape[1]
    out_up[...] = summed(mine[:, :low], x[:, :low])
    out_down[...] = summed(mine[:, low:], x[:, low:])


def add_far_kernel(mine_up, mine_down, x, up, down, out_up, out_down):
    low = up.shape[1]
    out_up[:, :low] = summed(mine_up[:, :low], x[0, :, :low], up[...])
    out_up[:, low:] = summed(mine_up[:, low:], x[0, :, low:])
    out_down[:, :low] = summed(mine_down[:, :low], x[1, :, :low])
    out_down[:, low:] = summed(mine_down[:, low:], x[1, :, low:], down[...])


def add_ring_kernel(mine_up, mine_down, x, up, down, out_up, out_down):
    out_up[...] = summed(mine_up[...], x[0], up[...])
    out_down[...] = summed(mine_down[...], x[1], down[...])


def gated_kernel(mine, x, up, down, out):
    width = out.shape[1]

    def total(lanes):
        parts = [ref[:, lanes].astype(F32) for ref in (mine, x, up, down)]
        return (parts[0] + parts[1]) + (parts[2] + parts[3])

    squares = total(slice(2 * width, 2 * width + LANE))
    scale = lax.rsqrt(jnp.sum(squares, axis=1, keepdims=True) * F32(1 / 16384) + 1e-05)
    gate = total(slice(0, width)) * scale
    lift = total(slice(width, 2 * width)) * scale
    out[...] = (gate / (1 + jnp.exp(-gate)) * lift).astype(BF)


def cost(rows, depth, columns):
    return pl.CostEstimate(
        flops=2 * rows * depth * columns, bytes_accessed=2 * depth * columns, transcendentals=0
    )


def local(kernel, shapes, *args, cost=None):
    return pl.pallas_call(
        kernel,
        out_shape=in_vmem(*shapes),
        in_specs=[VMEM] * len(args),
        out_specs=(VMEM,) * len(shapes) if len(shapes) > 1 else VMEM,
        compiler_params=PARAMS,
        cost_estimate=cost,
    )(*args)


def down_kernel(kept, *refs):
    own, up1, down1, up2, down2, up3, down3, up4, down4, x0, x1, x2, x3, x4, down_ref = refs[:15]
    out, rows = refs[15:]
    n = ROWS_DEV
    batch_index, mp_index = lax.axis_index("batch"), lax.axis_index("mp")
    z, flip = batch_index >> 1, (batch_index ^ mp_index) & 1
    ours = {0: own, 1: down1, 2: down2, 3: down3, 5: up3, 6: up2, 7: up1}
    partners = {0: x0, 7: x1.at[0], 1: x1.at[1], 6: x2.at[0], 2: x2.at[1], 5: x3.at[0], 3: x3.at[1], FAR: x4}

    def collect(found):
        for s in range(ZN):
            target = (z + s * (1 - 2 * (mp_index & 1))) & (ZN - 1)
            at = pl.ds(pl.multiple_of(target * n, n), n)
            if s in found:
                rows[at, :] = found[s][...]
            else:
                rows[at, : up4.shape[1]] = up4[...]
                rows[at, up4.shape[1] :] = down4[...]

    @pl.when(flip != kept)
    def _():
        collect(ours)

    @pl.when(flip == kept)
    def _():
        collect(partners)

    step = 2 * LANE
    for i in range(0, down_ref.shape[1], step):
        lanes = slice(i, i + step)
        product = jnp.dot(rows[...], down_ref[:, lanes], preferred_element_type=F32)
        for target in range(ZN):
            out[target, :, lanes] = product[target * n : (target + 1) * n].astype(out.dtype)


def project_down(blocks, down_weight, kept):
    hidden_width, width = down_weight.shape
    return pl.pallas_call(
        lambda *refs: down_kernel(kept, *refs),
        out_shape=in_vmem(((ZN, ROWS_DEV, width), F32 if kept else BF)),
        in_specs=[VMEM] * (len(blocks) + 1),
        out_specs=VMEM,
        scratch_shapes=[pltpu.VMEM((ZN * ROWS_DEV, hidden_width), BF)],
        compiler_params=PARAMS,
        cost_estimate=cost(ZN * ROWS_DEV, hidden_width, width),
    )(*blocks, down_weight)


def add_core_kernel(keep, come, out):
    out[...] = (keep[...] + come[...].astype(F32)).astype(BF)


def finish_kernel(own, parts, out):
    total = own[...].astype(F32)
    for i in range(parts.shape[0]):
        total = total + parts[i].astype(F32)
    out[...] = total.astype(BF)


def after(*values):
    return lax.optimization_barrier(values)


def body(
    hidden_in,
    queries,
    key_cache,
    value_cache,
    question,
    prefix_len,
    norm_gain,
    gate_weight,
    up_weight,
    down_weight,
):
    rows, width = queries.shape
    hidden_width = gate_weight.shape[1]

    sent = prepare(prefix_len, question, queries, hidden_in, key_cache, value_cache)
    sent, gate_weight, up_weight = after(sent, gate_weight, up_weight)
    came, gate_weight, up_weight = after(transpose_mesh(sent), *fetch(gate_weight, up_weight))
    mine = over_plane(jnp.broadcast_to(came[None], (ZN, *came.shape)))
    theirs = core_pair(mine)
    own, give, kept = project(prefix_len, norm_gain, mine, theirs, gate_weight, up_weight)
    part = kept[0].shape
    half = (part[1] // LANE) // 2 * LANE
    ends = [((rows, half), BF), ((rows, part[1] - half), BF)]

    far, ahead = after(give[4], give[3])
    far, following = x_pair(far), x_pair(ahead)
    up, down = local(add_first_kernel, ends, kept[4], far)
    for step in (4, 3, 2, 1):
        up, down, ahead = after(up, down, give[step - 2] if step > 1 else give[0])
        x = following
        if step > 1:
            following = x_pair(ahead)
        up, down = along_z(up, 1), along_z(down, -1)
        up, down, x = after(up, down, x)
        if step > 1:
            up, down = local(
                add_far_kernel if step == 4 else add_ring_kernel,
                [(part, BF)] * 2,
                kept[step - 1],
                kept[ZN + 1 - step],
                x,
                up,
                down,
            )
    hidden = local(gated_kernel, [((rows, hidden_width), BF)], kept[0], x, up, down)

    up, down, across = hidden, hidden, hidden
    blocks, partners = [hidden], []
    for step in range(3):
        up, down, across = after(up, down, across)
        up, down, came = mirrored(up, 1), mirrored(down, -1), x_pair(across)
        if partners:
            up, down, partners[-1] = after(up, down, partners[-1])
        else:
            up, down = after(up, down)
        partners.append(came)
        blocks += [up, down]
        across = jnp.stack([up, down])
    half = (hidden_width // LANE + 1) // 2 * LANE
    up, down, across = after(up[:, :half], down[:, half:], across)
    up, down, came = mirrored(up, 1), mirrored(down, -1), x_pair(across)
    up, down, partners[-1] = after(up, down, partners[-1])
    partners += [came, x_pair(jnp.concatenate([up, down], axis=1))]
    blocks += [up, down, *partners]
    send = project_down(blocks, down_weight, 0)
    send, down_weight = after(send, down_weight)
    keep = project_down(blocks, down_weight, 1)
    held = local(add_core_kernel, [(keep.shape, BF)], keep, core_pair(send))
    parts = over_plane(held)
    return pl.pallas_call(
        finish_kernel,
        out_shape=jax.ShapeDtypeStruct((rows, width), BF),
        in_specs=[VMEM, VMEM],
        out_specs=VMEM,
        compiler_params=PARAMS,
    )(own, parts)


def solution(mesh):
    return jax.shard_map(
        body,
        mesh=mesh,
        in_specs=(
            P("batch", None),
            P("batch", "mp"),
            P("batch", None),
            P("batch", None),
            P("batch"),
            P(),
            P(),
            P("batch", "mp"),
            P("batch", "mp"),
            P("mp", "batch"),
        ),
        out_specs=P("mp", "batch"),
        check_vma=False,
    )
```
